32 devices in a mesh: row: 4 (over y, x), col: 8 (over z, core).
Axes of the slice: x: 2, y: 2, z: 4, core: 2. Of those that a mesh axis runs over, the one named last changes fastest.
Arguments:
- tokens: bfloat16 [4096, 1152], P('col', 'row'), may hold values from -6 to 6
- cotangent: bfloat16 [4096, 1152], P('col', 'row'), may hold values from -6 to 6
- starts: int32 [4, 4], replicated, may hold values from 0 to 768, as said below
- gains: float32 [2, 1152], P(None, 'row'), may hold values from 0.2 to 2.1
- gains_m: float32 [2, 1152], P(None, 'row')
- gains_v: float32 [2, 1152], P(None, 'row')
- w_query: float32 [1152, 1152], P('row', 'col'), may hold values from -0.1875 to 0.1875
- w_query_m: float32 [1152, 1152], P('row', 'col')
- w_query_v: float32 [1152, 1152], P('row', 'col')
- w_keyval: float32 [2, 1152, 384], P(None, 'row', 'col'), may hold values from -0.1875 to 0.1875
- w_keyval_m: float32 [2, 1152, 384], P(None, 'row', 'col')
- w_keyval_v: float32 [2, 1152, 384], P(None, 'row', 'col')
- w_output: float32 [1152, 1152], P('col', 'row'), may hold values from -0.1875 to 0.1875
- w_output_m: float32 [1152, 1152], P('col', 'row')
- w_output_v: float32 [1152, 1152], P('col', 'row')
- w_gateup: float32 [2, 1152, 3072], P(None, 'row', 'col'), may hold values from -0.1875 to 0.1875
- w_gateup_m: float32 [2, 1152, 3072], P(None, 'row', 'col')
- w_gateup_v: float32 [2, 1152, 3072], P(None, 'row', 'col')
- w_down: float32 [3072, 1152], P('col', 'row'), may hold values from -0.109375 to 0.109375
- w_down_m: float32 [3072, 1152], P('col', 'row')
- w_down_v: float32 [3072, 1152], P('col', 'row')
Outputs:
- block_out: bfloat16 [4096, 1152], P('col', 'row')
- input_grad: bfloat16 [4096, 1152], P('col', 'row')
- gains_new_m: float32 [2, 1152], P(None, 'row')
- gains_new_v: float32 [2, 1152], P(None, 'row')
- gains_new: float32 [2, 1152], P(None, 'row')
- w_query_new_m: float32 [1152, 1152], P('row', 'col')
- w_query_new_v: float32 [1152, 1152], P('row', 'col')
- w_query_new: float32 [1152, 1152], P('row', 'col')
- w_query_low: bfloat16 [1152, 1152], P('row', 'col')
- w_keyval_new_m: float32 [2, 1152, 384], P(None, 'row', 'col')
- w_keyval_new_v: float32 [2, 1152, 384], P(None, 'row', 'col')
- w_keyval_new: float32 [2, 1152, 384], P(None, 'row', 'col')
- w_keyval_low: bfloat16 [2, 1152, 384], P(None, 'row', 'col')
- w_output_new_m: float32 [1152, 1152], P('col', 'row')
- w_output_new_v: float32 [1152, 1152], P('col', 'row')
- w_output_new: float32 [1152, 1152], P('col', 'row')
- w_output_low: bfloat16 [1152, 1152], P('col', 'row')
- w_gateup_new_m: float32 [2, 1152, 3072], P(None, 'row', 'col')
- w_gateup_new_v: float32 [2, 1152, 3072], P(None, 'row', 'col')
- w_gateup_new: float32 [2, 1152, 3072], P(None, 'row', 'col')
- w_gateup_low: bfloat16 [2, 1152, 3072], P(None, 'row', 'col')
- w_down_new_m: float32 [3072, 1152], P('col', 'row')
- w_down_new_v: float32 [3072, 1152], P('col', 'row')
- w_down_new: float32 [3072, 1152], P('col', 'row')
- w_down_low: bfloat16 [3072, 1152], P('col', 'row')
The draws below stay inside these ranges and needn't reach their ends.
Inputs may be any that keep to these rules, and one draw needn't show every extreme that they name: In each sequence piece j starts at j * 256 or later and ends by (j + 1) * 256, so pieces rise and never meet.
All inputs are finite; a program needn't handle non-finite values.
Results may differ from the reference program's by a relative error of at most 0.017.
The reference program's roundings to bfloat16 on the way count: a program that leaves them out, or rounds other values in their place, can miss the bound.
Values may be sent and summed in bfloat16 or wider, within the bound.
A program may use at most 192 MiB of HBM per device.

```python
import math
import jax
import jax.numpy as jnp
from jax import lax

D = 1152
HEADS = 18
KV_HEADS = 6
HD = 64
FF = 3072
PIECE = 256
PIECES = 4
STEP = 7
SEQ = 1024
SEQS = 4
TOKENS = 4096
KVD = 384


def grad_size(kind):
    root = math.sqrt(TOKENS)
    if kind == 0:
        return 1.5 * root / math.sqrt(D)
    if kind == 1:
        return 1.3 * root * math.sqrt(2.7 * math.log(SEQ) / SEQ)
    if kind == 2:
        return 0.42 * root
    if kind == 4:
        return 2.6 * root / math.sqrt(D)
    return 0.75 * root


def first_moment(key, shape, size):
    return size * jnp.clip(jax.random.normal(key, shape, jnp.float32), -4.0, 4.0)


def second_moment(key, shape, size):
    return size * size * jnp.exp(jax.random.uniform(key, shape, jnp.float32, 0.0, 1.3863))


def draw_tokens(key, part):
    key = jax.random.fold_in(key, 1)
    ramp = jnp.arange(D, dtype=jnp.float32) / D
    values = jnp.clip(jax.random.normal(key, (TOKENS, D), jnp.float32), -4.0, 4.0)
    return (values * (0.5 + ramp)[None, :]).astype(jnp.bfloat16)


def draw_cotangent(key, part):
    key = jax.random.fold_in(key, 2)
    ramp = jnp.arange(TOKENS, dtype=jnp.float32) / TOKENS
    values = jnp.clip(jax.random.normal(key, (TOKENS, D), jnp.float32), -3.3, 3.3)
    return (values * (0.6 + 1.2 * ramp)[:, None]).astype(jnp.bfloat16)


def draw_starts(key, part):
    key = jax.random.fold_in(key, 3)
    span = SEQ // PIECES
    offsets = jax.random.randint(key, (SEQS, PIECES), 0, span - PIECE + 1)
    offsets = offsets.at[0, 0].set(0)
    offsets = offsets.at[SEQS - 1, PIECES - 1].set(span - PIECE)
    return (offsets + jnp.arange(PIECES, dtype=jnp.int32)[None, :] * span).astype(jnp.int32)


def draw_gains(key, part):
    key = jax.random.fold_in(key, 4)
    ramp = jnp.arange(D, dtype=jnp.float32) / D
    rough = jax.random.uniform(key, (2, D), jnp.float32, 0.7, 1.4)
    return (0.5 + ramp)[None, :] * rough


def gain_sizes():
    root = math.sqrt(TOKENS)
    return jnp.array([[2.0 * root / math.sqrt(D)], [root]], jnp.float32)


def draw_gains_m(key, part):
    key = jax.random.fold_in(key, 5)
    return gain_sizes() * jnp.clip(jax.random.normal(key, (2, D), jnp.float32), -4.0, 4.0)


def draw_gains_v(key, part):
    key = jax.random.fold_in(key, 6)
    sizes = gain_sizes()
    return sizes * sizes * jnp.exp(jax.random.uniform(key, (2, D), jnp.float32, 0.0, 1.3863))


def draw_w_query_m(key, part):
    key = jax.random.fold_in(key, 7)
    return first_moment(key, (D, D), grad_size(0))


def draw_w_query_v(key, part):
    key = jax.random.fold_in(key, 8)
    return second_moment(key, (D, D), grad_size(0))


def draw_w_keyval_m(key, part):
    key = jax.random.fold_in(key, 9)
    return first_moment(key, (2, D, KVD), grad_size(4))


def draw_w_keyval_v(key, part):
    key = jax.random.fold_in(key, 10)
    return second_moment(key, (2, D, KVD), grad_size(4))


def draw_w_output_m(key, part):
    key = jax.random.fold_in(key, 11)
    return first_moment(key, (D, D), grad_size(1))


def draw_w_output_v(key, part):
    key = jax.random.fold_in(key, 12)
    return second_moment(key, (D, D), grad_size(1))


def draw_w_gateup_m(key, part):
    key = jax.random.fold_in(key, 13)
    return first_moment(key, (2, D, FF), grad_size(2))


def draw_w_gateup_v(key, part):
    key = jax.random.fold_in(key, 14)
    return second_moment(key, (2, D, FF), grad_size(2))


def draw_w_down_m(key, part):
    key = jax.random.fold_in(key, 15)
    return first_moment(key, (FF, D), grad_size(3))


def draw_w_down_v(key, part):
    key = jax.random.fold_in(key, 16)
    return second_moment(key, (FF, D), grad_size(3))


def block_scale(rng, shape, cuts, low, top_value):
    def one(position, shards_of):
        steps = jax.random.uniform(jax.random.fold_in(jax.random.fold_in(rng, 6), position), (shards_of,), jnp.float32, low / len(cuts), top_value / len(cuts))
        return jnp.repeat(jnp.exp(steps), shape[position] // shards_of).reshape((-1,) + (1,) * (len(shape) - position - 1))

    level = one(*cuts[0])
    for cut in cuts[1:]:
        level = level * one(*cut)
    return level


def noise(key, shape, spread, limit, cuts=(), kind=jnp.bfloat16):
    drawn = spread * jax.random.normal(key, shape, jnp.float32)
    if cuts:
        drawn = drawn * block_scale(key, shape, cuts, -0.22, 0.18)
    return jnp.clip(drawn, -limit, limit).astype(kind)


def setup_inputs(seed: int = 0) -> dict:
    key_list = jax.random.split(jax.random.key(seed), 22)
    return {
        "tokens": draw_tokens(jax.random.fold_in(key_list[21], 71), 0),
        "cotangent": draw_cotangent(jax.random.fold_in(key_list[21], 71), 0),
        "starts": draw_starts(jax.random.fold_in(key_list[21], 71), 0),
        "gains": draw_gains(jax.random.fold_in(key_list[21], 71), 0),
        "gains_m": draw_gains_m(jax.random.fold_in(key_list[21], 71), 0),
        "gains_v": draw_gains_v(jax.random.fold_in(key_list[21], 71), 0),
        "w_query": noise(key_list[6], (D, D), D ** -0.5, 0.1875, ((0, 4), (1, 8)), jnp.float32),
        "w_query_m": draw_w_query_m(jax.random.fold_in(key_list[21], 71), 0),
        "w_query_v": draw_w_query_v(jax.random.fold_in(key_list[21], 71), 0),
        "w_keyval": noise(key_list[9], (2, D, KVD), D ** -0.5, 0.1875, ((1, 4), (2, 8)), jnp.float32),
        "w_keyval_m": draw_w_keyval_m(jax.random.fold_in(key_list[21], 71), 0),
        "w_keyval_v": draw_w_keyval_v(jax.random.fold_in(key_list[21], 71), 0),
        "w_output": noise(key_list[12], (D, D), D ** -0.5, 0.1875, ((0, 8), (1, 4)), jnp.float32),
        "w_output_m": draw_w_output_m(jax.random.fold_in(key_list[21], 71), 0),
        "w_output_v": draw_w_output_v(jax.random.fold_in(key_list[21], 71), 0),
        "w_gateup": noise(key_list[15], (2, D, FF), D ** -0.5, 0.1875, ((1, 4), (2, 8)), jnp.float32),
        "w_gateup_m": draw_w_gateup_m(jax.random.fold_in(key_list[21], 71), 0),
        "w_gateup_v": draw_w_gateup_v(jax.random.fold_in(key_list[21], 71), 0),
        "w_down": noise(key_list[18], (FF, D), FF ** -0.5, 0.109375, ((0, 8), (1, 4)), jnp.float32),
        "w_down_m": draw_w_down_m(jax.random.fold_in(key_list[21], 71), 0),
        "w_down_v": draw_w_down_v(jax.random.fold_in(key_list[21], 71), 0),
    }


@jax.custom_vjp
def low(v):
    return lax.optimization_barrier(v.astype(jnp.bfloat16)).astype(jnp.float32)

@jax.custom_vjp
def low_back(v):
    return v

def low_keep(v):
    return (low(v), None)

def low_pass(kept, grad):
    return (grad,)

def back_keep(v):
    return (v, None)

def back_low(kept, grad):
    return (low(grad),)
low.defvjp(low_keep, low_pass)
low_back.defvjp(back_keep, back_low)
EPS = 1e-05
BETA = 0.5
TINY = 1e-08
DECAY = 0.1
MASKED = -1e+30
HIGH = lax.Precision.HIGHEST

def matmul(left, right):
    return jnp.dot(left, right, precision=HIGH)

def normalize(hidden, gain):
    scale = lax.rsqrt(lax.optimization_barrier(jnp.mean(hidden * hidden, axis=-1, keepdims=True)) + EPS)
    return low(hidden * scale * gain)

def rotary(places):
    half = HD // 2
    freq = 10000.0 ** (-2.0 * jnp.arange(half, dtype=jnp.float32) / HD)
    angle = places[:, None] * freq[None, :]
    return (jnp.cos(angle), jnp.sin(angle))

def rotate(heads, cosine, sine):
    half = HD // 2
    first = heads[..., :half]
    second = heads[..., half:]
    cosine = cosine[:, None, :]
    sine = sine[:, None, :]
    return jnp.concatenate([first * cosine - second * sine, second * cosine + first * sine], axis=-1)

def piece_ids(pieces, places):
    inside = (places[:, None] >= pieces[None, :]) & (places[:, None] < pieces[None, :] + PIECE)
    number = jnp.arange(1, PIECES + 1, dtype=jnp.int32)
    return lax.optimization_barrier(jnp.sum(jnp.where(inside, number[None, :], 0), axis=1)).astype(jnp.int32) - 1

def attend_sequence(queries, keys, values, pieces):
    places = jnp.arange(SEQ, dtype=jnp.int32)
    ids = piece_ids(pieces, places)
    width = min(512, SEQ)
    count = SEQ // width
    group = queries.shape[2]
    factor = HD ** (-0.5)

    def one_block(item):
        block_queries = item[0]
        block_places = item[1]
        block_ids = item[2]
        scores = low_back(jnp.einsum('tkgd,skd->kgts', block_queries, keys, precision=HIGH) * factor)
        allowed = (places[None, :] <= block_places[:, None]) | (ids[None, :] == block_ids[:, None]) & (block_ids[:, None] >= 0)
        scores = jnp.where(allowed[None, None], scores, MASKED)
        probs = low(jax.nn.softmax(scores, axis=-1))
        return jnp.einsum('kgts,skd->tkgd', probs, values, precision=HIGH)
    blocks = (queries.reshape(count, width, KV_HEADS, group, HD), places.reshape(count, width), ids.reshape(count, width))
    return lax.map(jax.checkpoint(one_block), blocks).reshape(SEQ, KV_HEADS * group * HD)

def forward(hidden, gains, w_query, w_keyval, w_output, w_gateup, w_down, starts):
    normed = normalize(hidden, gains[0])
    queries = low_back(low(matmul(normed, low(w_query))))
    keys = low_back(low(matmul(normed, low(w_keyval[0]))))
    values = low_back(low(matmul(normed, low(w_keyval[1]))))
    places = (jnp.arange(TOKENS, dtype=jnp.int32) % SEQ).astype(jnp.float32)
    cosine, sine = rotary(places)
    queries = low(rotate(queries.reshape(TOKENS, HEADS, HD), cosine, sine))
    keys = low(rotate(keys.reshape(TOKENS, KV_HEADS, HD), cosine, sine))
    group = HEADS // KV_HEADS

    def per_sequence(item):
        return attend_sequence(item[0], item[1], item[2], item[3])
    attended = lax.map(per_sequence, (queries.reshape(SEQS, SEQ, KV_HEADS, group, HD), keys.reshape(SEQS, SEQ, KV_HEADS, HD), values.reshape(SEQS, SEQ, KV_HEADS, HD), starts))
    attended = low_back(low(attended.reshape(TOKENS, D)))
    branch = low_back(matmul(attended, low(w_output)))
    middle = hidden + branch
    normed_two = normalize(middle, gains[1])
    gate = low_back(matmul(normed_two, low(w_gateup[0])))
    upward = low_back(matmul(normed_two, low(w_gateup[1])))
    activated = low(jax.nn.silu(gate) * upward)
    return middle + matmul(activated, low(w_down))

def adamw(weight, first, second, grad, rate, decay):
    first_new = BETA * first + (1.0 - BETA) * grad
    second_new = BETA * second + (1.0 - BETA) * grad * grad
    fix = 1.0 - BETA ** STEP
    update = first_new / fix / (jnp.sqrt(second_new / fix) + TINY)
    weight_new = weight - rate * (update + decay * weight)
    return (first_new, second_new, weight_new)

def reference(tokens, cotangent, starts, gains, gains_m, gains_v, w_query, w_query_m, w_query_v, w_keyval, w_keyval_m, w_keyval_v, w_output, w_output_m, w_output_v, w_gateup, w_gateup_m, w_gateup_v, w_down, w_down_m, w_down_v):
    hidden = tokens.astype(jnp.float32)

    def layer(hidden, gains, w_query, w_keyval, w_output, w_gateup, w_down):
        return forward(hidden, gains, w_query, w_keyval, w_output, w_gateup, w_down, starts)
    result, pull = jax.vjp(layer, hidden, gains, w_query, w_keyval, w_output, w_gateup, w_down)
    grads = pull(cotangent.astype(jnp.float32))
    rate_in = D ** (-0.5)
    rate_down = FF ** (-0.5)
    gain_m, gain_v, gain_w = adamw(gains, gains_m, gains_v, grads[1], 0.25, 0.0)
    query_m, query_v, query_w = adamw(w_query, w_query_m, w_query_v, grads[2], rate_in, DECAY)
    keyval_m, keyval_v, keyval_w = adamw(w_keyval, w_keyval_m, w_keyval_v, grads[3], rate_in, DECAY)
    output_m, output_v, output_w = adamw(w_output, w_output_m, w_output_v, grads[4], rate_in, DECAY)
    gateup_m, gateup_v, gateup_w = adamw(w_gateup, w_gateup_m, w_gateup_v, grads[5], rate_in, DECAY)
    down_m, down_v, down_w = adamw(w_down, w_down_m, w_down_v, grads[6], rate_down, DECAY)
    return (result.astype(jnp.bfloat16), grads[0].astype(jnp.bfloat16), gain_m, gain_v, gain_w, query_m, query_v, query_w, query_w.astype(jnp.bfloat16), keyval_m, keyval_v, keyval_w, keyval_w.astype(jnp.bfloat16), output_m, output_v, output_w, output_w.astype(jnp.bfloat16), gateup_m, gateup_v, gateup_w, gateup_w.astype(jnp.bfloat16), down_m, down_v, down_w, down_w.astype(jnp.bfloat16))
```

```python
import jax
import jax.numpy as jnp
from jax import lax
from jax.experimental import pallas as pl
from jax.experimental.pallas import tpu as pltpu
from jax.sharding import PartitionSpec as P

D = 1152
HEADS = 18
KV_HEADS = 6
HD = 64
FF = 3072
TD = 128
PIECE = 256
PIECES = 4
STEP = 7


EPS = 1e-05
BETA = 0.5
TINY = 1e-08
DECAY = 0.1
MASKED = -1e30


def to_half(value):
    return value.astype(jnp.bfloat16)


def product(left, right):
    return jnp.dot(left, right, preferred_element_type=jnp.float32)


def product_left(left, right):
    return lax.dot_general(
        left, right, (((0,), (0,)), ((), ())), preferred_element_type=jnp.float32
    )


def product_right(left, right):
    return lax.dot_general(
        left, right, (((1,), (1,)), ((), ())), preferred_element_type=jnp.float32
    )


def col_collect(value):
    return lax.all_gather(value, "col", axis=0, tiled=True)


def row_collect(value):
    return lax.all_gather(value, "row", axis=0, tiled=True)


def row_reduce(value):
    return lax.psum_scatter(value, "row", scatter_dimension=0, tiled=True)


def col_reduce(value):
    return lax.psum_scatter(value, "col", scatter_dimension=0, tiled=True)


def row_total(value):
    return lax.psum(value, "row")


def to_heads(value):
    return lax.all_to_all(value, "col", split_axis=0, concat_axis=1, tiled=True)


def to_rows(value):
    return lax.all_to_all(value, "col", split_axis=1, concat_axis=0, tiled=True)


def norm_forward(hidden, gain):
    total = row_total(jnp.sum(hidden * hidden, axis=1))
    scale = lax.rsqrt(total / D + EPS)
    return (scale, to_half(hidden * scale[:, None] * gain[None, :]))


def norm_backward(hidden, gain, scale, grad):
    inner = row_total(jnp.sum(grad * gain[None, :] * hidden, axis=1))
    back = (
        grad * gain[None, :] * scale[:, None]
        - hidden * (scale * scale * scale * inner / D)[:, None]
    )
    gain_grad = jnp.sum(grad * hidden * scale[:, None], axis=0)
    return (back, gain_grad)


def rotary(places):
    half = HD // 2
    freq = 10000.0 ** (-2.0 * jnp.arange(half, dtype=jnp.float32) / HD)
    angle = places[:, None] * freq[None, :]
    return (jnp.cos(angle), jnp.sin(angle))


def rotate(heads, cosine, sine):
    half = HD // 2
    first = heads[..., :half]
    second = heads[..., half:]
    cosine = cosine[:, None, :]
    sine = sine[:, None, :]
    return jnp.concatenate(
        [first * cosine - second * sine, second * cosine + first * sine], axis=-1
    )


def rotate_back(heads, cosine, sine):
    half = HD // 2
    first = heads[..., :half]
    second = heads[..., half:]
    cosine = cosine[:, None, :]
    sine = sine[:, None, :]
    return jnp.concatenate(
        [first * cosine + second * sine, second * cosine - first * sine], axis=-1
    )


def piece_ids(pieces, places):
    inside = (places[:, None] >= pieces[None, :]) & (places[:, None] < pieces[None, :] + PIECE)
    number = jnp.arange(1, PIECES + 1, dtype=jnp.int32)
    return jnp.sum(jnp.where(inside, number[None, :], 0), axis=1) - 1


def block_scores(queries, keys, places, ids, pieces, start):
    key_places = start + jnp.arange(keys.shape[0], dtype=jnp.int32)
    key_ids = piece_ids(pieces, key_places)
    raw = jnp.einsum("tkgd,skd->kgts", queries, keys, preferred_element_type=jnp.float32) * HD ** (
        -0.5
    )
    allowed = (key_places[None, :] <= places[:, None]) | (key_ids[None, :] == ids[:, None]) & (
        ids[:, None] >= 0
    )
    allowed = allowed[None, None]
    return (jnp.where(allowed, raw, MASKED), allowed)


def split_blocks(keyvals, width):
    count = keyvals.shape[0] // width
    blocks = keyvals.reshape(count, width, 2, KV_HEADS, HD)
    firsts = jnp.arange(count, dtype=jnp.int32) * width
    return (blocks, firsts)


def attend(queries, keyvals, places, ids, pieces, width):
    blocks, firsts = split_blocks(keyvals, width)
    shape = (KV_HEADS, queries.shape[2], queries.shape[0])

    def measure(carry, item):
        high, total = carry
        scores, allowed = block_scores(queries, item[0][:, 0], places, ids, pieces, item[1])
        new_high = jnp.maximum(high, jnp.max(scores, axis=-1))
        weights = jnp.where(allowed, jnp.exp(scores - new_high[..., None]), 0.0)
        return ((new_high, total * jnp.exp(high - new_high) + jnp.sum(weights, axis=-1)), None)

    start_state = (jnp.full(shape, MASKED, jnp.float32), jnp.zeros(shape, jnp.float32))
    (high, total), unused = lax.scan(measure, start_state, (blocks, firsts))
    logsum = high + jnp.log(total)

    def accumulate(acc, item):
        scores, allowed = block_scores(queries, item[0][:, 0], places, ids, pieces, item[1])
        probs = to_half(jnp.where(allowed, jnp.exp(scores - logsum[..., None]), 0.0))
        return (
            acc
            + jnp.einsum(
                "kgts,skd->tkgd", probs, item[0][:, 1], preferred_element_type=jnp.float32
            ),
            None,
        )

    output, unused = lax.scan(accumulate, jnp.zeros(queries.shape, jnp.float32), (blocks, firsts))
    return (output, logsum)


def attend_back(queries, keyvals, places, ids, pieces, width, logsum, grad_out, output):
    blocks, firsts = split_blocks(keyvals, width)
    delta = jnp.einsum("tkgd,tkgd->kgt", grad_out.astype(jnp.float32), output)
    factor = HD ** (-0.5)

    def sweep(acc, item):
        keys = item[0][:, 0]
        values = item[0][:, 1]
        scores, allowed = block_scores(queries, keys, places, ids, pieces, item[1])
        probs = jnp.where(allowed, jnp.exp(scores - logsum[..., None]), 0.0)
        grad_probs = jnp.einsum(
            "tkgd,skd->kgts", grad_out, values, preferred_element_type=jnp.float32
        )
        grad_scores = to_half(probs * (grad_probs - delta[..., None]))
        acc = (
            acc
            + jnp.einsum("kgts,skd->tkgd", grad_scores, keys, preferred_element_type=jnp.float32)
            * factor
        )
        grad_keys = (
            jnp.einsum("kgts,tkgd->skd", grad_scores, queries, preferred_element_type=jnp.float32)
            * factor
        )
        grad_values = jnp.einsum(
            "kgts,tkgd->skd", to_half(probs), grad_out, preferred_element_type=jnp.float32
        )
        joined = jnp.concatenate(
            [grad_keys.reshape(width, -1), grad_values.reshape(width, -1)], axis=1
        )
        return (acc, joined)

    grad_queries, grad_blocks = lax.scan(
        sweep, jnp.zeros(queries.shape, jnp.float32), (blocks, firsts)
    )
    return (grad_queries, grad_blocks.reshape(keyvals.shape[0], -1))


def adamw(weight, first, second, grad, rate, decay):
    first_new = BETA * first + (1.0 - BETA) * grad
    second_new = BETA * second + (1.0 - BETA) * grad * grad
    fix = 1.0 - BETA**STEP
    update = first_new / fix / (jnp.sqrt(second_new / fix) + TINY)
    weight_new = weight - rate * (update + decay * weight)
    return (first_new, second_new, weight_new)


def grid_plan(tokens, cotangent, starts, gains, w_query, w_keyval, w_output, w_gateup, w_down):
    columns = lax.axis_size("col")
    column = lax.axis_index("col")
    seq_len = TD * columns
    width = min(1024, seq_len)
    group = HEADS // KV_HEADS
    query_width = w_query.shape[1]
    key_width = w_keyval.shape[2]
    feed_width = w_gateup.shape[2]
    pieces = lax.dynamic_index_in_dim(starts, lax.axis_index("row"), 0, keepdims=False)
    hidden = tokens.astype(jnp.float32)
    inner_weights = to_half(jnp.concatenate([w_query, w_keyval[0], w_keyval[1]], axis=1))
    feed_weights = to_half(jnp.concatenate([w_gateup[0], w_gateup[1]], axis=1))
    out_weights = to_half(w_output)
    down_weights = to_half(w_down)
    scale_one, normed_one = norm_forward(hidden, gains[0])
    gathered_one = col_collect(normed_one)
    mixed = to_half(row_reduce(product(gathered_one, inner_weights)))
    spread = to_heads(mixed[:, None, :])
    query_raw = spread[:, :, :query_width].reshape(TD, HEADS, HD)
    key_raw = spread[:, :, query_width : query_width + key_width].reshape(TD, KV_HEADS, HD)
    value_heads = spread[:, :, query_width + key_width :].reshape(TD, KV_HEADS * HD)
    places = column * TD + jnp.arange(TD, dtype=jnp.int32)
    cosine, sine = rotary(places.astype(jnp.float32))
    queries = to_half(rotate(query_raw.astype(jnp.float32), cosine, sine)).reshape(
        TD, KV_HEADS, group, HD
    )
    keys = to_half(rotate(key_raw.astype(jnp.float32), cosine, sine))
    keyvals_local = jnp.concatenate([keys.reshape(TD, KV_HEADS * HD), value_heads], axis=1)
    keyvals = lax.all_gather(keyvals_local, "col", axis=0, tiled=True)
    ids = piece_ids(pieces, places)
    output, logsum = attend(queries, keyvals, places, ids, pieces, width)
    attended = to_half(output)
    attended_rows = to_rows(attended.reshape(TD, columns, query_width))[:, 0, :]
    gathered_att = row_collect(attended_rows)
    branch = col_reduce(product(gathered_att, out_weights))
    middle = hidden + branch
    scale_two, normed_two = norm_forward(middle, gains[1])
    gathered_two = col_collect(normed_two)
    feed = row_reduce(product(gathered_two, feed_weights))
    gate = feed[:, :feed_width]
    upward = feed[:, feed_width:]
    sigma = jax.nn.sigmoid(gate)
    swish = gate * sigma
    activated = to_half(swish * upward)
    gathered_act = row_collect(activated)
    result = middle + col_reduce(product(gathered_act, down_weights))
    block_out = to_half(result)
    both = lax.all_gather(jnp.stack([normed_one, normed_two]), "col", axis=1, tiled=True)
    back_one = both[0]
    back_two = both[1]
    grad_rows = col_collect(cotangent)
    grad_down = product_left(gathered_act, grad_rows)
    grad_act = row_reduce(product_right(grad_rows, down_weights))
    slope = sigma * (1.0 + gate * (1.0 - sigma))
    grad_feed = to_half(jnp.concatenate([grad_act * upward * slope, grad_act * swish], axis=1))
    gathered_feed = row_collect(grad_feed)
    grad_both = product_left(back_two, gathered_feed)
    grad_gateup = jnp.stack([grad_both[:, :feed_width], grad_both[:, feed_width:]])
    grad_normed_two = col_reduce(product_right(gathered_feed, feed_weights))
    norm_two_back, gain_two = norm_backward(middle, gains[1], scale_two, grad_normed_two)
    grad_middle = cotangent.astype(jnp.float32) + norm_two_back
    gathered_mid = col_collect(to_half(grad_middle))
    grad_output = product_left(gathered_att, gathered_mid)
    grad_att = to_half(row_reduce(product_right(gathered_mid, out_weights)))
    grad_heads = to_heads(grad_att[:, None, :]).reshape(TD, KV_HEADS, group, HD)
    keyvals_back = lax.all_gather(keyvals_local, "col", axis=0, tiled=True)
    grad_queries, grad_keyvals = attend_back(
        queries, keyvals_back, places, ids, pieces, width, logsum, grad_heads, output
    )
    local_keyvals = lax.psum_scatter(grad_keyvals, "col", scatter_dimension=0, tiled=True)
    kv_split = KV_HEADS * HD
    grad_query_raw = rotate_back(grad_queries.reshape(TD, HEADS, HD), cosine, sine)
    grad_key_raw = rotate_back(local_keyvals[:, :kv_split].reshape(TD, KV_HEADS, HD), cosine, sine)
    grad_value = local_keyvals[:, kv_split:]
    joined = jnp.concatenate(
        [
            to_half(grad_query_raw).reshape(TD, columns, query_width),
            to_half(grad_key_raw).reshape(TD, columns, key_width),
            to_half(grad_value).reshape(TD, columns, key_width),
        ],
        axis=2,
    )
    grad_mixed = to_rows(joined)[:, 0, :]
    gathered_mixed = row_collect(grad_mixed)
    grad_inner = product_left(back_one, gathered_mixed)
    grad_query = grad_inner[:, :query_width]
    grad_keyval = jnp.stack(
        [
            grad_inner[:, query_width : query_width + key_width],
            grad_inner[:, query_width + key_width :],
        ]
    )
    grad_normed_one = col_reduce(product_right(gathered_mixed, inner_weights))
    norm_one_back, gain_one = norm_backward(hidden, gains[0], scale_one, grad_normed_one)
    input_grad = to_half(grad_middle + norm_one_back)
    gain_grads = lax.psum(jnp.stack([gain_one, gain_two]), "col")
    return (
        block_out,
        input_grad,
        gain_grads,
        grad_query,
        grad_keyval,
        grad_output,
        grad_gateup,
        grad_down,
    )


def local_general(
    tokens,
    cotangent,
    starts,
    gains,
    gains_m,
    gains_v,
    w_query,
    w_query_m,
    w_query_v,
    w_keyval,
    w_keyval_m,
    w_keyval_v,
    w_output,
    w_output_m,
    w_output_v,
    w_gateup,
    w_gateup_m,
    w_gateup_v,
    w_down,
    w_down_m,
    w_down_v,
):
    results = grid_plan(
        tokens, cotangent, starts, gains, w_query, w_keyval, w_output, w_gateup, w_down
    )
    (
        block_out,
        input_grad,
        gain_grads,
        grad_query,
        grad_keyval,
        grad_output,
        grad_gateup,
        grad_down,
    ) = results
    rate_in = D ** (-0.5)
    rate_down = FF ** (-0.5)
    gain_m, gain_v, gain_w = adamw(gains, gains_m, gains_v, gain_grads, 0.25, 0.0)
    query_m, query_v, query_w = adamw(w_query, w_query_m, w_query_v, grad_query, rate_in, DECAY)
    keyval_m, keyval_v, keyval_w = adamw(
        w_keyval, w_keyval_m, w_keyval_v, grad_keyval, rate_in, DECAY
    )
    output_m, output_v, output_w = adamw(
        w_output, w_output_m, w_output_v, grad_output, rate_in, DECAY
    )
    gateup_m, gateup_v, gateup_w = adamw(
        w_gateup, w_gateup_m, w_gateup_v, grad_gateup, rate_in, DECAY
    )
    down_m, down_v, down_w = adamw(w_down, w_down_m, w_down_v, grad_down, rate_down, DECAY)
    return (
        block_out,
        input_grad,
        gain_m,
        gain_v,
        gain_w,
        query_m,
        query_v,
        query_w,
        to_half(query_w),
        keyval_m,
        keyval_v,
        keyval_w,
        to_half(keyval_w),
        output_m,
        output_v,
        output_w,
        to_half(output_w),
        gateup_m,
        gateup_v,
        gateup_w,
        to_half(gateup_w),
        down_m,
        down_v,
        down_w,
        to_half(down_w),
    )


TB = 128
MESH = pl.DeviceIdType.MESH
half = jnp.bfloat16
full = jnp.float32
VM = pl.BlockSpec(memory_space=pltpu.VMEM)
SM = pl.BlockSpec(memory_space=pltpu.SMEM)


def mate(r, m):
    x = lax.rem(lax.rem(r, 2) + lax.rem(m, 2), 2)
    y = lax.rem(r // 2 + m // 2, 2)
    return 2 * y + x


def other_core(c):
    return c + 1 - 2 * lax.rem(c, 2)


def z_ahead(c, m):
    return lax.rem(c + 2 * m, 8)


def block_rows(b):
    return pl.ds(pl.multiple_of(b * TB, TB), TB)


def part_rows(b, h):
    if h is None:
        return block_rows(b)
    return pl.ds(pl.multiple_of(b * TB + 64 * h, 64), 64)


def slice_rows(b, h=None):
    if h is None:
        return pl.ds(pl.multiple_of(b * 288, 32), 288)
    return pl.ds(pl.multiple_of(b * 288 + 144 * h, 16), 144)


def greet(targets):
    barrier = pltpu.get_barrier_semaphore()
    for target in targets:
        pl.semaphore_signal(barrier, inc=1, device_id=target, device_id_type=MESH)
    return lambda: pl.semaphore_wait(barrier, len(targets))


def remote(src, dst, send, recv, target):
    return pltpu.make_async_remote_copy(
        src_ref=src, dst_ref=dst, send_sem=send, recv_sem=recv, device_id=target, device_id_type=MESH
    )


class Gather:
    def __init__(self, view, r, c, send, recv):
        x, y, far = mate(r, 1), mate(r, 2), mate(r, 3)
        self.first = [
            remote(view(r, None), view(r, None), send.at[0], recv.at[0], (x, c)),
            remote(view(r, None), view(r, None), send.at[1], recv.at[1], (y, c)),
        ]
        self.onward = [
            remote(view(x, 0), view(x, 0), send.at[2], recv.at[2], (y, c)),
            remote(view(y, 1), view(y, 1), send.at[3], recv.at[3], (x, c)),
        ]
        self.arrive = [
            remote(view(x, None), view(x, None), send.at[0], recv.at[0], (x, c)),
            remote(view(y, None), view(y, None), send.at[1], recv.at[1], (y, c)),
            remote(view(far, 0), view(far, 0), send.at[2], recv.at[2], (y, c)),
            remote(view(far, 1), view(far, 1), send.at[3], recv.at[3], (x, c)),
        ]

    def start(self):
        for copy in self.first:
            copy.start()

    def relay(self):
        for i in range(2):
            self.arrive[i].wait_recv()
            self.onward[i].start()

    def finish(self):
        self.arrive[2].wait_recv()
        self.arrive[3].wait_recv()

    def sent(self):
        for copy in self.first + self.onward:
            copy.wait_send()


class Scatter:
    def __init__(self, out, near, mid, last, r, c, send, recv):
        x, y = (mate(r, 1), c), (mate(r, 2), c)
        up, low = pl.ds(0, 64), pl.ds(64, 64)
        self.out, self.near, self.mid, self.last = out, near, mid, last
        self.first = [
            remote(out.at[0, up], near.at[0, 0], send.at[0], recv.at[0], x),
            remote(out.at[1, low], near.at[1, 0], send.at[1], recv.at[1], y),
            remote(out.at[2, up], near.at[0, 1], send.at[2], recv.at[2], x),
            remote(out.at[2, low], near.at[1, 1], send.at[3], recv.at[3], y),
        ]
        self.second = [
            remote(mid.at[0], last.at[0], send.at[4], recv.at[4], y),
            remote(mid.at[1], last.at[1], send.at[5], recv.at[5], x),
        ]

    def start(self, which=(2, 3, 0, 1)):
        for i in which:
            self.first[i].start()

    def relay(self):
        self.first[2].wait_recv()
        self.mid[0] = (self.out[1, 0:64].astype(full) + self.near[0, 1].astype(full)).astype(half)
        self.second[0].start()
        self.first[3].wait_recv()
        self.mid[1] = (self.out[0, 64:128].astype(full) + self.near[1, 1].astype(full)).astype(half)
        self.second[1].start()

    def finish(self, own):
        for copy in self.first[:2] + self.second:
            copy.wait_recv()
        upper = own[0:64] + self.near[0, 0].astype(full) + self.last[0].astype(full)
        lower = own[64:128] + self.near[1, 0].astype(full) + self.last[1].astype(full)
        return jnp.concatenate([upper, lower], axis=0)

    def sent(self):
        for copy in self.first + self.second:
            copy.wait_send()


def scatter_buffers(width):
    v = pltpu.VMEM
    return [
        v((3, TB, width), half),
        v((2, 2, 64, width), half),
        v((2, 64, width), half),
        v((2, 64, width), half),
    ]


def idle_plane(r, k):
    x = lax.rem(r, 2)
    return 2 * (1 - lax.rem(x + k, 2)) + 1 - r // 2


def tile_place(r, k, z):
    return jnp.minimum(lax.rem(z - idle_plane(r, k) + 3, 4), 2)


def has_tile(b, z, k):
    return (b // 2 == lax.rem(z, 2)) | (lax.rem(b, 2) == lax.rem(k + z // 2, 2))


def tile_of(b, z):
    return jnp.where(b // 2 == lax.rem(z, 2), lax.rem(b, 2), 2)


def tile_cols(place):
    return pl.ds(pl.multiple_of(place * 128, 128), 128)


class TileGather:
    def __init__(self, mine, view, r, c, zs, zr, cs, cr):
        self.r, self.z, self.k = r, c // 2, lax.rem(c, 2)
        core = (r, other_core(c))
        z, k = self.z, self.k
        self.has = has_tile(r, z, k)
        here = view(3 * k + tile_place(r, k, z))
        self.out = [remote(mine, here, zs.at[m], zr.at[m], (r, z_ahead(c, m + 1))) for m in range(3)]
        self.out.append(remote(mine, here, cs.at[3], cr.at[3], core))
        self.relays = []
        for m in range(3):
            src = lax.rem(z + 3 - m, 4)
            slot = view(3 * k + tile_place(r, k, src))
            self.relays.append(
                (
                    has_tile(r, src, k),
                    remote(slot, slot, zs.at[m], zr.at[m], core),
                    remote(slot, slot, cs.at[m], cr.at[m], core),
                )
            )
        self.others = []
        for m in range(4):
            src = z if m == 3 else lax.rem(z + 3 - m, 4)
            slot = view(3 * (1 - k) + tile_place(r, 1 - k, src))
            self.others.append(
                (has_tile(r, src, 1 - k), remote(slot, slot, cs.at[m], cr.at[m], core))
            )

    def start(self):
        for copy in self.out:
            copy.start()

    def finish(self):
        for flag, come, go in self.relays:

            @pl.when(flag)
            def _():
                come.wait_recv()
                go.start()

        for flag, come in self.others:

            @pl.when(flag)
            def _():
                come.wait_recv()

    def sent(self):
        @pl.when(self.has)
        def _():
            for copy in self.out:
                copy.wait_send()

        for flag, come, go in self.relays:

            @pl.when(flag)
            def _():
                go.wait_send()


def turn(value, cosine, sine):
    lane = lax.broadcasted_iota(jnp.int32, (value.shape[0], 128), 1)
    first = lax.rem(lane, 64) < 32
    parts = []
    for i in range(value.shape[1] // 128):
        part = value[:, 128 * i : 128 * i + 128]
        swapped = jnp.where(first, pltpu.roll(part, 96, 1), pltpu.roll(part, 32, 1))
        parts.append(part * cosine + swapped * sine)
    return jnp.concatenate(parts, axis=1)


def mask_bias(starts_ref, seq, base):
    keys = lax.broadcasted_iota(jnp.int32, (1, 1024), 1)
    rows = lax.broadcasted_iota(jnp.int32, (TB, 1), 0) + base
    key_id = jnp.zeros((1, 1024), jnp.int32)
    row_id = jnp.zeros((TB, 1), jnp.int32)
    for j in range(PIECES):
        first = starts_ref[seq, j]
        key_id = key_id + jnp.where((keys >= first) & (keys < first + PIECE), j + 1, 0)
        row_id = row_id + jnp.where((rows >= first) & (rows < first + PIECE), j + 1, 0)
    row_id = jnp.where(row_id == 0, -1, row_id)
    allowed = (keys <= rows) | (key_id == row_id)
    return jnp.where(allowed, 0.0, MASKED)


def attend_kernel(
    tok_ref, cot_ref, wq_ref, wkv_ref, wo_ref, wgu_ref, wd_ref, gain1_ref, gain2_ref, cos_ref,
    sin_ref, starts_ref,
    n2_ref, mid_ref, cotall_ref, w_ref, tiled_ref, gain_ref, q_ref, kv_ref, lse_ref, out_ref,
    wof_ref, wi_ref, n1_ref, srow_ref, sown_ref,
    wsrc, osrc, w3, blk, tile, tok_own, sums, gain_parts, kv_own, q_own, wo_all,
    hid, kvb0, kvb1, kvb2, kvb3, qb0, qb1, qb2, qb3,
    zq_s, zq_r, cq_s, cq_r, a_s, a_r, zo_s, zo_r, po_s, po_r, co_s, co_r, t_s, t_r, c_s, c_r,
    g_s, g_r, kp_s, kp_r, qp_s, qp_r, kv_s, kv_r, ck_s, ck_r, zt_s, zt_r, ct_s, ct_r, ss_s, ss_r,
):
    r = lax.axis_index("row")
    c = lax.axis_index("col")
    z = c // 2
    k = lax.rem(c, 2)
    oc = other_core(c)
    mates = [(mate(r, m), c) for m in (1, 2, 3)]
    aheads = [(r, z_ahead(c, m)) for m in (1, 2, 3)]
    core = (r, oc)
    ready = greet(mates + [core] + aheads)
    mine = slice_rows(r)
    sent = []

    def send(src, dst, send_sem, recv_sem, target):
        copy = remote(src, dst, send_sem, recv_sem, target)
        copy.start()
        sent.append(copy)
        return copy

    joined = jnp.concatenate([wq_ref[...], wkv_ref[0], wkv_ref[1]], axis=0)
    wsrc[...] = jnp.transpose(joined).astype(half)
    blk[c] = wsrc[...]
    tokens = tok_ref[...].astype(full)
    sums[r] = jnp.broadcast_to(jnp.sum(tokens * tokens, axis=0, keepdims=True), (8, 512))
    ready()
    qz = [send(wsrc, blk.at[c], zq_s.at[m], zq_r.at[m], aheads[m]) for m in range(3)]
    q_core = [send(wsrc, blk.at[c], cq_s.at[3], cq_r.at[3], core)]
    sum_copies = [
        send(sums.at[r], sums.at[r], ss_s.at[m], ss_r.at[m], mates[m]) for m in range(3)
    ]
    tok_copies = [
        send(tok_ref.at[:, block_rows(mates[m][0])], tok_own.at[mine], t_s.at[m], t_r.at[m], mates[m])
        for m in range(3)
    ]
    gain_copies = [
        send(gain2_ref, gain_parts.at[r], g_s.at[m], g_r.at[m], mates[m]) for m in range(3)
    ]
    for i in range(3):
        for t in range(3):
            src = wd_ref[...] if t == 2 else wgu_ref[t]
            w3[i, t] = src[:, 128 * i : 128 * i + 128].astype(half)
    tile_sends = []
    for m in range(3):
        b = mates[m][0]
        copy = remote(
            w3.at[tile_of(b, z)], tile.at[:, mine, :], a_s.at[m], a_r.at[m], mates[m]
        )
        tile_sends.append((has_tile(b, z, k), copy))

        @pl.when(has_tile(b, z, k))
        def _():
            copy.start()

    cotall_ref[mine, :] = cot_ref[...]
    cot_gather = Gather(lambda b, h: cotall_ref.at[slice_rows(b, h)], r, c, c_s, c_r)
    cot_gather.start()
    for j in range(3):
        osrc[:, 288 * j : 288 * j + 288] = wo_ref[48 * j : 48 * j + 48, :].astype(half)
    wo_all[r, z, k] = osrc[...]
    tok_own[mine, :] = tok_ref[:, block_rows(r)]
    gain_parts[r] = gain2_ref[...]

    @pl.when(has_tile(r, z, k))
    def _():
        tile[:, mine, :] = w3[tile_of(r, z)]

    for copy in sum_copies:
        copy.wait_recv()
    scale_row = lax.rsqrt((sums[0] + sums[1] + sums[2] + sums[3]) / D + EPS)
    srow_ref[...] = scale_row
    n1_ref[...] = (tokens * scale_row[0:1, :] * gain1_ref[:, 0:1]).astype(half)
    for m in range(3):
        src = lax.rem(c + 6 - 2 * m, 8)
        remote(wsrc, blk.at[src], zq_s.at[m], zq_r.at[m], core).wait_recv()
        q_core.append(send(blk.at[src], blk.at[src], cq_s.at[m], cq_r.at[m], core))
    oz = [send(osrc, wo_all.at[r, z, k], zo_s.at[m], zo_r.at[m], aheads[m]) for m in range(3)]
    gate_up = TileGather(
        tile.at[0:2],
        lambda slot: w_ref.at[:, :, tile_cols(slot)],
        r, c, zt_s, zt_r, ct_s, ct_r,
    )

    @pl.when(gate_up.has)
    def _():
        for m in range(3):
            src = slice_rows(mates[m][0])
            remote(w3.at[0], tile.at[:, src, :], a_s.at[m], a_r.at[m], mates[m]).wait_recv()
        gate_up.start()

    for m in range(3):
        src = lax.rem(oc + 6 - 2 * m, 8)
        remote(blk.at[src], blk.at[src], cq_s.at[m], cq_r.at[m], core).wait_recv()
    remote(wsrc, blk.at[oc], cq_s.at[3], cq_r.at[3], core).wait_recv()
    for i in range(8):
        wi_ref[:, 144 * i : 144 * i + 144] = blk[i, :, 0:144]
        wi_ref[:, 1152 + 48 * i : 1200 + 48 * i] = blk[i, :, 144:192]
        wi_ref[:, 1536 + 48 * i : 1584 + 48 * i] = blk[i, :, 192:240]
    kv_scatter = Scatter(kvb0, kvb1, kvb2, kvb3, r, c, kp_s, kp_r)
    q_scatter = Scatter(qb0, qb1, qb2, qb3, r, c, qp_s, qp_r)
    for m in (2, 0, 1):
        part = n1_ref[:, block_rows(mates[m][0])]
        kvb0[m] = product_left(part, wi_ref[:, 1152:]).astype(half)
        kv_scatter.start(((0,), (1,), (2, 3))[m])
    cot_gather.relay()
    for m in (2, 0, 1):
        part = n1_ref[:, block_rows(mates[m][0])]
        qb0[m] = product_left(part, wi_ref[:, :1152]).astype(half)
        q_scatter.start(((0,), (1,), (2, 3))[m])
    kv_scatter.relay()
    part = n1_ref[:, block_rows(r)]
    kv_own[...] = product_left(part, wi_ref[:, 1152:])
    q_own[...] = product_left(part, wi_ref[:, :1152])
    for m in range(3):
        src = slice_rows(mates[m][0])
        remote(
            tok_ref.at[:, block_rows(0)], tok_own.at[src], t_s.at[m], t_r.at[m], mates[m]
        ).wait_recv()
    hidden = jnp.transpose(tok_own[...].astype(full))
    hid[...] = hidden
    scale = lax.rsqrt(jnp.sum(hidden * hidden, axis=1, keepdims=True) / D + EPS)
    sown_ref[...] = jnp.broadcast_to(scale, (TB, 128))
    cosine = cos_ref[...]
    sine = sin_ref[...]
    raw = kv_scatter.finish(kv_own).astype(half)
    my_block = block_rows(4 * k + r)
    kv_ref[my_block, 0:384] = turn(raw[:, 0:384].astype(full), cosine, sine).astype(half)
    kv_ref[my_block, 384:768] = raw[:, 384:768]
    kv_gather = Gather(lambda b, h: kv_ref.at[part_rows(4 * k + b, h)], r, c, kv_s, kv_r)
    kv_gather.start()

    def kv_core(j, b):
        rows = block_rows(4 * k + b)
        return send(kv_ref.at[rows], kv_ref.at[rows], ck_s.at[j], ck_r.at[j], core)

    kv_core(3, r)
    q_scatter.relay()
    for copy in oz:
        copy.wait_recv()
    wo_gather = Gather(
        lambda b, h: wo_all.at[b, :, k] if h is None else wo_all.at[b, 2 * h : 2 * h + 2, k],
        r, c, po_s, po_r,
    )
    kv_gather.relay()
    raw = q_scatter.finish(q_own).astype(half)
    queries = turn(raw.astype(full), cosine, sine).astype(half)
    q_ref[...] = queries
    queries = queries * jnp.bfloat16(0.125)
    wo_gather.start()
    for m in range(2):
        kv_core(m, mates[m][0])
    bias = mask_bias(starts_ref, z, 512 * k + TB * r)
    kv_gather.finish()
    kv_core(2, mates[2][0])
    for j in range(4):
        b = r if j == 3 else mates[j][0]
        rows = block_rows(4 * (1 - k) + b)
        remote(kv_ref.at[rows], kv_ref.at[rows], ck_s.at[j], ck_r.at[j], core).wait_recv()
    cot_gather.finish()
    def wo_swap(j, b):
        return send(wo_all.at[b, :, k], wo_all.at[b, :, k], co_s.at[j], co_r.at[j], core)

    for g in range(KV_HEADS):
        if g == 4:
            wo_swap(3, r)
            wo_gather.relay()
            wo_swap(0, mates[0][0])
            wo_swap(1, mates[1][0])
        keys = kv_ref[:, 64 * g : 64 * g + 64]
        values = kv_ref[:, 384 + 64 * g : 448 + 64 * g]
        heads = jnp.concatenate(
            [queries[:, 64 * h : 64 * h + 64] for h in range(3 * g, 3 * g + 3)], axis=0
        )
        scores = product_right(heads, keys).reshape(3, TB, 1024) + bias[None]
        high = jnp.max(scores, axis=-1, keepdims=True)
        weights = jnp.exp(scores - high)
        total = jnp.sum(weights, axis=-1, keepdims=True)
        probs = (weights * (1.0 / total)).astype(half).reshape(3 * TB, 1024)
        lse_ref[g] = jnp.broadcast_to((high + jnp.log(total)).reshape(3 * TB, 1), (3 * TB, 128))
        output = product(probs, values)
        for j in range(3):
            h = 3 * g + j
            out_ref[:, 64 * h : 64 * h + 64] = output[TB * j : TB * j + TB]
    attended = out_ref[...].astype(half)

    wo_gather.finish()
    wo_swap(2, mates[2][0])
    for j in range(4):
        b = r if j == 3 else mates[j][0]
        remote(
            wo_all.at[b, :, 1 - k], wo_all.at[b, :, 1 - k], co_s.at[j], co_r.at[j], core
        ).wait_recv()
    for b in range(4):
        for i in range(4):
            for kk in range(2):
                for j in range(3):
                    row = 144 * (2 * i + kk) + 48 * j
                    wof_ref[row : row + 48, 288 * b : 288 * b + 288] = wo_all[
                        b, i, kk, :, 288 * j : 288 * j + 288
                    ]
    middle = hid[...] + product(attended, wof_ref[...])
    mid_ref[...] = middle
    for copy in gain_copies:
        copy.wait_recv()
    gain = jnp.concatenate([gain_parts[i] for i in range(4)], axis=1)
    gain_ref[...] = gain
    scale = lax.rsqrt(jnp.sum(middle * middle, axis=1, keepdims=True) / D + EPS)
    n2_ref[...] = (middle * scale * gain[0:1, :]).astype(half)

    @pl.when(gate_up.has)
    def _():
        tiled_ref[...] = tile[2]
        w_ref[:, :, tile_cols(3 * k + tile_place(r, k, z))] = tile[0:2]

    gate_up.finish()
    for copy in sent:
        copy.wait_send()
    for gather in (cot_gather, kv_gather, wo_gather, gate_up, kv_scatter, q_scatter):
        gather.sent()
    for flag, copy in tile_sends:

        @pl.when(flag)
        def _():
            copy.wait_send()


def attend_fast(*args):
    shape = jax.ShapeDtypeStruct
    v = pltpu.VMEM
    sems = []
    for count in (3, 4, 3, 3, 4, 4, 3, 4, 3, 6, 6, 4, 4, 3, 4, 3):
        sems += [pltpu.SemaphoreType.DMA((count,))] * 2
    return pl.pallas_call(
        attend_kernel,
        out_shape=(
            shape((TB, D), half),
            shape((TB, D), full),
            shape((D, 512), half),
            shape((2, D, 768), half),
            shape((D, 128), half),
            shape((8, D), full),
            shape((TB, D), half),
            shape((1024, 768), half),
            shape((KV_HEADS, 3 * TB, 128), full),
            shape((TB, D), full),
            shape((D, D), half),
            shape((288, 1920), half),
            shape((288, 512), half),
            shape((8, 512), full),
            shape((TB, 128), full),
        ),
        in_specs=[VM] * 11 + [SM],
        out_specs=(VM,) * 15,
        scratch_shapes=[
            v((288, 240), half),
            v((48, 864), half),
            v((3, 3, 288, 128), half),
            v((8, 288, 240), half),
            v((3, D, 128), half),
            v((D, TB), half),
            v((4, 8, 512), full),
            v((4, 8, 288), full),
            v((TB, 768), full),
            v((TB, D), full),
            v((4, 4, 2, 48, 864), half),
            v((TB, D), full),
        ]
        + scatter_buffers(768)
        + scatter_buffers(D)
        + sems,
        compiler_params=pltpu.CompilerParams(
            collective_id=1, has_side_effects=True, vmem_limit_bytes=60 << 20
        ),
    )(*args)


def feed_kernel(
    n2_ref, cot_ref, w_ref, tiled_ref, mid_ref, gain_ref,
    all_ref, d_ref, down_ref, gm_ref, gain_out, dwd_ref,
    wd, act, slope, swish, px_out, px_in, dwz, zin, temp, own_grad, b0, b1, b2, b3,
    a_s, a_r, s_s, s_r, zt_s, zt_r, ct_s, ct_r, px_s, px_r, z_s, z_r,
):
    r = lax.axis_index("row")
    c = lax.axis_index("col")
    z = c // 2
    k = lax.rem(c, 2)
    mates = [(mate(r, m), c) for m in (1, 2, 3)]
    aheads = [(r, z_ahead(c, m)) for m in (1, 2, 3)]
    ahead_z = [lax.rem(z + m, 4) for m in (1, 2, 3)]
    core = (r, other_core(c))
    ready = greet(mates + [core] + aheads)
    mine = block_rows(r)
    all_ref[mine, :] = n2_ref[...]
    downs = TileGather(
        tiled_ref, lambda slot: wd.at[:, tile_cols(slot)], r, c, zt_s, zt_r, ct_s, ct_r
    )
    gather = Gather(lambda b, h: all_ref.at[part_rows(b, h)], r, c, a_s, a_r)
    scatter = Scatter(b0, b1, b2, b3, r, c, s_s, s_r)
    ready()
    gather.start()

    @pl.when(downs.has)
    def _():
        downs.start()
        wd[:, tile_cols(3 * k + tile_place(r, k, z))] = tiled_ref[...]

    def up_to(b):
        rows = block_rows(b)
        normed = all_ref[rows, :]
        for j in range(3):
            cs = slice(256 * j, 256 * j + 256)
            gate = product(normed, w_ref[0, :, cs])
            up = product(normed, w_ref[1, :, cs])
            sigma = 1.0 / (1.0 + jnp.exp(-gate))
            hidden = gate * sigma
            act[rows, cs] = (hidden * up).astype(half)
            swish[rows, cs] = hidden
            slope[rows, cs] = up * (sigma * (1.0 + gate * (1.0 - sigma)))

    up_to(r)
    gather.relay()
    up_to(mates[0][0])
    up_to(mates[1][0])
    gather.finish()
    up_to(mates[2][0])

    def tile_grads(core_index):
        cols = pl.ds(pl.multiple_of(384 * core_index, 128), 384)
        return product(cot_ref[...], act[:, cols])

    part = tile_grads(1 - k)
    for j in range(3):
        px_out[j] = part[:, 128 * j : 128 * j + 128].astype(half)
    px_copy = remote(px_out, px_in, px_s.at[0], px_r.at[0], core)
    px_copy.start()
    part = tile_grads(k)
    px_copy.wait_recv()
    for j in range(3):
        value = part[:, 128 * j : 128 * j + 128] + px_in[j].astype(full)
        temp[j] = value
        dwz[j] = value.astype(half)
    z_sends = []
    for m in range(3):
        place = tile_place(r, k, ahead_z[m])
        copy = remote(dwz.at[place], zin.at[m], z_s.at[m], z_r.at[m], aheads[m])
        z_sends.append((has_tile(r, ahead_z[m], k), copy))

    downs.finish()
    for flag, copy in z_sends:

        @pl.when(flag)
        def _():
            copy.start()

    def back(b):
        rows = block_rows(b)
        cot = cot_ref[:, rows]
        for j in range(3):
            cs = slice(256 * j, 256 * j + 256)
            grad = product_left(cot, wd[:, cs])
            d_ref[0, rows, cs] = (grad * slope[rows, cs]).astype(half)
            d_ref[1, rows, cs] = (grad * swish[rows, cs]).astype(half)
        return product_right(d_ref[0, rows, :], w_ref[0]) + product_right(
            d_ref[1, rows, :], w_ref[1]
        )

    for m in (2, 0, 1):
        b0[m] = back(mates[m][0]).astype(half)
        scatter.start(((0,), (1,), (2, 3))[m])
    own_grad[...] = back(r)
    scatter.relay()
    for i in range(2):
        rows = slice(256 * i, 256 * i + 256)
        down_ref[rows, :] = product_right(act[rows, :], wd[...]).astype(half)
    hidden = mid_ref[...]
    gain = gain_ref[0:1, :]
    scale = lax.rsqrt(jnp.sum(hidden * hidden, axis=1, keepdims=True) / D + EPS)
    cot = jnp.transpose(cot_ref[:, mine].astype(full))
    grad = scatter.finish(own_grad)
    inner = jnp.sum(grad * gain * hidden, axis=1, keepdims=True)
    gm = cot + grad * gain * scale - hidden * (scale * scale * scale * inner / D)
    gm_ref[...] = gm.astype(half)
    gain_out[...] = jnp.broadcast_to(
        jnp.sum(grad * hidden * scale, axis=0, keepdims=True), gain_out.shape
    )

    @pl.when(downs.has)
    def _():
        value = temp[tile_place(r, k, z)]
        for m in range(3):
            remote(dwz.at[0], zin.at[m], z_s.at[m], z_r.at[m], aheads[m]).wait_recv()
            value = value + zin[m].astype(full)
        dwd_ref[...] = value

    gather.sent()
    scatter.sent()
    downs.sent()
    px_copy.wait_send()
    for flag, copy in z_sends:

        @pl.when(flag)
        def _():
            copy.wait_send()


def feed(*args):
    shape = jax.ShapeDtypeStruct
    v = pltpu.VMEM
    sems = []
    for count in (4, 6, 3, 4, 1, 3):
        sems += [pltpu.SemaphoreType.DMA((count,))] * 2
    return pl.pallas_call(
        feed_kernel,
        out_shape=(
            shape((512, D), half),
            shape((2, 512, 768), half),
            shape((512, D), half),
            shape((TB, D), half),
            shape((8, D), full),
            shape((D, 128), full),
        ),
        in_specs=[VM] * 6,
        out_specs=(VM,) * 6,
        scratch_shapes=[
            v((D, 768), half),
            v((512, 768), half),
            v((512, 768), full),
            v((512, 768), full),
            v((3, D, 128), half),
            v((3, D, 128), half),
            v((3, D, 128), half),
            v((3, D, 128), half),
            v((3, D, 128), full),
            v((TB, D), full),
        ]
        + scatter_buffers(D)
        + sems,
        compiler_params=pltpu.CompilerParams(
            collective_id=2, has_side_effects=True, vmem_limit_bytes=60 << 20
        ),
    )(*args)


def back_kernel(
    gm_ref, down_ref, mid_ref, n2_ref, d_ref, dwd_ref, q_ref, kv_ref, lse_ref, out_ref, wof_ref,
    wi_ref, n1_ref, srow_ref, sown_ref, tok_ref, gain1_ref, gain2_ref, cos_ref, sin_ref,
    starts_ref,
    bo_ref, ig_ref, dw_ref, dq_ref, do_ref, gains_ref,
    gm_out, gm_nat, bo_out, px_out, px_in, dwz, zin, own, temp, tile_out, att_all,
    dkv, dkv_co, dkv_ci, sd, dqs, dwq, dwq_co, dwq_ci, dwq_z, dwq_in,
    dwo, dwo_co, dwo_ci, dwo_z, dwo_in, g2_out, g2_in, gl, gl_ci, gl_z, gl_in, coef_all, dn_own,
    n0, n1, n2, n3, e0, e1, e2, e3,
    gm_s, gm_r, dn_s, dn_r, bo_s, bo_r, px_s, px_r, z_s, z_r, t_s, t_r, kc_s, kc_r, kp_s, kp_r,
    sd_s, sd_r, qc_s, qc_r, qz_s, qz_r, oc_s, oc_r, oz_s, oz_r, g2_s, g2_r, gc_s, gc_r, gz_s, gz_r,
    at_s, at_r, cf_s, cf_r,
):
    r = lax.axis_index("row")
    c = lax.axis_index("col")
    z = c // 2
    k = lax.rem(c, 2)
    mates = [(mate(r, m), c) for m in (1, 2, 3)]
    aheads = [(r, z_ahead(c, m)) for m in (1, 2, 3)]
    ahead_z = [lax.rem(z + m, 4) for m in (1, 2, 3)]
    core = (r, other_core(c))
    ready = greet(mates + [core] + aheads)
    mine = block_rows(r)
    sent = []

    def send(src, dst, send_sem, recv_sem, target):
        copy = remote(src, dst, send_sem, recv_sem, target)
        copy.start()
        sent.append(copy)
        return copy

    turned = jnp.transpose(gm_ref[...].astype(full)).astype(half)
    for i in range(4):
        gm_out[i] = turned[288 * i : 288 * i + 288]
        g2_out[i] = gain2_ref[:, 288 * i : 288 * i + 288]
    gm_nat[:, mine] = gm_out[r]
    attended = out_ref[...].astype(half)
    att_all[mine, :] = attended
    ready()
    def tile_grads(t, core_index):
        cols = pl.ds(pl.multiple_of(384 * core_index, 128), 384)
        return product_left(n2_ref[...], d_ref[t, :, cols])

    px_copies = []
    for t in range(2):
        part = tile_grads(t, 1 - k)
        for j in range(3):
            px_out[t, j] = part[:, 128 * j : 128 * j + 128].astype(half)
        px_copies.append(send(px_out.at[t], px_in.at[t], px_s.at[t], px_r.at[t], core))
        if t == 0:
            gm_copies = [
                send(gm_out.at[mates[m][0]], gm_nat.at[:, mine], gm_s.at[m], gm_r.at[m], mates[m])
                for m in range(3)
            ]
            g2_copies = [
                send(g2_out.at[mates[m][0]], g2_in.at[m], g2_s.at[m], g2_r.at[m], mates[m])
                for m in range(3)
            ]
            for m in range(3):
                n0[m] = down_ref[block_rows(mates[m][0]), :]
            downs = Scatter(n0, n1, n2, n3, r, c, dn_s, dn_r)
            downs.start()
            att_gather = Gather(lambda b, h: att_all.at[part_rows(b, h)], r, c, at_s, at_r)
            att_gather.start()
    mine_has = has_tile(r, z, k)
    my_place = tile_place(r, k, z)
    z_flags = []
    for t in range(2):
        part = tile_grads(t, k)
        px_copies[t].wait_recv()
        for j in range(3):
            value = part[:, 128 * j : 128 * j + 128] + px_in[t, j].astype(full)
            temp[j] = value
            dwz[t, j] = value.astype(half)
        own[t] = temp[my_place]
        for m in range(3):
            place = tile_place(r, k, ahead_z[m])
            copy = remote(
                dwz.at[t, place], zin.at[m, t], z_s.at[2 * m + t], z_r.at[2 * m + t], aheads[m]
            )
            flag = has_tile(r, ahead_z[m], k)
            z_flags.append((flag, copy))

            @pl.when(flag)
            def _():
                copy.start()

    ga = product_right(gm_ref[...], wof_ref[...]).astype(half)
    gaf = ga.astype(full)
    queries = q_ref[...] * jnp.bfloat16(0.125)
    bias = mask_bias(starts_ref, z, 512 * k + TB * r)
    for g in range(KV_HEADS):
        if g == 2:
            downs.relay()
        if g == 4:
            att_gather.relay()
        keys = kv_ref[:, 64 * g : 64 * g + 64]
        values = kv_ref[:, 384 + 64 * g : 448 + 64 * g]
        heads = range(3 * g, 3 * g + 3)
        qh = jnp.concatenate([queries[:, 64 * h : 64 * h + 64] for h in heads], axis=0)
        gh = jnp.concatenate([ga[:, 64 * h : 64 * h + 64] for h in heads], axis=0)
        delta = jnp.concatenate(
            [
                jnp.sum(
                    gaf[:, 64 * h : 64 * h + 64] * out_ref[:, 64 * h : 64 * h + 64],
                    axis=1,
                    keepdims=True,
                )
                for h in heads
            ],
            axis=0,
        )
        scores = product_right(qh, keys).reshape(3, TB, 1024) + bias[None]
        probs = jnp.exp(scores.reshape(3 * TB, 1024) - lse_ref[g][:, 0:1])
        grad_probs = product_right(gh, values)
        grad_scores = (probs * (grad_probs - delta)).astype(half)
        grad_q = product(grad_scores, keys) * 0.125
        for j in range(3):
            h = 3 * g + j
            dqs[:, 64 * h : 64 * h + 64] = grad_q[TB * j : TB * j + TB]
        dkv[:, 64 * g : 64 * g + 64] = product_left(grad_scores, qh)
        dkv[:, 384 + 64 * g : 448 + 64 * g] = product_left(probs.astype(half), gh)
    other_rows = pl.ds(pl.multiple_of(512 * (1 - k), 512), 512)
    dkv_co[...] = dkv[other_rows, :].astype(half)
    kc = send(dkv_co, dkv_ci, kc_s.at[0], kc_r.at[0], core)
    cosine = cos_ref[...]
    sine = -sin_ref[...]
    grad_q = dqs[...]
    inner = jnp.sum(grad_q * q_ref[...].astype(full), axis=1, keepdims=True)
    sd[mine, 0:1152] = turn(grad_q, cosine, sine).astype(half)
    kc.wait_recv()
    pairs = Scatter(e0, e1, e2, e3, r, c, kp_s, kp_r)
    for m in (2, 0, 1):
        b = mates[m][0]
        e0[m] = (dkv[block_rows(4 * k + b), :] + dkv_ci[block_rows(b), :].astype(full)).astype(half)
        pairs.start(((0,), (1,), (2, 3))[m])
    my_block = block_rows(4 * k + r)
    dkv[my_block, :] = dkv[my_block, :] + dkv_ci[mine, :].astype(full)
    dn_own[...] = mid_ref[...] + down_ref[mine, :].astype(full)
    result = downs.finish(dn_own)
    result = jnp.transpose(result).astype(half)
    for i in range(4):
        bo_out[i] = result[288 * i : 288 * i + 288]
    bo_ref[:, mine] = bo_out[r]
    pairs.relay()
    for m in range(3):
        cols = block_rows(mates[m][0])
        remote(gm_out.at[0], gm_nat.at[:, cols], gm_s.at[m], gm_r.at[m], mates[m]).wait_recv()
    grad_kv = pairs.finish(dkv[my_block, :])
    inner = inner + jnp.sum(grad_kv * kv_ref[my_block, :].astype(full), axis=1, keepdims=True)
    sd[mine, 1152:1536] = turn(grad_kv[:, 0:384], cosine, sine).astype(half)
    sd[mine, 1536:1920] = grad_kv[:, 384:768].astype(half)
    sd_gather = Gather(lambda b, h: sd.at[part_rows(b, h)], r, c, sd_s, sd_r)
    sd_gather.start()
    scale = sown_ref[...]
    coef = jnp.transpose(inner * (scale * scale) / D)
    coef_all[r] = coef[0:8]
    coef_copies = [
        send(coef_all.at[r], coef_all.at[r], cf_s.at[m], cf_r.at[m], mates[m]) for m in range(3)
    ]
    bo_copies = [
        send(bo_out.at[mates[m][0]], bo_ref.at[:, mine], bo_s.at[m], bo_r.at[m], mates[m])
        for m in range(3)
    ]
    att_gather.finish()
    grad_wo = lax.dot_general(
        att_all[...], gm_nat[...], (((0,), (1,)), ((), ())), preferred_element_type=full
    )
    for i in range(8):
        dwo[i] = grad_wo[144 * i : 144 * i + 144]
    for i in range(4):
        dwo_co[i] = dwo[2 * i + 1 - k].astype(half)
    oc_copy = send(dwo_co, dwo_ci, oc_s.at[0], oc_r.at[0], core)
    oc_copy.wait_recv()
    for i in range(4):
        value = dwo[2 * i + k] + dwo_ci[i].astype(full)
        dwo_z[i] = value.astype(half)
        dwo[2 * i + k] = value
    oz_copies = [
        send(dwo_z.at[ahead_z[m]], dwo_in.at[m], oz_s.at[m], oz_r.at[m], aheads[m])
        for m in range(3)
    ]
    sd_gather.relay()
    t_copies = [
        remote(
            tile_out.at[mates[m][0]], dw_ref.at[tile_of(r, z)], t_s.at[m], t_r.at[m], mates[m]
        )
        for m in range(3)
    ]

    @pl.when(mine_has)
    def _():
        for t in range(3):
            value = dwd_ref[...] if t == 2 else own[t]
            if t < 2:
                for m in range(3):
                    remote(
                        dwz.at[t, 0], zin.at[m, t], z_s.at[2 * m + t], z_r.at[2 * m + t], aheads[m]
                    ).wait_recv()
                    value = value + zin[m, t].astype(full)
            for b in range(4):
                tile_out[b, t] = value[288 * b : 288 * b + 288].astype(half)
        dw_ref[tile_of(r, z)] = tile_out[r]

    sd_gather.finish()

    @pl.when(mine_has)
    def _():
        for copy in t_copies:
            copy.start()

    grad_wi = product(n1_ref[...], sd[...])
    for i in range(8):
        dwq[i, :, 0:144] = grad_wi[:, 144 * i : 144 * i + 144]
        dwq[i, :, 144:192] = grad_wi[:, 1152 + 48 * i : 1200 + 48 * i]
        dwq[i, :, 192:240] = grad_wi[:, 1536 + 48 * i : 1584 + 48 * i]
    for i in range(4):
        dwq_co[i] = dwq[2 * i + 1 - k].astype(half)
    qc_copy = send(dwq_co, dwq_ci, qc_s.at[0], qc_r.at[0], core)
    back = product_right(wi_ref[...], sd[...]) * srow_ref[0:1, :]
    qc_copy.wait_recv()
    for i in range(4):
        value = dwq[2 * i + k] + dwq_ci[i].astype(full)
        dwq_z[i] = value.astype(half)
        dwq[2 * i + k] = value
    qz_copies = [
        send(dwq_z.at[ahead_z[m]], dwq_in.at[m], qz_s.at[m], qz_r.at[m], aheads[m])
        for m in range(3)
    ]
    for m in range(3):
        b = mates[m][0]
        remote(coef_all.at[b], coef_all.at[b], cf_s.at[m], cf_r.at[m], mates[m]).wait_recv()
    coef = jnp.concatenate([coef_all[i] for i in range(4)], axis=1)[0:1, :]
    tokens = tok_ref[...].astype(full)
    ig_ref[...] = (gm_nat[...].astype(full) + back * gain1_ref[:, 0:1] - tokens * coef).astype(half)
    for copy in g2_copies:
        copy.wait_recv()
    column = jnp.sum(back * tokens, axis=1, keepdims=True)
    gl[0] = jnp.transpose(jnp.broadcast_to(column, (288, 128)))[0:8]
    gl[1] = g2_out[r] + g2_in[0] + g2_in[1] + g2_in[2]
    gc_copy = send(gl, gl_ci, gc_s.at[0], gc_r.at[0], core)
    gc_copy.wait_recv()
    gl_z[...] = gl[...] + gl_ci[...]
    gz_copies = [send(gl_z, gl_in.at[m], gz_s.at[m], gz_r.at[m], aheads[m]) for m in range(3)]
    for m in range(3):
        oz_copies[m].wait_recv()
    total = dwo[2 * z + k]
    for m in range(3):
        total = total + dwo_in[m].astype(full)
    do_ref[...] = total
    for m in range(3):
        cols = block_rows(mates[m][0])
        remote(bo_out.at[0], bo_ref.at[:, cols], bo_s.at[m], bo_r.at[m], mates[m]).wait_recv()
    for m in range(3):
        b = mates[m][0]

        @pl.when(has_tile(b, z, k))
        def _():
            remote(
                tile_out.at[0], dw_ref.at[tile_of(b, z)], t_s.at[m], t_r.at[m], mates[m]
            ).wait_recv()

    total = dwq[2 * z + k]
    for m in range(3):
        qz_copies[m].wait_recv()
        total = total + dwq_in[m].astype(full)
    dq_ref[...] = total
    total = gl_z[...]
    for m in range(3):
        gz_copies[m].wait_recv()
        total = total + gl_in[m]
    gains_ref[...] = total
    for copy in sent:
        copy.wait_send()
    for part in (downs, att_gather, pairs, sd_gather):
        part.sent()
    for flag, copy in z_flags:

        @pl.when(flag)
        def _():
            copy.wait_send()

    @pl.when(mine_has)
    def _():
        for copy in t_copies:
            copy.wait_send()


def back(*args):
    shape = jax.ShapeDtypeStruct
    sems = []
    for count in (3, 6, 3, 2, 6, 3, 1, 6, 4, 1, 3, 1, 3, 3, 1, 3, 4, 3):
        sems += [pltpu.SemaphoreType.DMA((count,))] * 2
    v = pltpu.VMEM
    return pl.pallas_call(
        back_kernel,
        out_shape=(
            shape((288, 512), half),
            shape((288, 512), half),
            shape((3, 3, 288, 128), half),
            shape((288, 240), full),
            shape((144, 288), full),
            shape((2, 8, 288), full),
        ),
        in_specs=[VM] * 20 + [SM],
        out_specs=(VM,) * 6,
        scratch_shapes=[
            v((4, 288, TB), half),
            v((288, 512), half),
            v((4, 288, TB), half),
            v((2, 3, D, 128), half),
            v((2, 3, D, 128), half),
            v((2, 3, D, 128), half),
            v((3, 2, D, 128), half),
            v((2, D, 128), full),
            v((3, D, 128), full),
            v((4, 3, 288, 128), half),
            v((512, D), half),
            v((1024, 768), full),
            v((512, 768), half),
            v((512, 768), half),
            v((512, 1920), half),
            v((TB, D), full),
            v((8, 288, 240), full),
            v((4, 288, 240), half),
            v((4, 288, 240), half),
            v((4, 288, 240), half),
            v((3, 288, 240), half),
            v((8, 144, 288), full),
            v((4, 144, 288), half),
            v((4, 144, 288), half),
            v((4, 144, 288), half),
            v((3, 144, 288), half),
            v((4, 8, 288), full),
            v((3, 8, 288), full),
            v((2, 8, 288), full),
            v((2, 8, 288), full),
            v((2, 8, 288), full),
            v((3, 2, 8, 288), full),
            v((4, 8, TB), full),
            v((TB, D), full),
        ]
        + scatter_buffers(D)
        + scatter_buffers(768)
        + sems,
        compiler_params=pltpu.CompilerParams(
            collective_id=3, has_side_effects=True, vmem_limit_bytes=60 << 20
        ),
    )(*args)


def update_kernel(
    bo_in, ig_in, dw_ref, dq_ref, do_ref, dg_ref,
    g_w, g_m, g_v, q_w, q_m, q_v, kv_w, kv_m, kv_v, o_w, o_m, o_v, gu_w, gu_m, gu_v, d_w, d_m, d_v,
    bo_out, ig_out, g_nm, g_nv, g_nw, q_nm, q_nv, q_nw, q_low, kv_nm, kv_nv, kv_nw, kv_low,
    o_nm, o_nv, o_nw, o_low, gu_nm, gu_nv, gu_nw, gu_low, d_nm, d_nv, d_nw, d_low,
):
    fix = 1.0 - BETA**STEP

    def step(at, grad, rate, decay, ins, outs):
        weight = ins[0][at]
        first = BETA * ins[1][at] + (1.0 - BETA) * grad
        second = BETA * ins[2][at] + (1.0 - BETA) * grad * grad
        change = first / fix / (jnp.sqrt(second / fix) + TINY)
        weight = weight - rate * (change + decay * weight)
        outs[0][at] = first
        outs[1][at] = second
        outs[2][at] = weight
        if len(outs) == 4:
            outs[3][at] = weight.astype(half)

    bo_out[...] = bo_in[...]
    ig_out[...] = ig_in[...]
    rate = D**-0.5
    every = (slice(None), slice(None))
    step(every, jnp.concatenate([dg_ref[0, 0:1], dg_ref[1, 0:1]], axis=0), 0.25, 0.0,
         (g_w, g_m, g_v), (g_nm, g_nv, g_nw))
    for i in range(3):
        cols = (slice(None), slice(128 * i, 128 * i + 128))
        for t in range(2):
            step((t,) + cols, dw_ref[i, t].astype(full), rate, DECAY,
                 (gu_w, gu_m, gu_v), (gu_nm, gu_nv, gu_nw, gu_low))
        step(cols, dw_ref[i, 2].astype(full), FF**-0.5, DECAY,
             (d_w, d_m, d_v), (d_nm, d_nv, d_nw, d_low))
    step(every, do_ref[...], rate, DECAY, (o_w, o_m, o_v), (o_nm, o_nv, o_nw, o_low))
    turned = jnp.transpose(dq_ref[...])
    step(every, turned[0:144], rate, DECAY, (q_w, q_m, q_v), (q_nm, q_nv, q_nw, q_low))
    for t in range(2):
        step((t, slice(None), slice(None)), turned[144 + 48 * t : 192 + 48 * t], rate, DECAY,
             (kv_w, kv_m, kv_v), (kv_nm, kv_nv, kv_nw, kv_low))


def update(*args):
    shape = jax.ShapeDtypeStruct
    outs = [shape((288, 512), half)] * 2 + [shape((2, 288), full)] * 3
    for dims in ((144, 288), (2, 48, 288), (144, 288), (2, 288, 384), (288, 384)):
        outs += [shape(dims, full)] * 3 + [shape(dims, half)]
    return pl.pallas_call(
        update_kernel,
        out_shape=tuple(outs),
        in_specs=[VM] * 24,
        out_specs=(VM,) * len(outs),
        compiler_params=pltpu.CompilerParams(vmem_limit_bytes=48 << 20),
    )(*args)


def swap(value):
    return jnp.swapaxes(value, -1, -2)


def local_fast(
    tokens,
    cotangent,
    starts,
    gains,
    gains_m,
    gains_v,
    w_query,
    w_query_m,
    w_query_v,
    w_keyval,
    w_keyval_m,
    w_keyval_v,
    w_output,
    w_output_m,
    w_output_v,
    w_gateup,
    w_gateup_m,
    w_gateup_v,
    w_down,
    w_down_m,
    w_down_v,
):
    r = lax.axis_index("row")
    k = lax.rem(lax.axis_index("col"), 2)
    tok = swap(tokens)
    gain_one = jnp.broadcast_to(gains[0][:, None], (288, 128))
    gain_two = jnp.broadcast_to(gains[1][None], (8, 288))
    places = 512 * k + TB * r + jnp.arange(TB, dtype=jnp.int32)
    cosine, sine = rotary(places.astype(jnp.float32))
    cosine = jnp.concatenate([cosine] * 4, axis=1)
    sine = jnp.concatenate([-sine, sine, -sine, sine], axis=1)
    n2, mid, cot, w, tiled, gain, q, kv, lse, out, wof, wi, n1, srow, sown = attend_fast(
        tok, swap(cotangent), swap(w_query), swap(w_keyval), w_output, w_gateup, swap(w_down),
        gain_one, gain_two, cosine, sine, starts
    )
    n2_all, d, down, gm, gain_two_grad, dwd = feed(n2, cot, w, tiled, mid, gain)
    grads = back(
        gm, down, mid, n2_all, d, dwd, q, kv, lse, out, wof, wi, n1, srow, sown, tok, gain_one,
        gain_two_grad, cosine, sine, starts
    )
    outs = update(
        *grads, gains, gains_m, gains_v, swap(w_query), swap(w_query_m), swap(w_query_v),
        swap(w_keyval), swap(w_keyval_m), swap(w_keyval_v), w_output, w_output_m, w_output_v,
        w_gateup, w_gateup_m, w_gateup_v, swap(w_down), swap(w_down_m), swap(w_down_v)
    )
    turned = (0, 1, 5, 6, 7, 8, 9, 10, 11, 12, 21, 22, 23, 24)
    return tuple(swap(value) if i in turned else value for i, value in enumerate(outs))


def local(tokens, *others):
    fits = lax.axis_size("row") == 4 and lax.axis_size("col") == 8 and tokens.shape == (512, 288)
    plan = local_fast if fits else local_general
    return plan(tokens, *others)


def solution(mesh):
    return jax.shard_map(
        local,
        mesh=mesh,
        in_specs=(
            P("col", "row"),
            P("col", "row"),
            P(),
            P(None, "row"),
            P(None, "row"),
            P(None, "row"),
            P("row", "col"),
            P("row", "col"),
            P("row", "col"),
            P(None, "row", "col"),
            P(None, "row", "col"),
            P(None, "row", "col"),
            P("col", "row"),
            P("col", "row"),
            P("col", "row"),
            P(None, "row", "col"),
            P(None, "row", "col"),
            P(None, "row", "col"),
            P("col", "row"),
            P("col", "row"),
            P("col", "row"),
        ),
        out_specs=(
            P("col", "row"),
            P("col", "row"),
            P(None, "row"),
            P(None, "row"),
            P(None, "row"),
            P("row", "col"),
            P("row", "col"),
            P("row", "col"),
            P("row", "col"),
            P(None, "row", "col"),
            P(None, "row", "col"),
            P(None, "row", "col"),
            P(None, "row", "col"),
            P("col", "row"),
            P("col", "row"),
            P("col", "row"),
            P("col", "row"),
            P(None, "row", "col"),
            P(None, "row", "col"),
            P(None, "row", "col"),
            P(None, "row", "col"),
            P("col", "row"),
            P("col", "row"),
            P("col", "row"),
            P("col", "row"),
        ),
        check_vma=False,
    )
```

```python
import jax
import jax.numpy as jnp
from jax import lax
from jax.experimental import pallas as pl
from jax.experimental.pallas import tpu as pltpu
from jax.sharding import PartitionSpec as P

D = 1152
HEADS = 18
KV_HEADS = 6
HD = 64
FF = 3072
TD = 128
PIECE = 256
PIECES = 4
STEP = 7


EPS = 1e-05
BETA = 0.5
TINY = 1e-08
DECAY = 0.1
MASKED = -1e30


def to_half(value):
    return value.astype(jnp.bfloat16)


def product(left, right):
    return jnp.dot(left, right, preferred_element_type=jnp.float32)


def product_left(left, right):
    return lax.dot_general(
        left, right, (((0,), (0,)), ((), ())), preferred_element_type=jnp.float32
    )


def product_right(left, right):
    return lax.dot_general(
        left, right, (((1,), (1,)), ((), ())), preferred_element_type=jnp.float32
    )


def col_collect(value):
    return lax.all_gather(value, "col", axis=0, tiled=True)


def row_collect(value):
    return lax.all_gather(value, "row", axis=0, tiled=True)


def row_reduce(value):
    return lax.psum_scatter(value, "row", scatter_dimension=0, tiled=True)


def col_reduce(value):
    return lax.psum_scatter(value, "col", scatter_dimension=0, tiled=True)


def row_total(value):
    return lax.psum(value, "row")


def to_heads(value):
    return lax.all_to_all(value, "col", split_axis=0, concat_axis=1, tiled=True)


def to_rows(value):
    return lax.all_to_all(value, "col", split_axis=1, concat_axis=0, tiled=True)


def norm_forward(hidden, gain):
    total = row_total(jnp.sum(hidden * hidden, axis=1))
    scale = lax.rsqrt(total / D + EPS)
    return (scale, to_half(hidden * scale[:, None] * gain[None, :]))


def norm_backward(hidden, gain, scale, grad):
    inner = row_total(jnp.sum(grad * gain[None, :] * hidden, axis=1))
    back = (
        grad * gain[None, :] * scale[:, None]
        - hidden * (scale * scale * scale * inner / D)[:, None]
    )
    gain_grad = jnp.sum(grad * hidden * scale[:, None], axis=0)
    return (back, gain_grad)


def rotary(places):
    half = HD // 2
    freq = 10000.0 ** (-2.0 * jnp.arange(half, dtype=jnp.float32) / HD)
    angle = places[:, None] * freq[None, :]
    return (jnp.cos(angle), jnp.sin(angle))


def rotate(heads, cosine, sine):
    half = HD // 2
    first = heads[..., :half]
    second = heads[..., half:]
    cosine = cosine[:, None, :]
    sine = sine[:, None, :]
    return jnp.concatenate(
        [first * cosine - second * sine, second * cosine + first * sine], axis=-1
    )


def rotate_back(heads, cosine, sine):
    half = HD // 2
    first = heads[..., :half]
    second = heads[..., half:]
    cosine = cosine[:, None, :]
    sine = sine[:, None, :]
    return jnp.concatenate(
        [first * cosine + second * sine, second * cosine - first * sine], axis=-1
    )


def piece_ids(pieces, places):
    inside = (places[:, None] >= pieces[None, :]) & (places[:, None] < pieces[None, :] + PIECE)
    number = jnp.arange(1, PIECES + 1, dtype=jnp.int32)
    return jnp.sum(jnp.where(inside, number[None, :], 0), axis=1) - 1


def block_scores(queries, keys, places, ids, pieces, start):
    key_places = start + jnp.arange(keys.shape[0], dtype=jnp.int32)
    key_ids = piece_ids(pieces, key_places)
    raw = jnp.einsum("tkgd,skd->kgts", queries, keys, preferred_element_type=jnp.float32) * HD ** (
        -0.5
    )
    allowed = (key_places[None, :] <= places[:, None]) | (key_ids[None, :] == ids[:, None]) & (
        ids[:, None] >= 0
    )
    allowed = allowed[None, None]
    return (jnp.where(allowed, raw, MASKED), allowed)


def split_blocks(keyvals, width):
    count = keyvals.shape[0] // width
    blocks = keyvals.reshape(count, width, 2, KV_HEADS, HD)
    firsts = jnp.arange(count, dtype=jnp.int32) * width
    return (blocks, firsts)


def attend(queries, keyvals, places, ids, pieces, width):
    blocks, firsts = split_blocks(keyvals, width)
    shape = (KV_HEADS, queries.shape[2], queries.shape[0])

    def measure(carry, item):
        high, total = carry
        scores, allowed = block_scores(queries, item[0][:, 0], places, ids, pieces, item[1])
        new_high = jnp.maximum(high, jnp.max(scores, axis=-1))
        weights = jnp.where(allowed, jnp.exp(scores - new_high[..., None]), 0.0)
        return ((new_high, total * jnp.exp(high - new_high) + jnp.sum(weights, axis=-1)), None)

    start_state = (jnp.full(shape, MASKED, jnp.float32), jnp.zeros(shape, jnp.float32))
    (high, total), unused = lax.scan(measure, start_state, (blocks, firsts))
    logsum = high + jnp.log(total)

    def accumulate(acc, item):
        scores, allowed = block_scores(queries, item[0][:, 0], places, ids, pieces, item[1])
        probs = to_half(jnp.where(allowed, jnp.exp(scores - logsum[..., None]), 0.0))
        return (
            acc
            + jnp.einsum(
                "kgts,skd->tkgd", probs, item[0][:, 1], preferred_element_type=jnp.float32
            ),
            None,
        )

    output, unused = lax.scan(accumulate, jnp.zeros(queries.shape, jnp.float32), (blocks, firsts))
    return (output, logsum)


def attend_back(queries, keyvals, places, ids, pieces, width, logsum, grad_out, output):
    blocks, firsts = split_blocks(keyvals, width)
    delta = jnp.einsum("tkgd,tkgd->kgt", grad_out.astype(jnp.float32), output)
    factor = HD ** (-0.5)

    def sweep(acc, item):
        keys = item[0][:, 0]
        values = item[0][:, 1]
        scores, allowed = block_scores(queries, keys, places, ids, pieces, item[1])
        probs = jnp.where(allowed, jnp.exp(scores - logsum[..., None]), 0.0)
        grad_probs = jnp.einsum(
            "tkgd,skd->kgts", grad_out, values, preferred_element_type=jnp.float32
        )
        grad_scores = to_half(probs * (grad_probs - delta[..., None]))
        acc = (
            acc
            + jnp.einsum("kgts,skd->tkgd", grad_scores, keys, preferred_element_type=jnp.float32)
            * factor
        )
        grad_keys = (
            jnp.einsum("kgts,tkgd->skd", grad_scores, queries, preferred_element_type=jnp.float32)
            * factor
        )
        grad_values = jnp.einsum(
            "kgts,tkgd->skd", to_half(probs), grad_out, preferred_element_type=jnp.float32
        )
        joined = jnp.concatenate(
            [grad_keys.reshape(width, -1), grad_values.reshape(width, -1)], axis=1
        )
        return (acc, joined)

    grad_queries, grad_blocks = lax.scan(
        sweep, jnp.zeros(queries.shape, jnp.float32), (blocks, firsts)
    )
    return (grad_queries, grad_blocks.reshape(keyvals.shape[0], -1))


def adamw(weight, first, second, grad, rate, decay):
    first_new = BETA * first + (1.0 - BETA) * grad
    second_new = BETA * second + (1.0 - BETA) * grad * grad
    fix = 1.0 - BETA**STEP
    update = first_new / fix / (jnp.sqrt(second_new / fix) + TINY)
    weight_new = weight - rate * (update + decay * weight)
    return (first_new, second_new, weight_new)


def grid_plan(tokens, cotangent, starts, gains, w_query, w_keyval, w_output, w_gateup, w_down):
    columns = lax.axis_size("col")
    column = lax.axis_index("col")
    seq_len = TD * columns
    width = min(1024, seq_len)
    group = HEADS // KV_HEADS
    query_width = w_query.shape[1]
    key_width = w_keyval.shape[2]
    feed_width = w_gateup.shape[2]
    pieces = lax.dynamic_index_in_dim(starts, lax.axis_index("row"), 0, keepdims=False)
    hidden = tokens.astype(jnp.float32)
    inner_weights = to_half(jnp.concatenate([w_query, w_keyval[0], w_keyval[1]], axis=1))
    feed_weights = to_half(jnp.concatenate([w_gateup[0], w_gateup[1]], axis=1))
    out_weights = to_half(w_output)
    down_weights = to_half(w_down)
    scale_one, normed_one = norm_forward(hidden, gains[0])
    gathered_one = col_collect(normed_one)
    mixed = to_half(row_reduce(product(gathered_one, inner_weights)))
    spread = to_heads(mixed[:, None, :])
    query_raw = spread[:, :, :query_width].reshape(TD, HEADS, HD)
    key_raw = spread[:, :, query_width : query_width + key_width].reshape(TD, KV_HEADS, HD)
    value_heads = spread[:, :, query_width + key_width :].reshape(TD, KV_HEADS * HD)
    places = column * TD + jnp.arange(TD, dtype=jnp.int32)
    cosine, sine = rotary(places.astype(jnp.float32))
    queries = to_half(rotate(query_raw.astype(jnp.float32), cosine, sine)).reshape(
        TD, KV_HEADS, group, HD
    )
    keys = to_half(rotate(key_raw.astype(jnp.float32), cosine, sine))
    keyvals_local = jnp.concatenate([keys.reshape(TD, KV_HEADS * HD), value_heads], axis=1)
    keyvals = lax.all_gather(keyvals_local, "col", axis=0, tiled=True)
    ids = piece_ids(pieces, places)
    output, logsum = attend(queries, keyvals, places, ids, pieces, width)
    attended = to_half(output)
    attended_rows = to_rows(attended.reshape(TD, columns, query_width))[:, 0, :]
    gathered_att = row_collect(attended_rows)
    branch = col_reduce(product(gathered_att, out_weights))
    middle = hidden + branch
    scale_two, normed_two = norm_forward(middle, gains[1])
    gathered_two = col_collect(normed_two)
    feed = row_reduce(product(gathered_two, feed_weights))
    gate = feed[:, :feed_width]
    upward = feed[:, feed_width:]
    sigma = jax.nn.sigmoid(gate)
    swish = gate * sigma
    activated = to_half(swish * upward)
    gathered_act = row_collect(activated)
    result = middle + col_reduce(product(gathered_act, down_weights))
    block_out = to_half(result)
    both = lax.all_gather(jnp.stack([normed_one, normed_two]), "col", axis=1, tiled=True)
    back_one = both[0]
    back_two = both[1]
    grad_rows = col_collect(cotangent)
    grad_down = product_left(gathered_act, grad_rows)
    grad_act = row_reduce(product_right(grad_rows, down_weights))
    slope = sigma * (1.0 + gate * (1.0 - sigma))
    grad_feed = to_half(jnp.concatenate([grad_act * upward * slope, grad_act * swish], axis=1))
    gathered_feed = row_collect(grad_feed)
    grad_both = product_left(back_two, gathered_feed)
    grad_gateup = jnp.stack([grad_both[:, :feed_width], grad_both[:, feed_width:]])
    grad_normed_two = col_reduce(product_right(gathered_feed, feed_weights))
    norm_two_back, gain_two = norm_backward(middle, gains[1], scale_two, grad_normed_two)
    grad_middle = cotangent.astype(jnp.float32) + norm_two_back
    gathered_mid = col_collect(to_half(grad_middle))
    grad_output = product_left(gathered_att, gathered_mid)
    grad_att = to_half(row_reduce(product_right(gathered_mid, out_weights)))
    grad_heads = to_heads(grad_att[:, None, :]).reshape(TD, KV_HEADS, group, HD)
    keyvals_back = lax.all_gather(keyvals_local, "col", axis=0, tiled=True)
    grad_queries, grad_keyvals = attend_back(
        queries, keyvals_back, places, ids, pieces, width, logsum, grad_heads, output
    )
    local_keyvals = lax.psum_scatter(grad_keyvals, "col", scatter_dimension=0, tiled=True)
    kv_split = KV_HEADS * HD
    grad_query_raw = rotate_back(grad_queries.reshape(TD, HEADS, HD), cosine, sine)
    grad_key_raw = rotate_back(local_keyvals[:, :kv_split].reshape(TD, KV_HEADS, HD), cosine, sine)
    grad_value = local_keyvals[:, kv_split:]
    joined = jnp.concatenate(
        [
            to_half(grad_query_raw).reshape(TD, columns, query_width),
            to_half(grad_key_raw).reshape(TD, columns, key_width),
            to_half(grad_value).reshape(TD, columns, key_width),
        ],
        axis=2,
    )
    grad_mixed = to_rows(joined)[:, 0, :]
    gathered_mixed = row_collect(grad_mixed)
    grad_inner = product_left(back_one, gathered_mixed)
    grad_query = grad_inner[:, :query_width]
    grad_keyval = jnp.stack(
        [
            grad_inner[:, query_width : query_width + key_width],
            grad_inner[:, query_width + key_width :],
        ]
    )
    grad_normed_one = col_reduce(product_right(gathered_mixed, inner_weights))
    norm_one_back, gain_one = norm_backward(hidden, gains[0], scale_one, grad_normed_one)
    input_grad = to_half(grad_middle + norm_one_back)
    gain_grads = lax.psum(jnp.stack([gain_one, gain_two]), "col")
    return (
        block_out,
        input_grad,
        gain_grads,
        grad_query,
        grad_keyval,
        grad_output,
        grad_gateup,
        grad_down,
    )


def local_general(
    tokens,
    cotangent,
    starts,
    gains,
    gains_m,
    gains_v,
    w_query,
    w_query_m,
    w_query_v,
    w_keyval,
    w_keyval_m,
    w_keyval_v,
    w_output,
    w_output_m,
    w_output_v,
    w_gateup,
    w_gateup_m,
    w_gateup_v,
    w_down,
    w_down_m,
    w_down_v,
):
    results = grid_plan(
        tokens, cotangent, starts, gains, w_query, w_keyval, w_output, w_gateup, w_down
    )
    (
        block_out,
        input_grad,
        gain_grads,
        grad_query,
        grad_keyval,
        grad_output,
        grad_gateup,
        grad_down,
    ) = results
    rate_in = D ** (-0.5)
    rate_down = FF ** (-0.5)
    gain_m, gain_v, gain_w = adamw(gains, gains_m, gains_v, gain_grads, 0.25, 0.0)
    query_m, query_v, query_w = adamw(w_query, w_query_m, w_query_v, grad_query, rate_in, DECAY)
    keyval_m, keyval_v, keyval_w = adamw(
        w_keyval, w_keyval_m, w_keyval_v, grad_keyval, rate_in, DECAY
    )
    output_m, output_v, output_w = adamw(
        w_output, w_output_m, w_output_v, grad_output, rate_in, DECAY
    )
    gateup_m, gateup_v, gateup_w = adamw(
        w_gateup, w_gateup_m, w_gateup_v, grad_gateup, rate_in, DECAY
    )
    down_m, down_v, down_w = adamw(w_down, w_down_m, w_down_v, grad_down, rate_down, DECAY)
    return (
        block_out,
        input_grad,
        gain_m,
        gain_v,
        gain_w,
        query_m,
        query_v,
        query_w,
        to_half(query_w),
        keyval_m,
        keyval_v,
        keyval_w,
        to_half(keyval_w),
        output_m,
        output_v,
        output_w,
        to_half(output_w),
        gateup_m,
        gateup_v,
        gateup_w,
        to_half(gateup_w),
        down_m,
        down_v,
        down_w,
        to_half(down_w),
    )


TB = 128
LOG_BASE = 9.210340371976184
MESH = pl.DeviceIdType.MESH
half = jnp.bfloat16
full = jnp.float32
VM = pl.BlockSpec(memory_space=pltpu.VMEM)
SM = pl.BlockSpec(memory_space=pltpu.SMEM)


def mate(r, m):
    x = lax.rem(lax.rem(r, 2) + lax.rem(m, 2), 2)
    y = lax.rem(r // 2 + m // 2, 2)
    return 2 * y + x


def other_core(c):
    return c + 1 - 2 * lax.rem(c, 2)


def z_ahead(c, m):
    return lax.rem(c + 2 * m, 8)


def block_rows(b):
    return pl.ds(pl.multiple_of(b * TB, TB), TB)


def part_rows(b, h):
    if h is None:
        return block_rows(b)
    return pl.ds(pl.multiple_of(b * TB + 64 * h, 64), 64)


def slice_rows(b, h=None):
    if h is None:
        return pl.ds(pl.multiple_of(b * 288, 32), 288)
    return pl.ds(pl.multiple_of(b * 288 + 144 * h, 16), 144)


def greet(targets):
    barrier = pltpu.get_barrier_semaphore()
    for target in targets:
        pl.semaphore_signal(barrier, inc=1, device_id=target, device_id_type=MESH)
    return lambda: pl.semaphore_wait(barrier, len(targets))


def remote(src, dst, send, recv, target):
    return pltpu.make_async_remote_copy(
        src_ref=src, dst_ref=dst, send_sem=send, recv_sem=recv, device_id=target, device_id_type=MESH
    )


class Gather:
    def __init__(self, view, r, c, send, recv):
        x, y, far = mate(r, 1), mate(r, 2), mate(r, 3)
        self.first = [
            remote(view(r, None), view(r, None), send.at[0], recv.at[0], (x, c)),
            remote(view(r, None), view(r, None), send.at[1], recv.at[1], (y, c)),
        ]
        self.onward = [
            remote(view(x, 0), view(x, 0), send.at[2], recv.at[2], (y, c)),
            remote(view(y, 1), view(y, 1), send.at[3], recv.at[3], (x, c)),
        ]
        self.arrive = [
            remote(view(x, None), view(x, None), send.at[0], recv.at[0], (x, c)),
            remote(view(y, None), view(y, None), send.at[1], recv.at[1], (y, c)),
            remote(view(far, 0), view(far, 0), send.at[2], recv.at[2], (y, c)),
            remote(view(far, 1), view(far, 1), send.at[3], recv.at[3], (x, c)),
        ]

    def start(self):
        for copy in self.first:
            copy.start()

    def relay(self):
        for i in range(2):
            self.arrive[i].wait_recv()
            self.onward[i].start()

    def finish(self):
        self.arrive[2].wait_recv()
        self.arrive[3].wait_recv()

    def sent(self):
        for copy in self.first + self.onward:
            copy.wait_send()


class Scatter:
    def __init__(self, out, near, mid, last, r, c, send, recv):
        x, y = (mate(r, 1), c), (mate(r, 2), c)
        up, low = pl.ds(0, 64), pl.ds(64, 64)
        self.out, self.near, self.mid, self.last = out, near, mid, last
        self.first = [
            remote(out.at[0, up], near.at[0, 0], send.at[0], recv.at[0], x),
            remote(out.at[1, low], near.at[1, 0], send.at[1], recv.at[1], y),
            remote(out.at[2, up], near.at[0, 1], send.at[2], recv.at[2], x),
            remote(out.at[2, low], near.at[1, 1], send.at[3], recv.at[3], y),
        ]
        self.second = [
            remote(mid.at[0], last.at[0], send.at[4], recv.at[4], y),
            remote(mid.at[1], last.at[1], send.at[5], recv.at[5], x),
        ]

    def start(self, which=(2, 3, 0, 1)):
        for i in which:
            self.first[i].start()

    def relay(self):
        self.first[2].wait_recv()
        self.mid[0] = (self.out[1, 0:64].astype(full) + self.near[0, 1].astype(full)).astype(half)
        self.second[0].start()
        self.first[3].wait_recv()
        self.mid[1] = (self.out[0, 64:128].astype(full) + self.near[1, 1].astype(full)).astype(half)
        self.second[1].start()

    def finish(self, own):
        for copy in self.first[:2] + self.second:
            copy.wait_recv()
        upper = own[0:64] + self.near[0, 0].astype(full) + self.last[0].astype(full)
        lower = own[64:128] + self.near[1, 0].astype(full) + self.last[1].astype(full)
        return jnp.concatenate([upper, lower], axis=0)

    def sent(self):
        for copy in self.first + self.second:
            copy.wait_send()


def scatter_buffers(width):
    v = pltpu.VMEM
    return [
        v((3, TB, width), half),
        v((2, 2, 64, width), half),
        v((2, 64, width), half),
        v((2, 64, width), half),
    ]


def idle_plane(r, k):
    x = lax.rem(r, 2)
    return 2 * (1 - lax.rem(x + k, 2)) + 1 - r // 2


def tile_place(r, k, z):
    return jnp.minimum(lax.rem(z - idle_plane(r, k) + 3, 4), 2)


def has_tile(b, z, k):
    return (b // 2 == lax.rem(z, 2)) | (lax.rem(b, 2) == lax.rem(k + z // 2, 2))


def tile_of(b, z):
    return jnp.where(b // 2 == lax.rem(z, 2), lax.rem(b, 2), 2)


def tile_cols(place):
    return pl.ds(pl.multiple_of(place * 128, 128), 128)


class TileGather:
    def __init__(self, mine, view, r, c, zs, zr, cs, cr):
        self.r, self.z, self.k = r, c // 2, lax.rem(c, 2)
        core = (r, other_core(c))
        z, k = self.z, self.k
        self.has = has_tile(r, z, k)
        here = view(3 * k + tile_place(r, k, z))
        self.out = [remote(mine, here, zs.at[m], zr.at[m], (r, z_ahead(c, m + 1))) for m in range(3)]
        self.out.append(remote(mine, here, cs.at[3], cr.at[3], core))
        self.relays = []
        for m in range(3):
            src = lax.rem(z + 3 - m, 4)
            slot = view(3 * k + tile_place(r, k, src))
            self.relays.append(
                (
                    has_tile(r, src, k),
                    remote(slot, slot, zs.at[m], zr.at[m], core),
                    remote(slot, slot, cs.at[m], cr.at[m], core),
                )
            )
        self.others = []
        for m in range(4):
            src = z if m == 3 else lax.rem(z + 3 - m, 4)
            slot = view(3 * (1 - k) + tile_place(r, 1 - k, src))
            self.others.append(
                (has_tile(r, src, 1 - k), remote(slot, slot, cs.at[m], cr.at[m], core))
            )

    def start(self):
        for copy in self.out:
            copy.start()

    def relay(self):
        for flag, come, go in self.relays:

            @pl.when(flag)
            def _():
                come.wait_recv()
                go.start()

    def finish(self):
        for flag, come in self.others:

            @pl.when(flag)
            def _():
                come.wait_recv()

    def sent(self):
        @pl.when(self.has)
        def _():
            for copy in self.out:
                copy.wait_send()

        for flag, come, go in self.relays:

            @pl.when(flag)
            def _():
                go.wait_send()


def turn(value, cosine, sine):
    lane = lax.broadcasted_iota(jnp.int32, (value.shape[0], 128), 1)
    first = lax.rem(lane, 64) < 32
    parts = []
    for i in range(value.shape[1] // 128):
        part = value[:, 128 * i : 128 * i + 128]
        swapped = jnp.where(first, pltpu.roll(part, 96, 1), pltpu.roll(part, 32, 1))
        parts.append(part * cosine + swapped * sine)
    return jnp.concatenate(parts, axis=1)


def turn_tables(base):
    lane = lax.broadcasted_iota(jnp.int32, (TB, 128), 1)
    place = (lax.broadcasted_iota(jnp.int32, (TB, 128), 0) + base).astype(full)
    power = lax.rem(lane, 32).astype(full) * (-2.0 / HD)
    angle = place * jnp.exp(power * LOG_BASE)
    sine = jnp.sin(angle)
    return jnp.cos(angle), jnp.where(lax.rem(lane, 64) < 32, -sine, sine)


def mask_bias(starts_ref, seq, base):
    keys = lax.broadcasted_iota(jnp.int32, (1, 1024), 1)
    rows = lax.broadcasted_iota(jnp.int32, (TB, 1), 0) + base
    key_id = jnp.zeros((1, 1024), jnp.int32)
    row_id = jnp.zeros((TB, 1), jnp.int32)
    for j in range(PIECES):
        first = starts_ref[seq, j]
        key_id = key_id + jnp.where((keys >= first) & (keys < first + PIECE), j + 1, 0)
        row_id = row_id + jnp.where((rows >= first) & (rows < first + PIECE), j + 1, 0)
    row_id = jnp.where(row_id == 0, -1, row_id)
    allowed = (keys <= rows) | (key_id == row_id)
    return jnp.where(allowed, 0.0, MASKED)


def forward_kernel(
    tok_ref, cot_ref, wq_ref, wkv_ref, wo_ref, wgu_ref, wd_ref, gains_ref, starts_ref,
    mid_ref, q_ref, kv_ref, lse_ref, out_ref, wof_ref, wi_ref, n1_ref, srow_ref, sown_ref,
    down_ref, gm_ref, att_all, gain_out, dwz, dwd_ref,
    gain2_src, cotall_ref, w_ref, all_ref, d_ref, wd, act, slope, swish, px_out, px_in, dwzd, zin,
    tempd, own_grad, b0, b1, b2, b3,
    wsrc, osrc, w3, blk, tile, tok_own, sums, gain_parts, kv_own, q_own, wo_all,
    hid, kvb0, kvb1, kvb2, kvb3, qb0, qb1, qb2, qb3,
    zq_s, zq_r, cq_s, cq_r, a_s, a_r, zo_s, zo_r, po_s, po_r, co_s, co_r, t_s, t_r, c_s, c_r,
    g_s, g_r, kp_s, kp_r, qp_s, qp_r, kv_s, kv_r, ck_s, ck_r, zt_s, zt_r, ct_s, ct_r, ss_s, ss_r,
    n_s, n_r, s_s, s_r, zd_s, zd_r, cd_s, cd_r, px_s, px_r, z_s, z_r, at_s, at_r,
):
    r = lax.axis_index("row")
    c = lax.axis_index("col")
    z = c // 2
    k = lax.rem(c, 2)
    oc = other_core(c)
    mates = [(mate(r, m), c) for m in (1, 2, 3)]
    aheads = [(r, z_ahead(c, m)) for m in (1, 2, 3)]
    core = (r, oc)
    ready = greet(mates + [core] + aheads)
    mine = slice_rows(r)
    sent = []

    def send(src, dst, send_sem, recv_sem, target):
        copy = remote(src, dst, send_sem, recv_sem, target)
        copy.start()
        sent.append(copy)
        return copy

    joined = jnp.concatenate([wq_ref[...], wkv_ref[0], wkv_ref[1]], axis=0)
    wsrc[...] = jnp.transpose(joined).astype(half)
    blk[c] = wsrc[...]
    tokens = tok_ref[...].astype(full)
    sums[r] = jnp.broadcast_to(jnp.sum(tokens * tokens, axis=0, keepdims=True), (8, 512))
    gain2_src[...] = jnp.broadcast_to(gains_ref[1:2, :], (8, 288))
    ready()
    qz = [send(wsrc, blk.at[c], zq_s.at[m], zq_r.at[m], aheads[m]) for m in range(3)]
    q_core = [send(wsrc, blk.at[c], cq_s.at[3], cq_r.at[3], core)]
    sum_copies = [
        send(sums.at[r], sums.at[r], ss_s.at[m], ss_r.at[m], mates[m]) for m in range(3)
    ]
    tok_copies = [
        send(tok_ref.at[:, block_rows(mates[m][0])], tok_own.at[mine], t_s.at[m], t_r.at[m], mates[m])
        for m in range(3)
    ]
    gain_copies = [
        send(gain2_src, gain_parts.at[r], g_s.at[m], g_r.at[m], mates[m]) for m in range(3)
    ]
    for i in range(3):
        for t in range(3):
            src = wd_ref[...] if t == 2 else wgu_ref[t]
            w3[i, t] = src[:, 128 * i : 128 * i + 128].astype(half)
    tile_sends = []
    for m in range(3):
        b = mates[m][0]
        copy = remote(
            w3.at[tile_of(b, z)], tile.at[:, mine, :], a_s.at[m], a_r.at[m], mates[m]
        )
        tile_sends.append((has_tile(b, z, k), copy))

        @pl.when(has_tile(b, z, k))
        def _():
            copy.start()

    cotall_ref[mine, :] = cot_ref[...]
    cot_gather = Gather(lambda b, h: cotall_ref.at[slice_rows(b, h)], r, c, c_s, c_r)
    cot_gather.start()
    for j in range(3):
        osrc[:, 288 * j : 288 * j + 288] = wo_ref[48 * j : 48 * j + 48, :].astype(half)
    wo_all[r, z, k] = osrc[...]
    tok_own[mine, :] = tok_ref[:, block_rows(r)]
    gain_parts[r] = gain2_src[...]

    @pl.when(has_tile(r, z, k))
    def _():
        tile[:, mine, :] = w3[tile_of(r, z)]

    for copy in sum_copies:
        copy.wait_recv()
    scale_row = lax.rsqrt((sums[0] + sums[1] + sums[2] + sums[3]) / D + EPS)
    srow_ref[...] = scale_row
    gain1 = jnp.transpose(jnp.broadcast_to(gains_ref[0:1, :], (128, 288)))[:, 0:1]
    n1_ref[...] = (tokens * scale_row[0:1, :] * gain1).astype(half)
    cosine, sine = turn_tables(512 * k + TB * r)
    bias = mask_bias(starts_ref, z, 512 * k + TB * r)
    for m in range(3):
        src = lax.rem(c + 6 - 2 * m, 8)
        remote(wsrc, blk.at[src], zq_s.at[m], zq_r.at[m], core).wait_recv()
        q_core.append(send(blk.at[src], blk.at[src], cq_s.at[m], cq_r.at[m], core))
    oz = [send(osrc, wo_all.at[r, z, k], zo_s.at[m], zo_r.at[m], aheads[m]) for m in range(3)]
    gate_up = TileGather(
        tile.at[0:2],
        lambda slot: w_ref.at[:, :, tile_cols(slot)],
        r, c, zt_s, zt_r, ct_s, ct_r,
    )

    downs = TileGather(
        tile.at[2], lambda slot: wd.at[:, tile_cols(slot)], r, c, zd_s, zd_r, cd_s, cd_r
    )

    @pl.when(gate_up.has)
    def _():
        for m in range(3):
            src = slice_rows(mates[m][0])
            remote(w3.at[0], tile.at[:, src, :], a_s.at[m], a_r.at[m], mates[m]).wait_recv()
        gate_up.start()

    for m in range(3):
        src = lax.rem(oc + 6 - 2 * m, 8)
        remote(blk.at[src], blk.at[src], cq_s.at[m], cq_r.at[m], core).wait_recv()
    remote(wsrc, blk.at[oc], cq_s.at[3], cq_r.at[3], core).wait_recv()
    for i in range(8):
        wi_ref[:, 144 * i : 144 * i + 144] = blk[i, :, 0:144]
        wi_ref[:, 1152 + 48 * i : 1200 + 48 * i] = blk[i, :, 144:192]
        wi_ref[:, 1536 + 48 * i : 1584 + 48 * i] = blk[i, :, 192:240]
    kv_scatter = Scatter(kvb0, kvb1, kvb2, kvb3, r, c, kp_s, kp_r)
    q_scatter = Scatter(qb0, qb1, qb2, qb3, r, c, qp_s, qp_r)
    for m in (2, 0, 1):
        part = n1_ref[:, block_rows(mates[m][0])]
        kvb0[m] = product_left(part, wi_ref[:, 1152:]).astype(half)
        kv_scatter.start(((0,), (1,), (2, 3))[m])
    cot_gather.relay()
    for m in (2, 0, 1):
        part = n1_ref[:, block_rows(mates[m][0])]
        qb0[m] = product_left(part, wi_ref[:, :1152]).astype(half)
        q_scatter.start(((0,), (1,), (2, 3))[m])
    kv_scatter.relay()
    part = n1_ref[:, block_rows(r)]
    kv_own[...] = product_left(part, wi_ref[:, 1152:])
    q_own[...] = product_left(part, wi_ref[:, :1152])
    for m in range(3):
        src = slice_rows(mates[m][0])
        remote(
            tok_ref.at[:, block_rows(0)], tok_own.at[src], t_s.at[m], t_r.at[m], mates[m]
        ).wait_recv()
    hidden = jnp.transpose(tok_own[...].astype(full))
    hid[...] = hidden
    scale = lax.rsqrt(jnp.sum(hidden * hidden, axis=1, keepdims=True) / D + EPS)
    sown_ref[...] = jnp.broadcast_to(scale, (TB, 128))
    raw = kv_scatter.finish(kv_own).astype(half)
    my_block = block_rows(4 * k + r)
    kv_ref[my_block, 0:384] = turn(raw[:, 0:384].astype(full), cosine, sine).astype(half)
    kv_ref[my_block, 384:768] = raw[:, 384:768]
    kv_gather = Gather(lambda b, h: kv_ref.at[part_rows(4 * k + b, h)], r, c, kv_s, kv_r)
    kv_gather.start()

    def kv_core(j, b):
        rows = block_rows(4 * k + b)
        return send(kv_ref.at[rows], kv_ref.at[rows], ck_s.at[j], ck_r.at[j], core)

    kv_core(3, r)
    q_scatter.relay()
    for copy in oz:
        copy.wait_recv()
    wo_gather = Gather(
        lambda b, h: wo_all.at[b, :, k] if h is None else wo_all.at[b, 2 * h : 2 * h + 2, k],
        r, c, po_s, po_r,
    )
    wo_gather.start()
    kv_gather.relay()
    raw = q_scatter.finish(q_own).astype(half)
    queries = turn(raw.astype(full), cosine, sine).astype(half)
    q_ref[...] = queries
    queries = queries * jnp.bfloat16(0.125)
    for m in range(2):
        kv_core(m, mates[m][0])
    kv_gather.finish()
    kv_core(2, mates[2][0])
    for j in range(4):
        b = r if j == 3 else mates[j][0]
        rows = block_rows(4 * (1 - k) + b)
        remote(kv_ref.at[rows], kv_ref.at[rows], ck_s.at[j], ck_r.at[j], core).wait_recv()
    cot_gather.finish()
    def wo_swap(j, b):
        return send(wo_all.at[b, :, k], wo_all.at[b, :, k], co_s.at[j], co_r.at[j], core)

    for g in range(KV_HEADS):
        if g == 3:

            @pl.when(downs.has)
            def _():
                downs.start()

        if g == 4:
            wo_swap(3, r)
            wo_gather.relay()
            wo_swap(0, mates[0][0])
            wo_swap(1, mates[1][0])
        keys = kv_ref[:, 64 * g : 64 * g + 64]
        values = kv_ref[:, 384 + 64 * g : 448 + 64 * g]
        heads = jnp.concatenate(
            [queries[:, 64 * h : 64 * h + 64] for h in range(3 * g, 3 * g + 3)], axis=0
        )
        scores = product_right(heads, keys).reshape(3, TB, 1024) + bias[None]
        high = jnp.max(scores, axis=-1, keepdims=True)
        weights = jnp.exp(scores - high)
        total = jnp.sum(weights, axis=-1, keepdims=True)
        probs = (weights * (1.0 / total)).astype(half).reshape(3 * TB, 1024)
        lse_ref[:, g : g + 1] = (high + jnp.log(total)).reshape(3 * TB, 1)
        output = product(probs, values)
        for j in range(3):
            h = 3 * g + j
            out_ref[:, 64 * h : 64 * h + 64] = output[TB * j : TB * j + TB]
    attended = out_ref[...].astype(half)
    gate_up.relay()

    wo_gather.finish()
    wo_swap(2, mates[2][0])
    for j in range(4):
        b = r if j == 3 else mates[j][0]
        remote(
            wo_all.at[b, :, 1 - k], wo_all.at[b, :, 1 - k], co_s.at[j], co_r.at[j], core
        ).wait_recv()
    for b in range(4):
        for i in range(4):
            for kk in range(2):
                for j in range(3):
                    row = 144 * (2 * i + kk) + 48 * j
                    wof_ref[row : row + 48, 288 * b : 288 * b + 288] = wo_all[
                        b, i, kk, :, 288 * j : 288 * j + 288
                    ]
    middle = hid[...] + product(attended, wof_ref[...])
    mid_ref[...] = middle
    for copy in gain_copies:
        copy.wait_recv()
    gain = jnp.concatenate([gain_parts[i] for i in range(4)], axis=1)
    scale_two = lax.rsqrt(jnp.sum(middle * middle, axis=1, keepdims=True) / D + EPS)
    my_rows = block_rows(r)
    all_ref[my_rows, :] = (middle * scale_two * gain[0:1, :]).astype(half)
    gather = Gather(lambda b, h: all_ref.at[part_rows(b, h)], r, c, n_s, n_r)
    scatter = Scatter(b0, b1, b2, b3, r, c, s_s, s_r)
    gather.start()

    @pl.when(gate_up.has)
    def _():
        cols = tile_cols(3 * k + tile_place(r, k, z))
        w_ref[:, :, cols] = tile[0:2]
        wd[:, cols] = tile[2]

    att_all[my_rows, :] = attended
    gate_up.finish()

    def up_to(b):
        rows = block_rows(b)
        normed = all_ref[rows, :]
        for j in range(3):
            cs = slice(256 * j, 256 * j + 256)
            gate = product(normed, w_ref[0, :, cs])
            up = product(normed, w_ref[1, :, cs])
            sigma = 1.0 / (1.0 + jnp.exp(-gate))
            hidden = gate * sigma
            act[rows, cs] = (hidden * up).astype(half)
            swish[rows, cs] = hidden
            slope[rows, cs] = up * (sigma * (1.0 + gate * (1.0 - sigma)))

    up_to(r)
    gather.relay()
    up_to(mates[0][0])
    up_to(mates[1][0])
    downs.relay()
    gather.finish()
    att_gather = Gather(lambda b, h: att_all.at[part_rows(b, h)], r, c, at_s, at_r)
    att_gather.start()
    up_to(mates[2][0])

    def tile_grads(t, core_index):
        cols = pl.ds(pl.multiple_of(384 * core_index, 128), 384)
        if t == 2:
            return product(cotall_ref[...], act[:, cols])
        return product_left(all_ref[...], d_ref[t, :, cols])

    px_copies = {}

    def to_other_core(t):
        part = tile_grads(t, 1 - k)
        for j in range(3):
            px_out[t, j] = part[:, 128 * j : 128 * j + 128].astype(half)
        px_copies[t] = send(px_out.at[t], px_in.at[t], px_s.at[t], px_r.at[t], core)

    to_other_core(2)
    downs.finish()

    def back(b):
        rows = block_rows(b)
        cot = cotall_ref[:, rows]
        for j in range(3):
            cs = slice(256 * j, 256 * j + 256)
            grad = product_left(cot, wd[:, cs])
            d_ref[0, rows, cs] = (grad * slope[rows, cs]).astype(half)
            d_ref[1, rows, cs] = (grad * swish[rows, cs]).astype(half)
        return product_right(d_ref[0, rows, :], w_ref[0]) + product_right(
            d_ref[1, rows, :], w_ref[1]
        )

    for m in (2, 0, 1):
        b0[m] = back(mates[m][0]).astype(half)
        scatter.start(((0,), (1,), (2, 3))[m])
    part = tile_grads(2, k)
    px_copies[2].wait_recv()
    for j in range(3):
        value = part[:, 128 * j : 128 * j + 128] + px_in[2, j].astype(full)
        tempd[j] = value
        dwzd[j] = value.astype(half)
    z_sends = []
    for m in range(3):
        ahead = lax.rem(z + m + 1, 4)
        place = tile_place(r, k, ahead)
        copy = remote(dwzd.at[place], zin.at[m], z_s.at[m], z_r.at[m], aheads[m])
        flag = has_tile(r, ahead, k)
        z_sends.append((flag, copy))

        @pl.when(flag)
        def _():
            copy.start()

    own_grad[...] = back(r)
    scatter.relay()
    att_gather.relay()
    to_other_core(0)
    to_other_core(1)
    for i in range(2):
        rows = slice(256 * i, 256 * i + 256)
        down_ref[rows, :] = product_right(act[rows, :], wd[...]).astype(half)
    scale = scale_two
    cot = jnp.transpose(cotall_ref[:, my_rows].astype(full))
    hidden = mid_ref[...]
    grad = scatter.finish(own_grad)
    inner = jnp.sum(grad * gain[0:1, :] * hidden, axis=1, keepdims=True)
    gm = cot + grad * gain[0:1, :] * scale - hidden * (scale * scale * scale * inner / D)
    gm_ref[...] = gm.astype(half)
    gain_out[...] = jnp.broadcast_to(
        jnp.sum(grad * hidden * scale, axis=0, keepdims=True), gain_out.shape
    )
    for t in range(2):
        part = tile_grads(t, k)
        px_copies[t].wait_recv()
        for j in range(3):
            value = part[:, 128 * j : 128 * j + 128] + px_in[t, j].astype(full)
            dwz[t, j] = value.astype(half)
    att_gather.finish()

    @pl.when(downs.has)
    def _():
        value = tempd[tile_place(r, k, z)]
        for m in range(3):
            remote(dwzd.at[0], zin.at[m], z_s.at[m], z_r.at[m], aheads[m]).wait_recv()
            value = value + zin[m].astype(full)
        dwd_ref[...] = value

    for copy in sent:
        copy.wait_send()
    for part in (
        cot_gather, kv_gather, wo_gather, gate_up, kv_scatter, q_scatter, downs, gather, scatter,
        att_gather,
    ):
        part.sent()
    for flag, copy in tile_sends + z_sends:

        @pl.when(flag)
        def _():
            copy.wait_send()


def forward(*args):
    shape = jax.ShapeDtypeStruct
    v = pltpu.VMEM
    sems = []
    counts = (3, 4, 3, 3, 4, 4, 3, 4, 3, 6, 6, 4, 4, 3, 4, 3, 4, 6, 3, 4, 3, 3, 4)
    for count in counts:
        sems += [pltpu.SemaphoreType.DMA((count,))] * 2
    return pl.pallas_call(
        forward_kernel,
        out_shape=(
            shape((TB, D), full),
            shape((TB, D), half),
            shape((1024, 768), half),
            shape((3 * TB, 128), full),
            shape((TB, D), full),
            shape((D, D), half),
            shape((288, 1920), half),
            shape((288, 512), half),
            shape((8, 512), full),
            shape((TB, 128), full),
            shape((512, D), half),
            shape((TB, D), half),
            shape((512, D), half),
            shape((8, D), full),
            shape((2, 3, D, 128), half),
            shape((D, 128), full),
        ),
        in_specs=[VM] * 8 + [SM],
        out_specs=(VM,) * 16,
        scratch_shapes=[
            v((8, 288), full),
            v((D, 512), half),
            v((2, D, 768), half),
            v((512, D), half),
            v((2, 512, 768), half),
            v((D, 768), half),
            v((512, 768), half),
            v((512, 768), full),
            v((512, 768), full),
            v((3, 3, D, 128), half),
            v((3, 3, D, 128), half),
            v((3, D, 128), half),
            v((3, D, 128), half),
            v((3, D, 128), full),
            v((TB, D), full),
        ]
        + scatter_buffers(D)
        + [
            v((288, 240), half),
            v((48, 864), half),
            v((3, 3, 288, 128), half),
            v((8, 288, 240), half),
            v((3, D, 128), half),
            v((D, TB), half),
            v((4, 8, 512), full),
            v((4, 8, 288), full),
            v((TB, 768), full),
            v((TB, D), full),
            v((4, 4, 2, 48, 864), half),
            v((TB, D), full),
        ]
        + scatter_buffers(768)
        + scatter_buffers(D)
        + sems,
        compiler_params=pltpu.CompilerParams(
            collective_id=1, has_side_effects=True, vmem_limit_bytes=60 << 20
        ),
    )(*args)


def back_kernel(
    mid_ref, q_ref, kv_ref, lse_ref, out_ref, wof_ref, wi_ref, n1_ref, srow_ref, sown_ref,
    down_ref, gm_ref, att_all, gain2_ref, dwz, dwd_ref, tok_ref, gains_in, starts_ref,
    bo_ref, ig_ref, dw_ref, dq_ref, do_ref, gains_ref,
    gm_out, gm_nat, bo_out, zin, tile_out, dkv, dkv_co, dkv_ci, sdq, sdk, dqs, dwq, dwq_co, dwq_ci, dwq_z, dwq_in,
    dwk, dwk_co, dwk_ci, dwk_z, dwk_in,
    dwo, dwo_co, dwo_ci, dwo_z, dwo_in, g2_out, g2_in, gl, gl_ci, gl_z, gl_in, coef_all, dn_own,
    n0, n1, n2, n3, e0, e1, e2, e3,
    dn_s, dn_r, bo_s, bo_r, z_s, z_r, t_s, t_r, kc_s, kc_r, kp_s, kp_r, sd_s, sd_r, sk_s, sk_r,
    qc_s, qc_r, qz_s, qz_r, kk_s, kk_r, kz_s, kz_r, oc_s, oc_r, oz_s, oz_r, g2_s, g2_r, gc_s, gc_r,
    gz_s, gz_r, cf_s, cf_r, gm_s, gm_r,
):
    r = lax.axis_index("row")
    c = lax.axis_index("col")
    z = c // 2
    k = lax.rem(c, 2)
    mates = [(mate(r, m), c) for m in (1, 2, 3)]
    aheads = [(r, z_ahead(c, m)) for m in (1, 2, 3)]
    ahead_z = [lax.rem(z + m, 4) for m in (1, 2, 3)]
    core = (r, other_core(c))
    ready = greet(mates + [core] + aheads)
    mine = block_rows(r)
    sent = []

    def send(src, dst, send_sem, recv_sem, target):
        copy = remote(src, dst, send_sem, recv_sem, target)
        copy.start()
        sent.append(copy)
        return copy

    for i in range(4):
        g2_out[i] = gain2_ref[:, 288 * i : 288 * i + 288]
    turned = jnp.transpose(gm_ref[...].astype(full)).astype(half)
    for i in range(4):
        gm_out[i] = turned[288 * i : 288 * i + 288]
    gm_nat[:, mine] = gm_out[r]
    for m in range(3):
        n0[m] = down_ref[block_rows(mates[m][0]), :]
    mine_has = has_tile(r, z, k)
    my_place = tile_place(r, k, z)
    ready()
    z_flags = []
    for t in range(2):
        for m in range(3):
            place = tile_place(r, k, ahead_z[m])
            copy = remote(
                dwz.at[t, place], zin.at[m, t], z_s.at[2 * m + t], z_r.at[2 * m + t], aheads[m]
            )
            flag = has_tile(r, ahead_z[m], k)
            z_flags.append((flag, copy))

            @pl.when(flag)
            def _():
                copy.start()

    gm_copies = [
        send(gm_out.at[mates[m][0]], gm_nat.at[:, mine], gm_s.at[m], gm_r.at[m], mates[m])
        for m in range(3)
    ]

    def tile_copy(t, m):
        return remote(
            tile_out.at[mates[m][0], t],
            dw_ref.at[tile_of(r, z), t],
            t_s.at[3 * t + m],
            t_r.at[3 * t + m],
            mates[m],
        )

    def tile_back(t):
        @pl.when(mine_has)
        def _():
            value = dwd_ref[...] if t == 2 else dwz[t, my_place].astype(full)
            if t < 2:
                for m in range(3):
                    remote(
                        dwz.at[t, 0], zin.at[m, t], z_s.at[2 * m + t], z_r.at[2 * m + t], aheads[m]
                    ).wait_recv()
                    value = value + zin[m, t].astype(full)
            for b in range(4):
                tile_out[b, t] = value[288 * b : 288 * b + 288].astype(half)
            for m in range(3):
                tile_copy(t, m).start()
            dw_ref[tile_of(r, z), t] = tile_out[r, t]

    tile_back(2)
    downs = Scatter(n0, n1, n2, n3, r, c, dn_s, dn_r)
    downs.start()
    g2_copies = [
        send(g2_out.at[mates[m][0]], g2_in.at[m], g2_s.at[m], g2_r.at[m], mates[m])
        for m in range(3)
    ]
    ga = product_right(gm_ref[...], wof_ref[...]).astype(half)
    gaf = ga.astype(full)
    queries = q_ref[...] * jnp.bfloat16(0.125)
    cosine, sine = turn_tables(512 * k + TB * r)
    sine = -sine
    bias = mask_bias(starts_ref, z, 512 * k + TB * r)
    for g in range(KV_HEADS):
        if g == 4:
            downs.relay()
        keys = kv_ref[:, 64 * g : 64 * g + 64]
        values = kv_ref[:, 384 + 64 * g : 448 + 64 * g]
        heads = range(3 * g, 3 * g + 3)
        qh = jnp.concatenate([queries[:, 64 * h : 64 * h + 64] for h in heads], axis=0)
        gh = jnp.concatenate([ga[:, 64 * h : 64 * h + 64] for h in heads], axis=0)
        delta = jnp.concatenate(
            [
                jnp.sum(
                    gaf[:, 64 * h : 64 * h + 64] * out_ref[:, 64 * h : 64 * h + 64],
                    axis=1,
                    keepdims=True,
                )
                for h in heads
            ],
            axis=0,
        )
        scores = product_right(qh, keys).reshape(3, TB, 1024) + bias[None]
        probs = jnp.exp(scores.reshape(3 * TB, 1024) - lse_ref[:, g : g + 1])
        grad_probs = product_right(gh, values)
        grad_scores = (probs * (grad_probs - delta)).astype(half)
        grad_q = product(grad_scores, keys) * 0.125
        for j in range(3):
            h = 3 * g + j
            dqs[:, 64 * h : 64 * h + 64] = grad_q[TB * j : TB * j + TB]
        dkv[:, 64 * g : 64 * g + 64] = product_left(grad_scores, qh)
        dkv[:, 384 + 64 * g : 448 + 64 * g] = product_left(probs.astype(half), gh)
    other_rows = pl.ds(pl.multiple_of(512 * (1 - k), 512), 512)
    dkv_co[...] = dkv[other_rows, :].astype(half)
    kc = send(dkv_co, dkv_ci, kc_s.at[0], kc_r.at[0], core)
    grad_q = dqs[...]
    inner = jnp.sum(grad_q * q_ref[...].astype(full), axis=1, keepdims=True)
    sdq[mine, :] = turn(grad_q, cosine, sine).astype(half)
    q_gather = Gather(lambda b, h: sdq.at[part_rows(b, h)], r, c, sd_s, sd_r)
    q_gather.start()
    kc.wait_recv()
    pairs = Scatter(e0, e1, e2, e3, r, c, kp_s, kp_r)
    for m in (2, 0, 1):
        b = mates[m][0]
        e0[m] = (dkv[block_rows(4 * k + b), :] + dkv_ci[block_rows(b), :].astype(full)).astype(half)
        pairs.start(((0,), (1,), (2, 3))[m])
    my_block = block_rows(4 * k + r)
    dkv[my_block, :] = dkv[my_block, :] + dkv_ci[mine, :].astype(full)
    for m in range(3):
        cols = block_rows(mates[m][0])
        remote(gm_out.at[0], gm_nat.at[:, cols], gm_s.at[m], gm_r.at[m], mates[m]).wait_recv()
    grad_wo = lax.dot_general(
        att_all[...], gm_nat[...], (((0,), (1,)), ((), ())), preferred_element_type=full
    )
    for i in range(8):
        dwo[i] = grad_wo[144 * i : 144 * i + 144]

    def wide(value):
        n = value.shape[0] // 3
        return jnp.concatenate([value[n * j : n * j + n] for j in range(3)], axis=1)

    def tall(value):
        n = value.shape[1] // 3
        return jnp.concatenate([value[:, n * j : n * j + n] for j in range(3)], axis=0)

    for i in range(4):
        dwo_co[i] = dwo[2 * i + 1 - k].astype(half)
    oc_copy = send(dwo_co, dwo_ci, oc_s.at[0], oc_r.at[0], core)
    pairs.relay()
    q_gather.relay()
    oc_copy.wait_recv()
    for i in range(4):
        value = dwo[2 * i + k] + dwo_ci[i].astype(full)
        dwo_z[i] = wide(value).astype(half)
        dwo[2 * i + k] = value
    oz_copies = [
        send(dwo_z.at[ahead_z[m]], dwo_in.at[m], oz_s.at[m], oz_r.at[m], aheads[m])
        for m in range(3)
    ]
    grad_kv = pairs.finish(dkv[my_block, :])
    sdk[mine, 0:384] = turn(grad_kv[:, 0:384], cosine, sine).astype(half)
    sdk[mine, 384:768] = grad_kv[:, 384:768].astype(half)
    k_gather = Gather(lambda b, h: sdk.at[part_rows(b, h)], r, c, sk_s, sk_r)
    k_gather.start()
    inner = inner + jnp.sum(grad_kv * kv_ref[my_block, :].astype(full), axis=1, keepdims=True)
    scale = sown_ref[...]
    coef = jnp.transpose(inner * (scale * scale) / D)
    coef_all[r] = coef[0:8]
    coef_copies = [
        send(coef_all.at[r], coef_all.at[r], cf_s.at[m], cf_r.at[m], mates[m]) for m in range(3)
    ]
    q_gather.finish()
    grad_wi = product(n1_ref[...], sdq[...])
    for i in range(8):
        dwq[i] = grad_wi[:, 144 * i : 144 * i + 144]
    for i in range(4):
        dwq_co[i] = dwq[2 * i + 1 - k].astype(half)
    qc_copy = send(dwq_co, dwq_ci, qc_s.at[0], qc_r.at[0], core)
    k_gather.relay()
    tile_back(0)
    qc_copy.wait_recv()
    for i in range(4):
        value = dwq[2 * i + k] + dwq_ci[i].astype(full)
        dwq_z[i] = wide(value).astype(half)
        dwq[2 * i + k] = value
    qz_copies = [
        send(dwq_z.at[ahead_z[m]], dwq_in.at[m], qz_s.at[m], qz_r.at[m], aheads[m])
        for m in range(3)
    ]
    back = product_right(wi_ref[:, 0:1152], sdq[...])
    k_gather.finish()
    grad_wi = product(n1_ref[...], sdk[...])
    for i in range(8):
        dwk[i, :, 0:48] = grad_wi[:, 48 * i : 48 * i + 48]
        dwk[i, :, 48:96] = grad_wi[:, 384 + 48 * i : 432 + 48 * i]
    for i in range(4):
        dwk_co[i] = dwk[2 * i + 1 - k].astype(half)
    kk_copy = send(dwk_co, dwk_ci, kk_s.at[0], kk_r.at[0], core)
    back = (back + product_right(wi_ref[:, 1152:1920], sdk[...])) * srow_ref[0:1, :]
    kk_copy.wait_recv()
    for i in range(4):
        value = dwk[2 * i + k] + dwk_ci[i].astype(full)
        dwk_z[i] = value.astype(half)
        dwk[2 * i + k] = value
    kz_copies = [
        send(dwk_z.at[ahead_z[m]], dwk_in.at[m], kz_s.at[m], kz_r.at[m], aheads[m])
        for m in range(3)
    ]
    tile_back(1)
    dn_own[...] = mid_ref[...] + down_ref[mine, :].astype(full)
    result = downs.finish(dn_own)
    result = jnp.transpose(result).astype(half)
    for i in range(4):
        bo_out[i] = result[288 * i : 288 * i + 288]
    bo_ref[:, mine] = bo_out[r]
    bo_copies = [
        send(bo_out.at[mates[m][0]], bo_ref.at[:, mine], bo_s.at[m], bo_r.at[m], mates[m])
        for m in range(3)
    ]
    for m in range(3):
        b = mates[m][0]
        remote(coef_all.at[b], coef_all.at[b], cf_s.at[m], cf_r.at[m], mates[m]).wait_recv()
    coef = jnp.concatenate([coef_all[i] for i in range(4)], axis=1)[0:1, :]
    tokens = tok_ref[...].astype(full)
    gain1 = jnp.transpose(jnp.broadcast_to(gains_in[0:1, :], (128, 288)))[:, 0:1]
    ig_ref[...] = (gm_nat[...].astype(full) + back * gain1 - tokens * coef).astype(half)
    for copy in g2_copies:
        copy.wait_recv()
    column = jnp.sum(back * tokens, axis=1, keepdims=True)
    gl[0] = jnp.transpose(jnp.broadcast_to(column, (288, 128)))[0:8]
    gl[1] = g2_out[r] + g2_in[0] + g2_in[1] + g2_in[2]
    gc_copy = send(gl, gl_ci, gc_s.at[0], gc_r.at[0], core)
    gc_copy.wait_recv()
    gl_z[...] = gl[...] + gl_ci[...]
    gz_copies = [send(gl_z, gl_in.at[m], gz_s.at[m], gz_r.at[m], aheads[m]) for m in range(3)]
    for m in range(3):
        oz_copies[m].wait_recv()
    total = dwo[2 * z + k]
    for m in range(3):
        total = total + tall(dwo_in[m].astype(full))
    do_ref[...] = total
    for m in range(3):
        cols = block_rows(mates[m][0])
        remote(bo_out.at[0], bo_ref.at[:, cols], bo_s.at[m], bo_r.at[m], mates[m]).wait_recv()
    for m in range(3):
        b = mates[m][0]

        @pl.when(has_tile(b, z, k))
        def _():
            for t in range(3):
                remote(
                    tile_out.at[0, t],
                    dw_ref.at[tile_of(b, z), t],
                    t_s.at[3 * t + m],
                    t_r.at[3 * t + m],
                    mates[m],
                ).wait_recv()

    total = dwq[2 * z + k]
    for m in range(3):
        qz_copies[m].wait_recv()
        total = total + tall(dwq_in[m].astype(full))
    dq_ref[:, 0:144] = total
    total = dwk[2 * z + k]
    for m in range(3):
        kz_copies[m].wait_recv()
        total = total + dwk_in[m].astype(full)
    dq_ref[:, 144:240] = total
    total = gl_z[...]
    for m in range(3):
        gz_copies[m].wait_recv()
        total = total + gl_in[m]
    gains_ref[...] = total
    for copy in sent:
        copy.wait_send()
    for part in (downs, pairs, q_gather, k_gather):
        part.sent()
    for flag, copy in z_flags:

        @pl.when(flag)
        def _():
            copy.wait_send()

    @pl.when(mine_has)
    def _():
        for t in range(3):
            for m in range(3):
                tile_copy(t, m).wait_send()


def back(*args):
    shape = jax.ShapeDtypeStruct
    sems = []
    for count in (6, 3, 6, 9, 1, 6, 4, 4, 1, 3, 1, 3, 1, 3, 3, 1, 3, 3, 3):
        sems += [pltpu.SemaphoreType.DMA((count,))] * 2
    v = pltpu.VMEM
    return pl.pallas_call(
        back_kernel,
        out_shape=(
            shape((288, 512), half),
            shape((288, 512), half),
            shape((3, 3, 288, 128), half),
            shape((288, 240), full),
            shape((144, 288), full),
            shape((2, 8, 288), full),
        ),
        in_specs=[VM] * 18 + [SM],
        out_specs=(VM,) * 6,
        scratch_shapes=[
            v((4, 288, TB), half),
            v((288, 512), half),
            v((4, 288, TB), half),
            v((3, 2, D, 128), half),
            v((4, 3, 288, 128), half),
            v((1024, 768), full),
            v((512, 768), half),
            v((512, 768), half),
            v((512, D), half),
            v((512, 768), half),
            v((TB, D), full),
            v((8, 288, 144), full),
            v((4, 288, 144), half),
            v((4, 288, 144), half),
            v((4, 96, 432), half),
            v((3, 96, 432), half),
            v((8, 288, 96), full),
            v((4, 288, 96), half),
            v((4, 288, 96), half),
            v((4, 288, 96), half),
            v((3, 288, 96), half),
            v((8, 144, 288), full),
            v((4, 144, 288), half),
            v((4, 144, 288), half),
            v((4, 48, 864), half),
            v((3, 48, 864), half),
            v((4, 8, 288), full),
            v((3, 8, 288), full),
            v((2, 8, 288), full),
            v((2, 8, 288), full),
            v((2, 8, 288), full),
            v((3, 2, 8, 288), full),
            v((4, 8, TB), full),
            v((TB, D), full),
        ]
        + scatter_buffers(D)
        + scatter_buffers(768)
        + sems,
        compiler_params=pltpu.CompilerParams(
            collective_id=3, has_side_effects=True, vmem_limit_bytes=60 << 20
        ),
    )(*args)


def update_kernel(
    bo_in, ig_in, dw_ref, dq_ref, do_ref, dg_ref,
    g_w, g_m, g_v, q_w, q_m, q_v, kv_w, kv_m, kv_v, o_w, o_m, o_v, gu_w, gu_m, gu_v, d_w, d_m, d_v,
    bo_out, ig_out, g_nm, g_nv, g_nw, q_nm, q_nv, q_nw, q_low, kv_nm, kv_nv, kv_nw, kv_low,
    o_nm, o_nv, o_nw, o_low, gu_nm, gu_nv, gu_nw, gu_low, d_nm, d_nv, d_nw, d_low,
):
    fix = 1.0 - BETA**STEP

    def step(at, grad, rate, decay, ins, outs):
        weight = ins[0][at]
        first = BETA * ins[1][at] + (1.0 - BETA) * grad
        second = BETA * ins[2][at] + (1.0 - BETA) * grad * grad
        change = first / fix / (jnp.sqrt(second / fix) + TINY)
        weight = weight - rate * (change + decay * weight)
        outs[0][at] = first
        outs[1][at] = second
        outs[2][at] = weight
        if len(outs) == 4:
            outs[3][at] = weight.astype(half)

    bo_out[...] = bo_in[...]
    ig_out[...] = ig_in[...]
    rate = D**-0.5
    every = (slice(None), slice(None))
    step(every, jnp.concatenate([dg_ref[0, 0:1], dg_ref[1, 0:1]], axis=0), 0.25, 0.0,
         (g_w, g_m, g_v), (g_nm, g_nv, g_nw))
    for i in range(3):
        cols = (slice(None), slice(128 * i, 128 * i + 128))
        for t in range(2):
            step((t,) + cols, dw_ref[i, t].astype(full), rate, DECAY,
                 (gu_w, gu_m, gu_v), (gu_nm, gu_nv, gu_nw, gu_low))
        step(cols, dw_ref[i, 2].astype(full), FF**-0.5, DECAY,
             (d_w, d_m, d_v), (d_nm, d_nv, d_nw, d_low))
    step(every, do_ref[...], rate, DECAY, (o_w, o_m, o_v), (o_nm, o_nv, o_nw, o_low))
    turned = jnp.transpose(dq_ref[...])
    step(every, turned[0:144], rate, DECAY, (q_w, q_m, q_v), (q_nm, q_nv, q_nw, q_low))
    for t in range(2):
        step((t, slice(None), slice(None)), turned[144 + 48 * t : 192 + 48 * t], rate, DECAY,
             (kv_w, kv_m, kv_v), (kv_nm, kv_nv, kv_nw, kv_low))


def update(*args):
    shape = jax.ShapeDtypeStruct
    outs = [shape((288, 512), half)] * 2 + [shape((2, 288), full)] * 3
    for dims in ((144, 288), (2, 48, 288), (144, 288), (2, 288, 384), (288, 384)):
        outs += [shape(dims, full)] * 3 + [shape(dims, half)]
    return pl.pallas_call(
        update_kernel,
        out_shape=tuple(outs),
        in_specs=[VM] * 24,
        out_specs=(VM,) * len(outs),
        compiler_params=pltpu.CompilerParams(vmem_limit_bytes=48 << 20),
    )(*args)


def swap(value):
    return jnp.swapaxes(value, -1, -2)


def local_fast(
    tokens,
    cotangent,
    starts,
    gains,
    gains_m,
    gains_v,
    w_query,
    w_query_m,
    w_query_v,
    w_keyval,
    w_keyval_m,
    w_keyval_v,
    w_output,
    w_output_m,
    w_output_v,
    w_gateup,
    w_gateup_m,
    w_gateup_v,
    w_down,
    w_down_m,
    w_down_v,
):
    tok = swap(tokens)
    kept = forward(
        tok, swap(cotangent), swap(w_query), swap(w_keyval), w_output, w_gateup, swap(w_down),
        gains, starts
    )
    grads = back(*kept, tok, gains, starts)
    outs = update(
        *grads, gains, gains_m, gains_v, swap(w_query), swap(w_query_m), swap(w_query_v),
        swap(w_keyval), swap(w_keyval_m), swap(w_keyval_v), w_output, w_output_m, w_output_v,
        w_gateup, w_gateup_m, w_gateup_v, swap(w_down), swap(w_down_m), swap(w_down_v)
    )
    turned = (0, 1, 5, 6, 7, 8, 9, 10, 11, 12, 21, 22, 23, 24)
    return tuple(swap(value) if i in turned else value for i, value in enumerate(outs))


def local(tokens, *others):
    fits = lax.axis_size("row") == 4 and lax.axis_size("col") == 8 and tokens.shape == (512, 288)
    plan = local_fast if fits else local_general
    return plan(tokens, *others)


def solution(mesh):
    return jax.shard_map(
        local,
        mesh=mesh,
        in_specs=(
            P("col", "row"),
            P("col", "row"),
            P(),
            P(None, "row"),
            P(None, "row"),
            P(None, "row"),
            P("row", "col"),
            P("row", "col"),
            P("row", "col"),
            P(None, "row", "col"),
            P(None, "row", "col"),
            P(None, "row", "col"),
            P("col", "row"),
            P("col", "row"),
            P("col", "row"),
            P(None, "row", "col"),
            P(None, "row", "col"),
            P(None, "row", "col"),
            P("col", "row"),
            P("col", "row"),
            P("col", "row"),
        ),
        out_specs=(
            P("col", "row"),
            P("col", "row"),
            P(None, "row"),
            P(None, "row"),
            P(None, "row"),
            P("row", "col"),
            P("row", "col"),
            P("row", "col"),
            P("row", "col"),
            P(None, "row", "col"),
            P(None, "row", "col"),
            P(None, "row", "col"),
            P(None, "row", "col"),
            P("col", "row"),
            P("col", "row"),
            P("col", "row"),
            P("col", "row"),
            P(None, "row", "col"),
            P(None, "row", "col"),
            P(None, "row", "col"),
            P(None, "row", "col"),
            P("col", "row"),
            P("col", "row"),
            P("col", "row"),
            P("col", "row"),
        ),
        check_vma=False,
    )
```

```python
import jax
import jax.numpy as jnp
from jax import lax
from jax.experimental import pallas as pl
from jax.experimental.pallas import tpu as pltpu
from jax.sharding import PartitionSpec as P

D = 1152
HEADS = 18
KV_HEADS = 6
HD = 64
FF = 3072
TD = 128
PIECE = 256
PIECES = 4
STEP = 7


EPS = 1e-05
BETA = 0.5
TINY = 1e-08
DECAY = 0.1
MASKED = -1e30


def to_half(value):
    return value.astype(jnp.bfloat16)


def product(left, right):
    return jnp.dot(left, right, preferred_element_type=jnp.float32)


def product_left(left, right):
    return lax.dot_general(
        left, right, (((0,), (0,)), ((), ())), preferred_element_type=jnp.float32
    )


def product_right(left, right):
    return lax.dot_general(
        left, right, (((1,), (1,)), ((), ())), preferred_element_type=jnp.float32
    )


def col_collect(value):
    return lax.all_gather(value, "col", axis=0, tiled=True)


def row_collect(value):
    return lax.all_gather(value, "row", axis=0, tiled=True)


def row_reduce(value):
    return lax.psum_scatter(value, "row", scatter_dimension=0, tiled=True)


def col_reduce(value):
    return lax.psum_scatter(value, "col", scatter_dimension=0, tiled=True)


def row_total(value):
    return lax.psum(value, "row")


def to_heads(value):
    return lax.all_to_all(value, "col", split_axis=0, concat_axis=1, tiled=True)


def to_rows(value):
    return lax.all_to_all(value, "col", split_axis=1, concat_axis=0, tiled=True)


def norm_forward(hidden, gain):
    total = row_total(jnp.sum(hidden * hidden, axis=1))
    scale = lax.rsqrt(total / D + EPS)
    return (scale, to_half(hidden * scale[:, None] * gain[None, :]))


def norm_backward(hidden, gain, scale, grad):
    inner = row_total(jnp.sum(grad * gain[None, :] * hidden, axis=1))
    back = (
        grad * gain[None, :] * scale[:, None]
        - hidden * (scale * scale * scale * inner / D)[:, None]
    )
    gain_grad = jnp.sum(grad * hidden * scale[:, None], axis=0)
    return (back, gain_grad)


def rotary(places):
    half = HD // 2
    freq = 10000.0 ** (-2.0 * jnp.arange(half, dtype=jnp.float32) / HD)
    angle = places[:, None] * freq[None, :]
    return (jnp.cos(angle), jnp.sin(angle))


def rotate(heads, cosine, sine):
    half = HD // 2
    first = heads[..., :half]
    second = heads[..., half:]
    cosine = cosine[:, None, :]
    sine = sine[:, None, :]
    return jnp.concatenate(
        [first * cosine - second * sine, second * cosine + first * sine], axis=-1
    )


def rotate_back(heads, cosine, sine):
    half = HD // 2
    first = heads[..., :half]
    second = heads[..., half:]
    cosine = cosine[:, None, :]
    sine = sine[:, None, :]
    return jnp.concatenate(
        [first * cosine + second * sine, second * cosine - first * sine], axis=-1
    )


def piece_ids(pieces, places):
    inside = (places[:, None] >= pieces[None, :]) & (places[:, None] < pieces[None, :] + PIECE)
    number = jnp.arange(1, PIECES + 1, dtype=jnp.int32)
    return jnp.sum(jnp.where(inside, number[None, :], 0), axis=1) - 1


def block_scores(queries, keys, places, ids, pieces, start):
    key_places = start + jnp.arange(keys.shape[0], dtype=jnp.int32)
    key_ids = piece_ids(pieces, key_places)
    raw = jnp.einsum("tkgd,skd->kgts", queries, keys, preferred_element_type=jnp.float32) * HD ** (
        -0.5
    )
    allowed = (key_places[None, :] <= places[:, None]) | (key_ids[None, :] == ids[:, None]) & (
        ids[:, None] >= 0
    )
    allowed = allowed[None, None]
    return (jnp.where(allowed, raw, MASKED), allowed)


def split_blocks(keyvals, width):
    count = keyvals.shape[0] // width
    blocks = keyvals.reshape(count, width, 2, KV_HEADS, HD)
    firsts = jnp.arange(count, dtype=jnp.int32) * width
    return (blocks, firsts)


def attend(queries, keyvals, places, ids, pieces, width):
    blocks, firsts = split_blocks(keyvals, width)
    shape = (KV_HEADS, queries.shape[2], queries.shape[0])

    def measure(carry, item):
        high, total = carry
        scores, allowed = block_scores(queries, item[0][:, 0], places, ids, pieces, item[1])
        new_high = jnp.maximum(high, jnp.max(scores, axis=-1))
        weights = jnp.where(allowed, jnp.exp(scores - new_high[..., None]), 0.0)
        return ((new_high, total * jnp.exp(high - new_high) + jnp.sum(weights, axis=-1)), None)

    start_state = (jnp.full(shape, MASKED, jnp.float32), jnp.zeros(shape, jnp.float32))
    (high, total), unused = lax.scan(measure, start_state, (blocks, firsts))
    logsum = high + jnp.log(total)

    def accumulate(acc, item):
        scores, allowed = block_scores(queries, item[0][:, 0], places, ids, pieces, item[1])
        probs = to_half(jnp.where(allowed, jnp.exp(scores - logsum[..., None]), 0.0))
        return (
            acc
            + jnp.einsum(
                "kgts,skd->tkgd", probs, item[0][:, 1], preferred_element_type=jnp.float32
            ),
            None,
        )

    output, unused = lax.scan(accumulate, jnp.zeros(queries.shape, jnp.float32), (blocks, firsts))
    return (output, logsum)


def attend_back(queries, keyvals, places, ids, pieces, width, logsum, grad_out, output):
    blocks, firsts = split_blocks(keyvals, width)
    delta = jnp.einsum("tkgd,tkgd->kgt", grad_out.astype(jnp.float32), output)
    factor = HD ** (-0.5)

    def sweep(acc, item):
        keys = item[0][:, 0]
        values = item[0][:, 1]
        scores, allowed = block_scores(queries, keys, places, ids, pieces, item[1])
        probs = jnp.where(allowed, jnp.exp(scores - logsum[..., None]), 0.0)
        grad_probs = jnp.einsum(
            "tkgd,skd->kgts", grad_out, values, preferred_element_type=jnp.float32
        )
        grad_scores = to_half(probs * (grad_probs - delta[..., None]))
        acc = (
            acc
            + jnp.einsum("kgts,skd->tkgd", grad_scores, keys, preferred_element_type=jnp.float32)
            * factor
        )
        grad_keys = (
            jnp.einsum("kgts,tkgd->skd", grad_scores, queries, preferred_element_type=jnp.float32)
            * factor
        )
        grad_values = jnp.einsum(
            "kgts,tkgd->skd", to_half(probs), grad_out, preferred_element_type=jnp.float32
        )
        joined = jnp.concatenate(
            [grad_keys.reshape(width, -1), grad_values.reshape(width, -1)], axis=1
        )
        return (acc, joined)

    grad_queries, grad_blocks = lax.scan(
        sweep, jnp.zeros(queries.shape, jnp.float32), (blocks, firsts)
    )
    return (grad_queries, grad_blocks.reshape(keyvals.shape[0], -1))


def adamw(weight, first, second, grad, rate, decay):
    first_new = BETA * first + (1.0 - BETA) * grad
    second_new = BETA * second + (1.0 - BETA) * grad * grad
    fix = 1.0 - BETA**STEP
    update = first_new / fix / (jnp.sqrt(second_new / fix) + TINY)
    weight_new = weight - rate * (update + decay * weight)
    return (first_new, second_new, weight_new)


def grid_plan(tokens, cotangent, starts, gains, w_query, w_keyval, w_output, w_gateup, w_down):
    columns = lax.axis_size("col")
    column = lax.axis_index("col")
    seq_len = TD * columns
    width = min(1024, seq_len)
    group = HEADS // KV_HEADS
    query_width = w_query.shape[1]
    key_width = w_keyval.shape[2]
    feed_width = w_gateup.shape[2]
    pieces = lax.dynamic_index_in_dim(starts, lax.axis_index("row"), 0, keepdims=False)
    hidden = tokens.astype(jnp.float32)
    inner_weights = to_half(jnp.concatenate([w_query, w_keyval[0], w_keyval[1]], axis=1))
    feed_weights = to_half(jnp.concatenate([w_gateup[0], w_gateup[1]], axis=1))
    out_weights = to_half(w_output)
    down_weights = to_half(w_down)
    scale_one, normed_one = norm_forward(hidden, gains[0])
    gathered_one = col_collect(normed_one)
    mixed = to_half(row_reduce(product(gathered_one, inner_weights)))
    spread = to_heads(mixed[:, None, :])
    query_raw = spread[:, :, :query_width].reshape(TD, HEADS, HD)
    key_raw = spread[:, :, query_width : query_width + key_width].reshape(TD, KV_HEADS, HD)
    value_heads = spread[:, :, query_width + key_width :].reshape(TD, KV_HEADS * HD)
    places = column * TD + jnp.arange(TD, dtype=jnp.int32)
    cosine, sine = rotary(places.astype(jnp.float32))
    queries = to_half(rotate(query_raw.astype(jnp.float32), cosine, sine)).reshape(
        TD, KV_HEADS, group, HD
    )
    keys = to_half(rotate(key_raw.astype(jnp.float32), cosine, sine))
    keyvals_local = jnp.concatenate([keys.reshape(TD, KV_HEADS * HD), value_heads], axis=1)
    keyvals = lax.all_gather(keyvals_local, "col", axis=0, tiled=True)
    ids = piece_ids(pieces, places)
    output, logsum = attend(queries, keyvals, places, ids, pieces, width)
    attended = to_half(output)
    attended_rows = to_rows(attended.reshape(TD, columns, query_width))[:, 0, :]
    gathered_att = row_collect(attended_rows)
    branch = col_reduce(product(gathered_att, out_weights))
    middle = hidden + branch
    scale_two, normed_two = norm_forward(middle, gains[1])
    gathered_two = col_collect(normed_two)
    feed = row_reduce(product(gathered_two, feed_weights))
    gate = feed[:, :feed_width]
    upward = feed[:, feed_width:]
    sigma = jax.nn.sigmoid(gate)
    swish = gate * sigma
    activated = to_half(swish * upward)
    gathered_act = row_collect(activated)
    result = middle + col_reduce(product(gathered_act, down_weights))
    block_out = to_half(result)
    both = lax.all_gather(jnp.stack([normed_one, normed_two]), "col", axis=1, tiled=True)
    back_one = both[0]
    back_two = both[1]
    grad_rows = col_collect(cotangent)
    grad_down = product_left(gathered_act, grad_rows)
    grad_act = row_reduce(product_right(grad_rows, down_weights))
    slope = sigma * (1.0 + gate * (1.0 - sigma))
    grad_feed = to_half(jnp.concatenate([grad_act * upward * slope, grad_act * swish], axis=1))
    gathered_feed = row_collect(grad_feed)
    grad_both = product_left(back_two, gathered_feed)
    grad_gateup = jnp.stack([grad_both[:, :feed_width], grad_both[:, feed_width:]])
    grad_normed_two = col_reduce(product_right(gathered_feed, feed_weights))
    norm_two_back, gain_two = norm_backward(middle, gains[1], scale_two, grad_normed_two)
    grad_middle = cotangent.astype(jnp.float32) + norm_two_back
    gathered_mid = col_collect(to_half(grad_middle))
    grad_output = product_left(gathered_att, gathered_mid)
    grad_att = to_half(row_reduce(product_right(gathered_mid, out_weights)))
    grad_heads = to_heads(grad_att[:, None, :]).reshape(TD, KV_HEADS, group, HD)
    keyvals_back = lax.all_gather(keyvals_local, "col", axis=0, tiled=True)
    grad_queries, grad_keyvals = attend_back(
        queries, keyvals_back, places, ids, pieces, width, logsum, grad_heads, output
    )
    local_keyvals = lax.psum_scatter(grad_keyvals, "col", scatter_dimension=0, tiled=True)
    kv_split = KV_HEADS * HD
    grad_query_raw = rotate_back(grad_queries.reshape(TD, HEADS, HD), cosine, sine)
    grad_key_raw = rotate_back(local_keyvals[:, :kv_split].reshape(TD, KV_HEADS, HD), cosine, sine)
    grad_value = local_keyvals[:, kv_split:]
    joined = jnp.concatenate(
        [
            to_half(grad_query_raw).reshape(TD, columns, query_width),
            to_half(grad_key_raw).reshape(TD, columns, key_width),
            to_half(grad_value).reshape(TD, columns, key_width),
        ],
        axis=2,
    )
    grad_mixed = to_rows(joined)[:, 0, :]
    gathered_mixed = row_collect(grad_mixed)
    grad_inner = product_left(back_one, gathered_mixed)
    grad_query = grad_inner[:, :query_width]
    grad_keyval = jnp.stack(
        [
            grad_inner[:, query_width : query_width + key_width],
            grad_inner[:, query_width + key_width :],
        ]
    )
    grad_normed_one = col_reduce(product_right(gathered_mixed, inner_weights))
    norm_one_back, gain_one = norm_backward(hidden, gains[0], scale_one, grad_normed_one)
    input_grad = to_half(grad_middle + norm_one_back)
    gain_grads = lax.psum(jnp.stack([gain_one, gain_two]), "col")
    return (
        block_out,
        input_grad,
        gain_grads,
        grad_query,
        grad_keyval,
        grad_output,
        grad_gateup,
        grad_down,
    )


def local_general(
    tokens,
    cotangent,
    starts,
    gains,
    gains_m,
    gains_v,
    w_query,
    w_query_m,
    w_query_v,
    w_keyval,
    w_keyval_m,
    w_keyval_v,
    w_output,
    w_output_m,
    w_output_v,
    w_gateup,
    w_gateup_m,
    w_gateup_v,
    w_down,
    w_down_m,
    w_down_v,
):
    results = grid_plan(
        tokens, cotangent, starts, gains, w_query, w_keyval, w_output, w_gateup, w_down
    )
    (
        block_out,
        input_grad,
        gain_grads,
        grad_query,
        grad_keyval,
        grad_output,
        grad_gateup,
        grad_down,
    ) = results
    rate_in = D ** (-0.5)
    rate_down = FF ** (-0.5)
    gain_m, gain_v, gain_w = adamw(gains, gains_m, gains_v, gain_grads, 0.25, 0.0)
    query_m, query_v, query_w = adamw(w_query, w_query_m, w_query_v, grad_query, rate_in, DECAY)
    keyval_m, keyval_v, keyval_w = adamw(
        w_keyval, w_keyval_m, w_keyval_v, grad_keyval, rate_in, DECAY
    )
    output_m, output_v, output_w = adamw(
        w_output, w_output_m, w_output_v, grad_output, rate_in, DECAY
    )
    gateup_m, gateup_v, gateup_w = adamw(
        w_gateup, w_gateup_m, w_gateup_v, grad_gateup, rate_in, DECAY
    )
    down_m, down_v, down_w = adamw(w_down, w_down_m, w_down_v, grad_down, rate_down, DECAY)
    return (
        block_out,
        input_grad,
        gain_m,
        gain_v,
        gain_w,
        query_m,
        query_v,
        query_w,
        to_half(query_w),
        keyval_m,
        keyval_v,
        keyval_w,
        to_half(keyval_w),
        output_m,
        output_v,
        output_w,
        to_half(output_w),
        gateup_m,
        gateup_v,
        gateup_w,
        to_half(gateup_w),
        down_m,
        down_v,
        down_w,
        to_half(down_w),
    )


TB = 128
LOG_BASE = 9.210340371976184
MESH = pl.DeviceIdType.MESH
half = jnp.bfloat16
full = jnp.float32
VM = pl.BlockSpec(memory_space=pltpu.VMEM)
SM = pl.BlockSpec(memory_space=pltpu.SMEM)


def mate(r, m):
    x = lax.rem(lax.rem(r, 2) + lax.rem(m, 2), 2)
    y = lax.rem(r // 2 + m // 2, 2)
    return 2 * y + x


def other_core(c):
    return c + 1 - 2 * lax.rem(c, 2)


def z_ahead(c, m):
    return lax.rem(c + 2 * m, 8)


def block_rows(b):
    return pl.ds(pl.multiple_of(b * TB, TB), TB)


def part_rows(b, h):
    if h is None:
        return block_rows(b)
    return pl.ds(pl.multiple_of(b * TB + 64 * h, 64), 64)


def slice_rows(b, h=None):
    if h is None:
        return pl.ds(pl.multiple_of(b * 288, 32), 288)
    return pl.ds(pl.multiple_of(b * 288 + 144 * h, 16), 144)


def greet(targets):
    barrier = pltpu.get_barrier_semaphore()
    for target in targets:
        pl.semaphore_signal(barrier, inc=1, device_id=target, device_id_type=MESH)
    return lambda: pl.semaphore_wait(barrier, len(targets))


def remote(src, dst, send, recv, target):
    return pltpu.make_async_remote_copy(
        src_ref=src, dst_ref=dst, send_sem=send, recv_sem=recv, device_id=target, device_id_type=MESH
    )


class Gather:
    def __init__(self, view, r, c, send, recv):
        x, y, far = mate(r, 1), mate(r, 2), mate(r, 3)
        self.first = [
            remote(view(r, None), view(r, None), send.at[0], recv.at[0], (x, c)),
            remote(view(r, None), view(r, None), send.at[1], recv.at[1], (y, c)),
        ]
        self.onward = [
            remote(view(x, 0), view(x, 0), send.at[2], recv.at[2], (y, c)),
            remote(view(y, 1), view(y, 1), send.at[3], recv.at[3], (x, c)),
        ]
        self.arrive = [
            remote(view(x, None), view(x, None), send.at[0], recv.at[0], (x, c)),
            remote(view(y, None), view(y, None), send.at[1], recv.at[1], (y, c)),
            remote(view(far, 0), view(far, 0), send.at[2], recv.at[2], (y, c)),
            remote(view(far, 1), view(far, 1), send.at[3], recv.at[3], (x, c)),
        ]

    def start(self):
        for copy in self.first:
            copy.start()

    def relay(self):
        for i in range(2):
            self.arrive[i].wait_recv()
            self.onward[i].start()

    def finish(self):
        self.arrive[2].wait_recv()
        self.arrive[3].wait_recv()

    def sent(self):
        for copy in self.first + self.onward:
            copy.wait_send()


class Scatter:
    def __init__(self, out, near, mid, last, r, c, send, recv):
        x, y = (mate(r, 1), c), (mate(r, 2), c)
        up, low = pl.ds(0, 64), pl.ds(64, 64)
        self.out, self.near, self.mid, self.last = out, near, mid, last
        self.first = [
            remote(out.at[0, up], near.at[0, 0], send.at[0], recv.at[0], x),
            remote(out.at[1, low], near.at[1, 0], send.at[1], recv.at[1], y),
            remote(out.at[2, up], near.at[0, 1], send.at[2], recv.at[2], x),
            remote(out.at[2, low], near.at[1, 1], send.at[3], recv.at[3], y),
        ]
        self.second = [
            remote(mid.at[0], last.at[0], send.at[4], recv.at[4], y),
            remote(mid.at[1], last.at[1], send.at[5], recv.at[5], x),
        ]

    def start(self, which=(2, 3, 0, 1)):
        for i in which:
            self.first[i].start()

    def relay(self):
        self.first[2].wait_recv()
        self.mid[0] = (self.out[1, 0:64].astype(full) + self.near[0, 1].astype(full)).astype(half)
        self.second[0].start()
        self.first[3].wait_recv()
        self.mid[1] = (self.out[0, 64:128].astype(full) + self.near[1, 1].astype(full)).astype(half)
        self.second[1].start()

    def finish(self, own):
        for copy in self.first[:2] + self.second:
            copy.wait_recv()
        upper = own[0:64] + self.near[0, 0].astype(full) + self.last[0].astype(full)
        lower = own[64:128] + self.near[1, 0].astype(full) + self.last[1].astype(full)
        return jnp.concatenate([upper, lower], axis=0)

    def sent(self):
        for copy in self.first + self.second:
            copy.wait_send()


def scatter_buffers(width):
    v = pltpu.VMEM
    return [
        v((3, TB, width), half),
        v((2, 2, 64, width), half),
        v((2, 64, width), half),
        v((2, 64, width), half),
    ]


def idle_plane(r, k):
    x = lax.rem(r, 2)
    return 2 * (1 - lax.rem(x + k, 2)) + 1 - r // 2


def tile_place(r, k, z):
    return jnp.minimum(lax.rem(z - idle_plane(r, k) + 3, 4), 2)


def has_tile(b, z, k):
    return (b // 2 == lax.rem(z, 2)) | (lax.rem(b, 2) == lax.rem(k + z // 2, 2))


def tile_of(b, z):
    return jnp.where(b // 2 == lax.rem(z, 2), lax.rem(b, 2), 2)


def tile_cols(place):
    return pl.ds(pl.multiple_of(place * 128, 128), 128)


class TileGather:
    def __init__(self, mine, view, r, c, zs, zr, cs, cr):
        self.r, self.z, self.k = r, c // 2, lax.rem(c, 2)
        core = (r, other_core(c))
        z, k = self.z, self.k
        self.has = has_tile(r, z, k)
        here = view(3 * k + tile_place(r, k, z))
        self.out = [remote(mine, here, zs.at[m], zr.at[m], (r, z_ahead(c, m + 1))) for m in range(3)]
        self.out.append(remote(mine, here, cs.at[3], cr.at[3], core))
        self.relays = []
        for m in range(3):
            src = lax.rem(z + 3 - m, 4)
            slot = view(3 * k + tile_place(r, k, src))
            self.relays.append(
                (
                    has_tile(r, src, k),
                    remote(slot, slot, zs.at[m], zr.at[m], core),
                    remote(slot, slot, cs.at[m], cr.at[m], core),
                )
            )
        self.others = []
        for m in range(4):
            src = z if m == 3 else lax.rem(z + 3 - m, 4)
            slot = view(3 * (1 - k) + tile_place(r, 1 - k, src))
            self.others.append(
                (has_tile(r, src, 1 - k), remote(slot, slot, cs.at[m], cr.at[m], core))
            )

    def start(self):
        for copy in self.out:
            copy.start()

    def relay(self):
        for flag, come, go in self.relays:

            @pl.when(flag)
            def _():
                come.wait_recv()
                go.start()

    def finish(self):
        for flag, come in self.others:

            @pl.when(flag)
            def _():
                come.wait_recv()

    def sent(self):
        @pl.when(self.has)
        def _():
            for copy in self.out:
                copy.wait_send()

        for flag, come, go in self.relays:

            @pl.when(flag)
            def _():
                go.wait_send()


class PlaneSum:
    def __init__(self, part, over, joint, last, r, c, send, recv, has=None):
        z, k = c // 2, lax.rem(c, 2)
        side = z // 2
        beside = 2 * side + 1 - lax.rem(z, 2)
        self.far = (2 - side, 3 - 3 * side)
        self.part, self.over, self.joint, self.last = part, over, joint, last
        has = has or (lambda plane: plane >= 0)
        at_end = (z == 0) | (z == 3)
        self.owns = has(z)
        to = lambda plane: (r, 2 * plane + k)
        self.direct = (
            has(beside), remote(part(beside), last.at[0], send.at[0], recv.at[0], to(beside))
        )
        self.first = []
        self.second = []
        for i in range(2):
            plane = self.far[i]
            self.first.append(
                (
                    at_end & has(plane),
                    remote(part(plane), over.at[i], send.at[1 + i], recv.at[1 + i], to(beside)),
                )
            )
            self.second.append(
                (
                    (1 - at_end.astype(jnp.int32) > 0) & has(plane),
                    remote(joint.at[i], last.at[1], send.at[3 + i], recv.at[3], to(plane)),
                )
            )

    def start(self):
        for flag, copy in (self.first[1], self.first[0], self.direct):

            @pl.when(flag)
            def _():
                copy.start()

    def relay(self):
        for i in (1, 0):
            flag, copy = self.second[i]

            @pl.when(flag)
            def _():
                self.first[i][1].wait_recv()
                value = self.part(self.far[i])[...].astype(full) + self.over[i].astype(full)
                self.joint[i] = value.astype(half)
                copy.start()

    def arrive(self):
        self.direct[1].wait_recv()
        self.second[0][1].wait_recv()
        return self.last[0].astype(full) + self.last[1].astype(full)

    def sent(self):
        for flag, copy in [self.direct] + self.first + self.second:

            @pl.when(flag)
            def _():
                copy.wait_send()


def turn(value, cosine, sine):
    lane = lax.broadcasted_iota(jnp.int32, (value.shape[0], 128), 1)
    first = lax.rem(lane, 64) < 32
    parts = []
    for i in range(value.shape[1] // 128):
        part = value[:, 128 * i : 128 * i + 128]
        swapped = jnp.where(first, pltpu.roll(part, 96, 1), pltpu.roll(part, 32, 1))
        parts.append(part * cosine + swapped * sine)
    return jnp.concatenate(parts, axis=1)


def turn_tables(base):
    lane = lax.broadcasted_iota(jnp.int32, (TB, 128), 1)
    place = (lax.broadcasted_iota(jnp.int32, (TB, 128), 0) + base).astype(full)
    power = lax.rem(lane, 32).astype(full) * (-2.0 / HD)
    angle = place * jnp.exp(power * LOG_BASE)
    sine = jnp.sin(angle)
    return jnp.cos(angle), jnp.where(lax.rem(lane, 64) < 32, -sine, sine)


def mask_bias(starts_ref, seq, base):
    keys = lax.broadcasted_iota(jnp.int32, (1, 1024), 1)
    rows = lax.broadcasted_iota(jnp.int32, (TB, 1), 0) + base
    key_id = jnp.zeros((1, 1024), jnp.int32)
    row_id = jnp.zeros((TB, 1), jnp.int32)
    for j in range(PIECES):
        first = starts_ref[seq, j]
        key_id = key_id + jnp.where((keys >= first) & (keys < first + PIECE), j + 1, 0)
        row_id = row_id + jnp.where((rows >= first) & (rows < first + PIECE), j + 1, 0)
    row_id = jnp.where(row_id == 0, -1, row_id)
    allowed = (keys <= rows) | (key_id == row_id)
    return jnp.where(allowed, 0.0, MASKED)


def forward_kernel(
    tok_ref, cot_ref, wq_ref, wkv_ref, wo_ref, wgu_ref, wd_ref, gains_ref, starts_ref,
    mid_hbm, q_hbm, kv_hbm, lse_hbm, out_hbm, wof_hbm, wi_hbm, n1_hbm, srow_hbm, sown_hbm,
    down_hbm, gm_hbm, att_hbm, gain_hbm, dwz_hbm, dwd_hbm,
    mid_ref, q_ref, kv_ref, lse_ref, out_ref, wof_ref, wi_ref, n1_ref, srow_ref, sown_ref,
    down_ref, gm_ref, att_all, gain_out, dwz, dwd_ref,
    gain2_src, cotall_ref, w_ref, all_ref, d_ref, wd, act, slope, swish, px_out, px_in, dwzd, zin,
    tempd, own_grad, b0, b1, b2, b3,
    wsrc, osrc, w3, blk, tile, tok_own, sums, gain_parts, kv_own, q_own, wo_all,
    hid, kvb0, kvb1, kvb2, kvb3, qb0, qb1, qb2, qb3,
    zq_s, zq_r, cq_s, cq_r, a_s, a_r, zo_s, zo_r, po_s, po_r, co_s, co_r, t_s, t_r, c_s, c_r,
    g_s, g_r, kp_s, kp_r, qp_s, qp_r, kv_s, kv_r, ck_s, ck_r, zt_s, zt_r, ct_s, ct_r, ss_s, ss_r,
    n_s, n_r, s_s, s_r, zd_s, zd_r, cd_s, cd_r, px_s, px_r, z_s, z_r, at_s, at_r, out_s,
):
    r = lax.axis_index("row")
    c = lax.axis_index("col")
    z = c // 2
    k = lax.rem(c, 2)
    oc = other_core(c)
    mates = [(mate(r, m), c) for m in (1, 2, 3)]
    aheads = [(r, z_ahead(c, m)) for m in (1, 2, 3)]
    core = (r, oc)
    ready = greet(mates + [core] + aheads)
    mine = slice_rows(r)
    sent = []

    def send(src, dst, send_sem, recv_sem, target):
        copy = remote(src, dst, send_sem, recv_sem, target)
        copy.start()
        sent.append(copy)
        return copy

    stores = []

    def store(src, dst):
        copy = pltpu.make_async_copy(src, dst, out_s.at[len(stores)])
        copy.start()
        stores.append(copy)

    joined = jnp.concatenate([wq_ref[...], wkv_ref[0], wkv_ref[1]], axis=0)
    wsrc[...] = jnp.transpose(joined).astype(half)
    blk[c] = wsrc[...]
    tokens = tok_ref[...].astype(full)
    sums[r] = jnp.broadcast_to(jnp.sum(tokens * tokens, axis=0, keepdims=True), (8, 512))
    gain2_src[...] = jnp.broadcast_to(gains_ref[1:2, :], (8, 288))
    ready()
    qz = [send(wsrc, blk.at[c], zq_s.at[m], zq_r.at[m], aheads[m]) for m in range(3)]
    q_core = [send(wsrc, blk.at[c], cq_s.at[3], cq_r.at[3], core)]
    sum_copies = [
        send(sums.at[r], sums.at[r], ss_s.at[m], ss_r.at[m], mates[m]) for m in range(3)
    ]
    tok_copies = [
        send(tok_ref.at[:, block_rows(mates[m][0])], tok_own.at[mine], t_s.at[m], t_r.at[m], mates[m])
        for m in range(3)
    ]
    gain_copies = [
        send(gain2_src, gain_parts.at[r], g_s.at[m], g_r.at[m], mates[m]) for m in range(3)
    ]
    for i in range(3):
        for t in range(3):
            src = wd_ref[...] if t == 2 else wgu_ref[t]
            w3[i, t] = src[:, 128 * i : 128 * i + 128].astype(half)
    tile_sends = []
    for m in range(3):
        b = mates[m][0]
        copy = remote(
            w3.at[tile_of(b, z)], tile.at[:, mine, :], a_s.at[m], a_r.at[m], mates[m]
        )
        tile_sends.append((has_tile(b, z, k), copy))

        @pl.when(has_tile(b, z, k))
        def _():
            copy.start()

    cotall_ref[mine, :] = cot_ref[...]
    cot_gather = Gather(lambda b, h: cotall_ref.at[slice_rows(b, h)], r, c, c_s, c_r)
    cot_gather.start()
    for j in range(3):
        osrc[:, 288 * j : 288 * j + 288] = wo_ref[48 * j : 48 * j + 48, :].astype(half)
    wo_all[r, z, k] = osrc[...]
    tok_own[mine, :] = tok_ref[:, block_rows(r)]
    gain_parts[r] = gain2_src[...]

    @pl.when(has_tile(r, z, k))
    def _():
        tile[:, mine, :] = w3[tile_of(r, z)]

    for copy in sum_copies:
        copy.wait_recv()
    scale_row = lax.rsqrt((sums[0] + sums[1] + sums[2] + sums[3]) / D + EPS)
    srow_ref[...] = scale_row
    gain1 = jnp.transpose(jnp.broadcast_to(gains_ref[0:1, :], (128, 288)))[:, 0:1]
    n1_ref[...] = (tokens * scale_row[0:1, :] * gain1).astype(half)
    cosine, sine = turn_tables(512 * k + TB * r)
    bias = mask_bias(starts_ref, z, 512 * k + TB * r)
    for m in range(3):
        src = lax.rem(c + 6 - 2 * m, 8)
        remote(wsrc, blk.at[src], zq_s.at[m], zq_r.at[m], core).wait_recv()
        q_core.append(send(blk.at[src], blk.at[src], cq_s.at[m], cq_r.at[m], core))
    oz = [send(osrc, wo_all.at[r, z, k], zo_s.at[m], zo_r.at[m], aheads[m]) for m in range(3)]
    gate_up = TileGather(
        tile.at[0:2],
        lambda slot: w_ref.at[:, :, tile_cols(slot)],
        r, c, zt_s, zt_r, ct_s, ct_r,
    )

    downs = TileGather(
        tile.at[2], lambda slot: wd.at[:, tile_cols(slot)], r, c, zd_s, zd_r, cd_s, cd_r
    )

    @pl.when(gate_up.has)
    def _():
        for m in range(3):
            src = slice_rows(mates[m][0])
            remote(w3.at[0], tile.at[:, src, :], a_s.at[m], a_r.at[m], mates[m]).wait_recv()
        gate_up.start()

    for m in range(3):
        src = lax.rem(oc + 6 - 2 * m, 8)
        remote(blk.at[src], blk.at[src], cq_s.at[m], cq_r.at[m], core).wait_recv()
    remote(wsrc, blk.at[oc], cq_s.at[3], cq_r.at[3], core).wait_recv()
    for i in range(8):
        wi_ref[:, 144 * i : 144 * i + 144] = blk[i, :, 0:144]
        wi_ref[:, 1152 + 48 * i : 1200 + 48 * i] = blk[i, :, 144:192]
        wi_ref[:, 1536 + 48 * i : 1584 + 48 * i] = blk[i, :, 192:240]
    store(wi_ref, wi_hbm)
    store(n1_ref, n1_hbm)
    store(srow_ref, srow_hbm)
    kv_scatter = Scatter(kvb0, kvb1, kvb2, kvb3, r, c, kp_s, kp_r)
    q_scatter = Scatter(qb0, qb1, qb2, qb3, r, c, qp_s, qp_r)
    for m in (2, 0, 1):
        part = n1_ref[:, block_rows(mates[m][0])]
        kvb0[m] = product_left(part, wi_ref[:, 1152:]).astype(half)
        kv_scatter.start(((0,), (1,), (2, 3))[m])
    cot_gather.relay()
    for m in (2, 0, 1):
        part = n1_ref[:, block_rows(mates[m][0])]
        qb0[m] = product_left(part, wi_ref[:, :1152]).astype(half)
    kv_scatter.relay()
    q_scatter.start()
    part = n1_ref[:, block_rows(r)]
    kv_own[...] = product_left(part, wi_ref[:, 1152:])
    q_own[...] = product_left(part, wi_ref[:, :1152])
    for m in range(3):
        src = slice_rows(mates[m][0])
        remote(
            tok_ref.at[:, block_rows(0)], tok_own.at[src], t_s.at[m], t_r.at[m], mates[m]
        ).wait_recv()
    hidden = jnp.transpose(tok_own[...].astype(full))
    hid[...] = hidden
    scale = lax.rsqrt(jnp.sum(hidden * hidden, axis=1, keepdims=True) / D + EPS)
    sown_ref[...] = jnp.broadcast_to(scale, (TB, 128))
    raw = kv_scatter.finish(kv_own).astype(half)
    my_block = block_rows(4 * k + r)
    kv_ref[my_block, 0:384] = turn(raw[:, 0:384].astype(full), cosine, sine).astype(half)
    kv_ref[my_block, 384:768] = raw[:, 384:768]
    kv_gather = Gather(lambda b, h: kv_ref.at[part_rows(4 * k + b, h)], r, c, kv_s, kv_r)
    kv_gather.start()

    def kv_core(j, b):
        rows = block_rows(4 * k + b)
        return send(kv_ref.at[rows], kv_ref.at[rows], ck_s.at[j], ck_r.at[j], core)

    kv_core(3, r)
    q_scatter.relay()
    for copy in oz:
        copy.wait_recv()
    wo_gather = Gather(
        lambda b, h: wo_all.at[b, :, k] if h is None else wo_all.at[b, 2 * h : 2 * h + 2, k],
        r, c, po_s, po_r,
    )
    kv_gather.relay()
    wo_gather.start()
    raw = q_scatter.finish(q_own).astype(half)
    queries = turn(raw.astype(full), cosine, sine).astype(half)
    q_ref[...] = queries
    queries = queries * jnp.bfloat16(0.125)
    for m in range(2):
        kv_core(m, mates[m][0])
    kv_gather.finish()
    kv_core(2, mates[2][0])
    for j in range(4):
        b = r if j == 3 else mates[j][0]
        rows = block_rows(4 * (1 - k) + b)
        remote(kv_ref.at[rows], kv_ref.at[rows], ck_s.at[j], ck_r.at[j], core).wait_recv()
    cot_gather.finish()
    def wo_swap(j, b):
        return send(wo_all.at[b, :, k], wo_all.at[b, :, k], co_s.at[j], co_r.at[j], core)

    store(kv_ref, kv_hbm)
    store(q_ref, q_hbm)
    store(sown_ref, sown_hbm)
    for g in range(KV_HEADS):
        if g == 3:

            @pl.when(downs.has)
            def _():
                downs.start()

        if g == 4:
            wo_swap(3, r)
            wo_gather.relay()
            wo_swap(0, mates[0][0])
            wo_swap(1, mates[1][0])
        keys = kv_ref[:, 64 * g : 64 * g + 64]
        values = kv_ref[:, 384 + 64 * g : 448 + 64 * g]
        heads = jnp.concatenate(
            [queries[:, 64 * h : 64 * h + 64] for h in range(3 * g, 3 * g + 3)], axis=0
        )
        scores = product_right(heads, keys).reshape(3, TB, 1024) + bias[None]
        high = jnp.max(scores, axis=-1, keepdims=True)
        weights = jnp.exp(scores - high)
        total = jnp.sum(weights, axis=-1, keepdims=True)
        probs = (weights * (1.0 / total)).astype(half).reshape(3 * TB, 1024)
        lse_ref[:, g : g + 1] = (high + jnp.log(total)).reshape(3 * TB, 1)
        output = product(probs, values)
        for j in range(3):
            h = 3 * g + j
            out_ref[:, 64 * h : 64 * h + 64] = output[TB * j : TB * j + TB]
    attended = out_ref[...].astype(half)
    store(lse_ref, lse_hbm)
    store(out_ref, out_hbm)
    gate_up.relay()

    wo_gather.finish()
    wo_swap(2, mates[2][0])
    for j in range(4):
        b = r if j == 3 else mates[j][0]
        remote(
            wo_all.at[b, :, 1 - k], wo_all.at[b, :, 1 - k], co_s.at[j], co_r.at[j], core
        ).wait_recv()
    for b in range(4):
        for i in range(4):
            for kk in range(2):
                for j in range(3):
                    row = 144 * (2 * i + kk) + 48 * j
                    wof_ref[row : row + 48, 288 * b : 288 * b + 288] = wo_all[
                        b, i, kk, :, 288 * j : 288 * j + 288
                    ]
    middle = hid[...] + product(attended, wof_ref[...])
    mid_ref[...] = middle
    store(wof_ref, wof_hbm)
    store(mid_ref, mid_hbm)
    for copy in gain_copies:
        copy.wait_recv()
    gain = jnp.concatenate([gain_parts[i] for i in range(4)], axis=1)
    scale_two = lax.rsqrt(jnp.sum(middle * middle, axis=1, keepdims=True) / D + EPS)
    my_rows = block_rows(r)
    all_ref[my_rows, :] = (middle * scale_two * gain[0:1, :]).astype(half)
    gather = Gather(lambda b, h: all_ref.at[part_rows(b, h)], r, c, n_s, n_r)
    scatter = Scatter(b0, b1, b2, b3, r, c, s_s, s_r)
    gather.start()

    @pl.when(gate_up.has)
    def _():
        cols = tile_cols(3 * k + tile_place(r, k, z))
        w_ref[:, :, cols] = tile[0:2]
        wd[:, cols] = tile[2]

    att_all[my_rows, :] = attended
    gate_up.finish()

    def up_to(b):
        rows = block_rows(b)
        normed = all_ref[rows, :]
        for j in range(3):
            cs = slice(256 * j, 256 * j + 256)
            gate = product(normed, w_ref[0, :, cs])
            up = product(normed, w_ref[1, :, cs])
            sigma = 1.0 / (1.0 + jnp.exp(-gate))
            hidden = gate * sigma
            act[rows, cs] = (hidden * up).astype(half)
            swish[rows, cs] = hidden
            slope[rows, cs] = up * (sigma * (1.0 + gate * (1.0 - sigma)))

    up_to(r)
    gather.relay()
    up_to(mates[0][0])
    up_to(mates[1][0])
    downs.relay()
    gather.finish()
    att_gather = Gather(lambda b, h: att_all.at[part_rows(b, h)], r, c, at_s, at_r)
    att_gather.start()
    up_to(mates[2][0])

    def tile_grads(t, core_index):
        cols = pl.ds(pl.multiple_of(384 * core_index, 128), 384)
        if t == 2:
            return product(cotall_ref[...], act[:, cols])
        return product_left(all_ref[...], d_ref[t, :, cols])

    px_copies = {}

    def to_other_core(t):
        part = tile_grads(t, 1 - k)
        for j in range(3):
            px_out[t, j] = part[:, 128 * j : 128 * j + 128].astype(half)
        px_copies[t] = send(px_out.at[t], px_in.at[t], px_s.at[t], px_r.at[t], core)

    downs.finish()

    def back(b):
        rows = block_rows(b)
        cot = cotall_ref[:, rows]
        for j in range(3):
            cs = slice(256 * j, 256 * j + 256)
            grad = product_left(cot, wd[:, cs])
            d_ref[0, rows, cs] = (grad * slope[rows, cs]).astype(half)
            d_ref[1, rows, cs] = (grad * swish[rows, cs]).astype(half)
        return product_right(d_ref[0, rows, :], w_ref[0]) + product_right(
            d_ref[1, rows, :], w_ref[1]
        )

    for m in (2, 0, 1):
        b0[m] = back(mates[m][0]).astype(half)
        scatter.start(((0,), (1,), (2, 3))[m])
        if m == 2:
            to_other_core(2)
    part = tile_grads(2, k)
    px_copies[2].wait_recv()
    for j in range(3):
        value = part[:, 128 * j : 128 * j + 128] + px_in[2, j].astype(full)
        tempd[j] = value
        dwzd[j] = value.astype(half)
    z_sends = []
    for m in range(3):
        ahead = lax.rem(z + m + 1, 4)
        place = tile_place(r, k, ahead)
        copy = remote(dwzd.at[place], zin.at[m], z_s.at[m], z_r.at[m], aheads[m])
        flag = has_tile(r, ahead, k)
        z_sends.append((flag, copy))

        @pl.when(flag)
        def _():
            copy.start()

    own_grad[...] = back(r)
    scatter.relay()
    att_gather.relay()
    to_other_core(0)
    to_other_core(1)
    for i in range(2):
        rows = slice(256 * i, 256 * i + 256)
        down_ref[rows, :] = product_right(act[rows, :], wd[...]).astype(half)
    store(down_ref, down_hbm)
    scale = scale_two
    cot = jnp.transpose(cotall_ref[:, my_rows].astype(full))
    hidden = mid_ref[...]
    grad = scatter.finish(own_grad)
    inner = jnp.sum(grad * gain[0:1, :] * hidden, axis=1, keepdims=True)
    gm = cot + grad * gain[0:1, :] * scale - hidden * (scale * scale * scale * inner / D)
    gm_ref[...] = gm.astype(half)
    store(gm_ref, gm_hbm)
    gain_out[...] = jnp.broadcast_to(
        jnp.sum(grad * hidden * scale, axis=0, keepdims=True), gain_out.shape
    )
    for t in range(2):
        part = tile_grads(t, k)
        px_copies[t].wait_recv()
        for j in range(3):
            value = part[:, 128 * j : 128 * j + 128] + px_in[t, j].astype(full)
            dwz[t, j] = value.astype(half)
    store(gain_out, gain_hbm)
    store(dwz, dwz_hbm)
    att_gather.finish()
    store(att_all, att_hbm)

    dwd_ref[...] = jnp.zeros_like(dwd_ref)

    @pl.when(downs.has)
    def _():
        value = tempd[tile_place(r, k, z)]
        for m in range(3):
            remote(dwzd.at[0], zin.at[m], z_s.at[m], z_r.at[m], aheads[m]).wait_recv()
            value = value + zin[m].astype(full)
        dwd_ref[...] = value

    store(dwd_ref, dwd_hbm)
    for copy in sent:
        copy.wait_send()
    for part in (
        cot_gather, kv_gather, wo_gather, gate_up, kv_scatter, q_scatter, downs, gather, scatter,
        att_gather,
    ):
        part.sent()
    for copy in stores:
        copy.wait()
    for flag, copy in tile_sends + z_sends:

        @pl.when(flag)
        def _():
            copy.wait_send()


def forward(*args):
    shape = jax.ShapeDtypeStruct
    v = pltpu.VMEM
    sems = []
    counts = (3, 4, 3, 3, 4, 4, 3, 4, 3, 6, 6, 4, 4, 3, 4, 3, 4, 6, 3, 4, 3, 3, 4)
    for count in counts:
        sems += [pltpu.SemaphoreType.DMA((count,))] * 2
    return pl.pallas_call(
        forward_kernel,
        out_shape=(
            shape((TB, D), full),
            shape((TB, D), half),
            shape((1024, 768), half),
            shape((3 * TB, 128), full),
            shape((TB, D), full),
            shape((D, D), half),
            shape((288, 1920), half),
            shape((288, 512), half),
            shape((8, 512), full),
            shape((TB, 128), full),
            shape((512, D), half),
            shape((TB, D), half),
            shape((512, D), half),
            shape((8, D), full),
            shape((2, 3, D, 128), half),
            shape((D, 128), full),
        ),
        in_specs=[VM] * 8 + [SM],
        out_specs=(pl.BlockSpec(memory_space=pl.ANY),) * 16,
        scratch_shapes=[
            v((TB, D), full),
            v((TB, D), half),
            v((1024, 768), half),
            v((3 * TB, 128), full),
            v((TB, D), full),
            v((D, D), half),
            v((288, 1920), half),
            v((288, 512), half),
            v((8, 512), full),
            v((TB, 128), full),
            v((512, D), half),
            v((TB, D), half),
            v((512, D), half),
            v((8, D), full),
            v((2, 3, D, 128), half),
            v((D, 128), full),
            v((8, 288), full),
            v((D, 512), half),
            v((2, D, 768), half),
            v((512, D), half),
            v((2, 512, 768), half),
            v((D, 768), half),
            v((512, 768), half),
            v((512, 768), full),
            v((512, 768), full),
            v((3, 3, D, 128), half),
            v((3, 3, D, 128), half),
            v((3, D, 128), half),
            v((3, D, 128), half),
            v((3, D, 128), full),
            v((TB, D), full),
        ]
        + scatter_buffers(D)
        + [
            v((288, 240), half),
            v((48, 864), half),
            v((3, 3, 288, 128), half),
            v((8, 288, 240), half),
            v((3, D, 128), half),
            v((D, TB), half),
            v((4, 8, 512), full),
            v((4, 8, 288), full),
            v((TB, 768), full),
            v((TB, D), full),
            v((4, 4, 2, 48, 864), half),
            v((TB, D), full),
        ]
        + scatter_buffers(768)
        + scatter_buffers(D)
        + sems
        + [pltpu.SemaphoreType.DMA((16,))],
        compiler_params=pltpu.CompilerParams(
            collective_id=1, has_side_effects=True, vmem_limit_bytes=60 << 20
        ),
    )(*args)


def back_kernel(
    mid_in, q_in, kv_in, lse_in, out_in, wof_in, wi_in, n1_in, srow_in, sown_in, down_in, gm_in,
    att_in, gain2_in, dwz_in, dwd_in, tok_ref, gains_in, starts_ref,
    bo_ref, ig_ref, dw_ref, dq_ref, do_ref, gains_ref,
    mid_ref, q_ref, kv_ref, lse_ref, out_ref, wof_ref, wi_ref, n1_ref, srow_ref, sown_ref,
    down_ref, gm_ref, att_all, gain2_ref, dwz, dwd_ref,
    gm_out, gm_nat, bo_out, z_over, z_joint, z_last, tile_out, dkv, dkv_co, dkv_ci, sdq, sdk, dqs, dwq, dwq_co, dwq_ci, dwq_z,
    dwq_over, dwq_joint, dwq_in,
    dwk, dwk_co, dwk_ci, dwk_z, dwk_in,
    dwo, dwo_co, dwo_ci, dwo_z, dwo_over, dwo_joint, dwo_in, g2_out, g2_in, gl, gl_ci, gl_z, gl_in, coef_all, dn_own,
    n0, n1, n2, n3, e0, e1, e2, e3,
    dn_s, dn_r, bo_s, bo_r, z_s, z_r, t_s, t_r, kc_s, kc_r, kp_s, kp_r, sd_s, sd_r, sk_s, sk_r,
    qc_s, qc_r, qz_s, qz_r, kk_s, kk_r, kz_s, kz_r, oc_s, oc_r, oz_s, oz_r, g2_s, g2_r, gc_s, gc_r,
    gz_s, gz_r, cf_s, cf_r, gm_s, gm_r, in_s,
):
    r = lax.axis_index("row")
    c = lax.axis_index("col")
    z = c // 2
    k = lax.rem(c, 2)
    mates = [(mate(r, m), c) for m in (1, 2, 3)]
    aheads = [(r, z_ahead(c, m)) for m in (1, 2, 3)]
    ahead_z = [lax.rem(z + m, 4) for m in (1, 2, 3)]
    core = (r, other_core(c))
    ready = greet(mates + [core] + aheads)
    loads = {}
    order = (
        ("dwz", dwz_in, dwz), ("gm", gm_in, gm_ref), ("gain2", gain2_in, gain2_ref),
        ("dwd", dwd_in, dwd_ref), ("down", down_in, down_ref), ("wof", wof_in, wof_ref),
        ("q", q_in, q_ref), ("kv", kv_in, kv_ref), ("lse", lse_in, lse_ref),
        ("out", out_in, out_ref), ("att", att_in, att_all), ("n1", n1_in, n1_ref),
        ("wi", wi_in, wi_ref), ("sown", sown_in, sown_ref), ("srow", srow_in, srow_ref),
        ("mid", mid_in, mid_ref),
    )
    for i, (name, src, dst) in enumerate(order):
        loads[name] = pltpu.make_async_copy(src, dst, in_s.at[i])
        loads[name].start()
    mine = block_rows(r)
    sent = []

    def send(src, dst, send_sem, recv_sem, target):
        copy = remote(src, dst, send_sem, recv_sem, target)
        copy.start()
        sent.append(copy)
        return copy

    loads["gm"].wait()
    loads["gain2"].wait()
    for i in range(4):
        g2_out[i] = gain2_ref[:, 288 * i : 288 * i + 288]
    turned = jnp.transpose(gm_ref[...].astype(full)).astype(half)
    for i in range(4):
        gm_out[i] = turned[288 * i : 288 * i + 288]
    gm_nat[:, mine] = gm_out[r]
    loads["down"].wait()
    for m in range(3):
        n0[m] = down_ref[block_rows(mates[m][0]), :]
    mine_has = has_tile(r, z, k)
    my_place = tile_place(r, k, z)
    ready()
    loads["dwz"].wait()
    tile_sums = [
        PlaneSum(
            lambda plane, t=t: dwz.at[t, tile_place(r, k, plane)],
            z_over.at[t], z_joint.at[t], z_last.at[t], r, c, z_s.at[t], z_r.at[t],
            lambda plane: has_tile(r, plane, k),
        )
        for t in range(2)
    ]
    tile_sums[0].start()
    gm_copies = [
        send(gm_out.at[mates[m][0]], gm_nat.at[:, mine], gm_s.at[m], gm_r.at[m], mates[m])
        for m in range(3)
    ]

    def tile_copy(t, m):
        return remote(
            tile_out.at[mates[m][0], t],
            dw_ref.at[tile_of(r, z), t],
            t_s.at[3 * t + m],
            t_r.at[3 * t + m],
            mates[m],
        )

    def tile_back(t):
        @pl.when(mine_has)
        def _():
            value = dwd_ref[...] if t == 2 else dwz[t, my_place].astype(full)
            if t < 2:
                value = value + tile_sums[t].arrive()
            for b in range(4):
                tile_out[b, t] = value[288 * b : 288 * b + 288].astype(half)
            for m in range(3):
                tile_copy(t, m).start()
            dw_ref[tile_of(r, z), t] = tile_out[r, t]

    downs = Scatter(n0, n1, n2, n3, r, c, dn_s, dn_r)
    downs.start()
    g2_copies = [
        send(g2_out.at[mates[m][0]], g2_in.at[m], g2_s.at[m], g2_r.at[m], mates[m])
        for m in range(3)
    ]
    loads["wof"].wait()
    ga = product_right(gm_ref[...], wof_ref[...]).astype(half)
    gaf = ga.astype(full)
    loads["q"].wait()
    queries = q_ref[...] * jnp.bfloat16(0.125)
    cosine, sine = turn_tables(512 * k + TB * r)
    sine = -sine
    bias = mask_bias(starts_ref, z, 512 * k + TB * r)
    loads["kv"].wait()
    loads["lse"].wait()
    loads["out"].wait()
    for g in range(KV_HEADS):
        if g == 5:
            tile_sums[0].relay()
            tile_sums[1].start()
        keys = kv_ref[:, 64 * g : 64 * g + 64]
        values = kv_ref[:, 384 + 64 * g : 448 + 64 * g]
        heads = range(3 * g, 3 * g + 3)
        qh = jnp.concatenate([queries[:, 64 * h : 64 * h + 64] for h in heads], axis=0)
        gh = jnp.concatenate([ga[:, 64 * h : 64 * h + 64] for h in heads], axis=0)
        delta = jnp.concatenate(
            [
                jnp.sum(
                    gaf[:, 64 * h : 64 * h + 64] * out_ref[:, 64 * h : 64 * h + 64],
                    axis=1,
                    keepdims=True,
                )
                for h in heads
            ],
            axis=0,
        )
        scores = product_right(qh, keys).reshape(3, TB, 1024) + bias[None]
        probs = jnp.exp(scores.reshape(3 * TB, 1024) - lse_ref[:, g : g + 1])
        grad_probs = product_right(gh, values)
        grad_scores = (probs * (grad_probs - delta)).astype(half)
        grad_q = product(grad_scores, keys) * 0.125
        for j in range(3):
            h = 3 * g + j
            dqs[:, 64 * h : 64 * h + 64] = grad_q[TB * j : TB * j + TB]
        dkv[:, 64 * g : 64 * g + 64] = product_left(grad_scores, qh)
        dkv[:, 384 + 64 * g : 448 + 64 * g] = product_left(probs.astype(half), gh)
    other_rows = pl.ds(pl.multiple_of(512 * (1 - k), 512), 512)
    dkv_co[...] = dkv[other_rows, :].astype(half)
    kc = send(dkv_co, dkv_ci, kc_s.at[0], kc_r.at[0], core)
    grad_q = dqs[...]
    inner = jnp.sum(grad_q * q_ref[...].astype(full), axis=1, keepdims=True)
    sdq[mine, :] = turn(grad_q, cosine, sine).astype(half)
    q_gather = Gather(lambda b, h: sdq.at[part_rows(b, h)], r, c, sd_s, sd_r)
    q_gather.start()
    kc.wait_recv()
    pairs = Scatter(e0, e1, e2, e3, r, c, kp_s, kp_r)
    for m in (2, 0, 1):
        b = mates[m][0]
        e0[m] = (dkv[block_rows(4 * k + b), :] + dkv_ci[block_rows(b), :].astype(full)).astype(half)
        pairs.start(((0,), (1,), (2, 3))[m])
    my_block = block_rows(4 * k + r)
    dkv[my_block, :] = dkv[my_block, :] + dkv_ci[mine, :].astype(full)
    for m in range(3):
        cols = block_rows(mates[m][0])
        remote(gm_out.at[0], gm_nat.at[:, cols], gm_s.at[m], gm_r.at[m], mates[m]).wait_recv()
    loads["att"].wait()
    grad_wo = lax.dot_general(
        att_all[...], gm_nat[...], (((0,), (1,)), ((), ())), preferred_element_type=full
    )
    for i in range(8):
        dwo[i] = grad_wo[144 * i : 144 * i + 144]

    def wide(value):
        n = value.shape[0] // 3
        return jnp.concatenate([value[n * j : n * j + n] for j in range(3)], axis=1)

    def tall(value):
        n = value.shape[1] // 3
        return jnp.concatenate([value[:, n * j : n * j + n] for j in range(3)], axis=0)

    for i in range(4):
        dwo_co[i] = dwo[2 * i + 1 - k].astype(half)
    oc_copy = send(dwo_co, dwo_ci, oc_s.at[0], oc_r.at[0], core)
    pairs.relay()
    q_gather.relay()
    tile_sums[1].relay()
    downs.relay()
    oc_copy.wait_recv()
    for i in range(4):
        value = dwo[2 * i + k] + dwo_ci[i].astype(full)
        dwo_z[i] = wide(value).astype(half)
        dwo[2 * i + k] = value
    o_sum = PlaneSum(lambda plane: dwo_z.at[plane], dwo_over, dwo_joint, dwo_in, r, c, oz_s, oz_r)
    o_sum.start()
    grad_kv = pairs.finish(dkv[my_block, :])
    sdk[mine, 0:384] = turn(grad_kv[:, 0:384], cosine, sine).astype(half)
    sdk[mine, 384:768] = grad_kv[:, 384:768].astype(half)
    k_gather = Gather(lambda b, h: sdk.at[part_rows(b, h)], r, c, sk_s, sk_r)
    k_gather.start()
    inner = inner + jnp.sum(grad_kv * kv_ref[my_block, :].astype(full), axis=1, keepdims=True)
    loads["sown"].wait()
    scale = sown_ref[...]
    coef = jnp.transpose(inner * (scale * scale) / D)
    coef_all[r] = coef[0:8]
    coef_copies = [
        send(coef_all.at[r], coef_all.at[r], cf_s.at[m], cf_r.at[m], mates[m]) for m in range(3)
    ]
    o_sum.relay()
    loads["n1"].wait()
    q_gather.finish()
    grad_wi = product(n1_ref[...], sdq[...])
    for i in range(8):
        dwq[i] = grad_wi[:, 144 * i : 144 * i + 144]
    for i in range(4):
        dwq_co[i] = dwq[2 * i + 1 - k].astype(half)
    qc_copy = send(dwq_co, dwq_ci, qc_s.at[0], qc_r.at[0], core)
    k_gather.relay()
    loads["dwd"].wait()
    tile_back(2)
    tile_back(0)
    qc_copy.wait_recv()
    for i in range(4):
        value = dwq[2 * i + k] + dwq_ci[i].astype(full)
        dwq_z[i] = wide(value).astype(half)
        dwq[2 * i + k] = value
    q_sum = PlaneSum(lambda plane: dwq_z.at[plane], dwq_over, dwq_joint, dwq_in, r, c, qz_s, qz_r)
    q_sum.start()
    loads["wi"].wait()
    back = product_right(wi_ref[:, 0:1152], sdq[...])
    k_gather.finish()
    grad_wi = product(n1_ref[...], sdk[...])
    for i in range(8):
        dwk[i, :, 0:48] = grad_wi[:, 48 * i : 48 * i + 48]
        dwk[i, :, 48:96] = grad_wi[:, 384 + 48 * i : 432 + 48 * i]
    for i in range(4):
        dwk_co[i] = dwk[2 * i + 1 - k].astype(half)
    kk_copy = send(dwk_co, dwk_ci, kk_s.at[0], kk_r.at[0], core)
    loads["srow"].wait()
    back = (back + product_right(wi_ref[:, 1152:1920], sdk[...])) * srow_ref[0:1, :]
    kk_copy.wait_recv()
    for i in range(4):
        value = dwk[2 * i + k] + dwk_ci[i].astype(full)
        dwk_z[i] = value.astype(half)
        dwk[2 * i + k] = value
    kz_copies = [
        send(dwk_z.at[ahead_z[m]], dwk_in.at[m], kz_s.at[m], kz_r.at[m], aheads[m])
        for m in range(3)
    ]
    q_sum.relay()
    tile_back(1)
    loads["mid"].wait()
    dn_own[...] = mid_ref[...] + down_ref[mine, :].astype(full)
    result = downs.finish(dn_own)
    result = jnp.transpose(result).astype(half)
    for i in range(4):
        bo_out[i] = result[288 * i : 288 * i + 288]
    bo_ref[:, mine] = bo_out[r]
    bo_copies = [
        send(bo_out.at[mates[m][0]], bo_ref.at[:, mine], bo_s.at[m], bo_r.at[m], mates[m])
        for m in range(3)
    ]
    for m in range(3):
        b = mates[m][0]
        remote(coef_all.at[b], coef_all.at[b], cf_s.at[m], cf_r.at[m], mates[m]).wait_recv()
    coef = jnp.concatenate([coef_all[i] for i in range(4)], axis=1)[0:1, :]
    tokens = tok_ref[...].astype(full)
    gain1 = jnp.transpose(jnp.broadcast_to(gains_in[0:1, :], (128, 288)))[:, 0:1]
    ig_ref[...] = (gm_nat[...].astype(full) + back * gain1 - tokens * coef).astype(half)
    for copy in g2_copies:
        copy.wait_recv()
    column = jnp.sum(back * tokens, axis=1, keepdims=True)
    gl[0] = jnp.transpose(jnp.broadcast_to(column, (288, 128)))[0:8]
    gl[1] = g2_out[r] + g2_in[0] + g2_in[1] + g2_in[2]
    gc_copy = send(gl, gl_ci, gc_s.at[0], gc_r.at[0], core)
    gc_copy.wait_recv()
    gl_z[...] = gl[...] + gl_ci[...]
    gz_copies = [send(gl_z, gl_in.at[m], gz_s.at[m], gz_r.at[m], aheads[m]) for m in range(3)]
    total = dwo[2 * z + k] + tall(o_sum.arrive())
    do_ref[...] = total
    for m in range(3):
        cols = block_rows(mates[m][0])
        remote(bo_out.at[0], bo_ref.at[:, cols], bo_s.at[m], bo_r.at[m], mates[m]).wait_recv()
    for m in range(3):
        b = mates[m][0]

        @pl.when(has_tile(b, z, k))
        def _():
            for t in range(3):
                remote(
                    tile_out.at[0, t],
                    dw_ref.at[tile_of(b, z), t],
                    t_s.at[3 * t + m],
                    t_r.at[3 * t + m],
                    mates[m],
                ).wait_recv()

    total = dwq[2 * z + k] + tall(q_sum.arrive())
    dq_ref[:, 0:144] = total
    total = dwk[2 * z + k]
    for m in range(3):
        kz_copies[m].wait_recv()
        total = total + dwk_in[m].astype(full)
    dq_ref[:, 144:240] = total
    total = gl_z[...]
    for m in range(3):
        gz_copies[m].wait_recv()
        total = total + gl_in[m]
    gains_ref[...] = total
    for copy in sent:
        copy.wait_send()
    for part in (downs, pairs, q_gather, k_gather, o_sum, q_sum, *tile_sums):
        part.sent()
    @pl.when(mine_has)
    def _():
        for t in range(3):
            for m in range(3):
                tile_copy(t, m).wait_send()


def back(*args):
    shape = jax.ShapeDtypeStruct
    sems = []
    for count in (6, 3, (2, 5), 9, 1, 6, 4, 4, 1, 5, 1, 3, 1, 5, 3, 1, 3, 3, 3):
        count = count if isinstance(count, tuple) else (count,)
        sems += [pltpu.SemaphoreType.DMA(count)] * 2
    v = pltpu.VMEM
    return pl.pallas_call(
        back_kernel,
        out_shape=(
            shape((288, 512), half),
            shape((288, 512), half),
            shape((3, 3, 288, 128), half),
            shape((288, 240), full),
            shape((144, 288), full),
            shape((2, 8, 288), full),
        ),
        in_specs=[pl.BlockSpec(memory_space=pl.ANY)] * 16 + [VM] * 2 + [SM],
        out_specs=(VM,) * 6,
        scratch_shapes=[
            v((TB, D), full),
            v((TB, D), half),
            v((1024, 768), half),
            v((3 * TB, 128), full),
            v((TB, D), full),
            v((D, D), half),
            v((288, 1920), half),
            v((288, 512), half),
            v((8, 512), full),
            v((TB, 128), full),
            v((512, D), half),
            v((TB, D), half),
            v((512, D), half),
            v((8, D), full),
            v((2, 3, D, 128), half),
            v((D, 128), full),
            v((4, 288, TB), half),
            v((288, 512), half),
            v((4, 288, TB), half),
            v((2, 2, D, 128), half),
            v((2, 2, D, 128), half),
            v((2, 2, D, 128), half),
            v((4, 3, 288, 128), half),
            v((1024, 768), full),
            v((512, 768), half),
            v((512, 768), half),
            v((512, D), half),
            v((512, 768), half),
            v((TB, D), full),
            v((8, 288, 144), full),
            v((4, 288, 144), half),
            v((4, 288, 144), half),
            v((4, 96, 432), half),
            v((2, 96, 432), half),
            v((2, 96, 432), half),
            v((2, 96, 432), half),
            v((8, 288, 96), full),
            v((4, 288, 96), half),
            v((4, 288, 96), half),
            v((4, 288, 96), half),
            v((3, 288, 96), half),
            v((8, 144, 288), full),
            v((4, 144, 288), half),
            v((4, 144, 288), half),
            v((4, 48, 864), half),
            v((2, 48, 864), half),
            v((2, 48, 864), half),
            v((2, 48, 864), half),
            v((4, 8, 288), full),
            v((3, 8, 288), full),
            v((2, 8, 288), full),
            v((2, 8, 288), full),
            v((2, 8, 288), full),
            v((3, 2, 8, 288), full),
            v((4, 8, TB), full),
            v((TB, D), full),
        ]
        + scatter_buffers(D)
        + scatter_buffers(768)
        + sems
        + [pltpu.SemaphoreType.DMA((16,))],
        compiler_params=pltpu.CompilerParams(
            collective_id=3, has_side_effects=True, vmem_limit_bytes=60 << 20
        ),
    )(*args)


SETS = (("gu", (2, 288, 384)), ("d", (288, 384)), ("o", (144, 288)), ("q", (144, 288)),
        ("kv", (2, 48, 288)), ("g", (2, 288)))


def update_kernel(*refs):
    grads, refs = refs[:6], refs[6:]
    ins, refs = refs[:18], refs[18:]
    acts, refs = refs[:2], refs[2:]
    outs, refs = refs[:23], refs[23:]
    grad_v, refs = refs[:6], refs[6:]
    in_v, refs = refs[:18], refs[18:]
    out_v, refs = refs[:23], refs[23:]
    grad_s, in_s, out_s = refs
    loads = []
    for n in range(6):
        for i in range(3):
            j = 3 * n + i
            loads.append(pltpu.make_async_copy(ins[j], in_v[j], in_s.at[j]))
    grad_loads = [pltpu.make_async_copy(grads[i], grad_v[i], grad_s.at[i]) for i in range(6)]
    grad_loads[2].start()
    for copy in loads[:6]:
        copy.start()
    for i in (4, 3, 5, 0, 1):
        grad_loads[i].start()
    for copy in loads[6:]:
        copy.start()
    stores = []

    def store(src, dst):
        copy = pltpu.make_async_copy(src, dst, out_s.at[len(stores)])
        copy.start()
        stores.append(copy)

    fix = 1.0 - BETA**STEP

    def step(n, at, grad, rate, decay):
        weight = in_v[3 * n][at]
        first = BETA * in_v[3 * n + 1][at] + (1.0 - BETA) * grad
        second = BETA * in_v[3 * n + 2][at] + (1.0 - BETA) * grad * grad
        change = first / fix / (jnp.sqrt(second / fix) + TINY)
        weight = weight - rate * (change + decay * weight)
        out_v[4 * n][at] = first
        out_v[4 * n + 1][at] = second
        out_v[4 * n + 2][at] = weight
        if n < 5:
            out_v[4 * n + 3][at] = weight.astype(half)

    def ready(n):
        for copy in loads[3 * n : 3 * n + 3]:
            copy.wait()

    def done(n, at=None):
        for j in range(4 * n, min(4 * n + 4, 23)):
            if at is None:
                store(out_v[j], outs[j])
            else:
                store(out_v[j].at[at], outs[j].at[at])

    rate = D**-0.5
    every = (slice(None), slice(None))
    cols = [(slice(None), slice(128 * i, 128 * i + 128)) for i in range(3)]
    dw, dq, do, dg = grad_v[2:]
    grad_loads[2].wait()
    ready(0)
    for t in range(2):
        for i in range(3):
            step(0, (t,) + cols[i], dw[i, t].astype(full), rate, DECAY)
        done(0, t)
    ready(1)
    for i in range(3):
        step(1, cols[i], dw[i, 2].astype(full), FF**-0.5, DECAY)
    done(1)
    grad_loads[4].wait()
    ready(2)
    step(2, every, do[...], rate, DECAY)
    done(2)
    grad_loads[3].wait()
    ready(3)
    turned = jnp.transpose(dq[...])
    step(3, every, turned[0:144], rate, DECAY)
    done(3)
    ready(4)
    for t in range(2):
        step(4, (t, slice(None), slice(None)), turned[144 + 48 * t : 192 + 48 * t], rate, DECAY)
    done(4)
    grad_loads[5].wait()
    ready(5)
    step(5, every, jnp.concatenate([dg[0, 0:1], dg[1, 0:1]], axis=0), 0.25, 0.0)
    done(5)
    for i in range(2):
        grad_loads[i].wait()
        store(grad_v[i], acts[i])
    for copy in stores:
        copy.wait()


def update(grads, params):
    shape = jax.ShapeDtypeStruct
    v = pltpu.VMEM
    outs = []
    for name, dims in SETS:
        outs += [shape(dims, full)] * 3
        if name != "g":
            outs.append(shape(dims, half))
    acts = [shape((288, 512), half)] * 2
    hbm = pl.BlockSpec(memory_space=pl.ANY)
    result = pl.pallas_call(
        update_kernel,
        out_shape=tuple(acts + outs),
        in_specs=[hbm] * 24,
        out_specs=(hbm,) * 25,
        scratch_shapes=[v(g.shape, g.dtype) for g in grads]
        + [v(dims, full) for name, dims in SETS for i in range(3)]
        + [v(o.shape, o.dtype) for o in outs]
        + [
            pltpu.SemaphoreType.DMA((6,)),
            pltpu.SemaphoreType.DMA((18,)),
            pltpu.SemaphoreType.DMA((32,)),
        ],
        compiler_params=pltpu.CompilerParams(vmem_limit_bytes=60 << 20),
    )(*grads, *params)
    gu, d, o, q, kv, g = (result[2 + 4 * n : 6 + 4 * n] for n in range(6))
    return (*result[:2], *g, *q, *kv, *o, *gu, *d)


def swap(value):
    return jnp.swapaxes(value, -1, -2)


def local_fast(
    tokens,
    cotangent,
    starts,
    gains,
    gains_m,
    gains_v,
    w_query,
    w_query_m,
    w_query_v,
    w_keyval,
    w_keyval_m,
    w_keyval_v,
    w_output,
    w_output_m,
    w_output_v,
    w_gateup,
    w_gateup_m,
    w_gateup_v,
    w_down,
    w_down_m,
    w_down_v,
):
    tok = swap(tokens)
    kept = forward(
        tok, swap(cotangent), swap(w_query), swap(w_keyval), w_output, w_gateup, swap(w_down),
        gains, starts
    )
    grads = back(*kept, tok, gains, starts)
    params = []
    for group in (
        (w_gateup, w_gateup_m, w_gateup_v),
        (swap(w_down), swap(w_down_m), swap(w_down_v)),
        (w_output, w_output_m, w_output_v),
        (swap(w_query), swap(w_query_m), swap(w_query_v)),
        (swap(w_keyval), swap(w_keyval_m), swap(w_keyval_v)),
        (gains, gains_m, gains_v),
    ):
        params += group
    outs = update(grads, params)
    turned = (0, 1, 5, 6, 7, 8, 9, 10, 11, 12, 21, 22, 23, 24)
    return tuple(swap(value) if i in turned else value for i, value in enumerate(outs))


def local(tokens, *others):
    fits = lax.axis_size("row") == 4 and lax.axis_size("col") == 8 and tokens.shape == (512, 288)
    plan = local_fast if fits else local_general
    return plan(tokens, *others)


def solution(mesh):
    return jax.shard_map(
        local,
        mesh=mesh,
        in_specs=(
            P("col", "row"),
            P("col", "row"),
            P(),
            P(None, "row"),
            P(None, "row"),
            P(None, "row"),
            P("row", "col"),
            P("row", "col"),
            P("row", "col"),
            P(None, "row", "col"),
            P(None, "row", "col"),
            P(None, "row", "col"),
            P("col", "row"),
            P("col", "row"),
            P("col", "row"),
            P(None, "row", "col"),
            P(None, "row", "col"),
            P(None, "row", "col"),
            P("col", "row"),
            P("col", "row"),
            P("col", "row"),
        ),
        out_specs=(
            P("col", "row"),
            P("col", "row"),
            P(None, "row"),
            P(None, "row"),
            P(None, "row"),
            P("row", "col"),
            P("row", "col"),
            P("row", "col"),
            P("row", "col"),
            P(None, "row", "col"),
            P(None, "row", "col"),
            P(None, "row", "col"),
            P(None, "row", "col"),
            P("col", "row"),
            P("col", "row"),
            P("col", "row"),
            P("col", "row"),
            P(None, "row", "col"),
            P(None, "row", "col"),
            P(None, "row", "col"),
            P(None, "row", "col"),
            P("col", "row"),
            P("col", "row"),
            P("col", "row"),
            P("col", "row"),
        ),
        check_vma=False,
    )
```

```python
import jax
import jax.numpy as jnp
from jax import lax
from jax.experimental import pallas as pl
from jax.experimental.pallas import tpu as pltpu
from jax.sharding import PartitionSpec as P

D = 1152
HEADS = 18
KV_HEADS = 6
HD = 64
FF = 3072
TD = 128
PIECE = 256
PIECES = 4
STEP = 7


EPS = 1e-05
BETA = 0.5
TINY = 1e-08
DECAY = 0.1
MASKED = -1e30


def to_half(value):
    return value.astype(jnp.bfloat16)


def product(left, right):
    return jnp.dot(left, right, preferred_element_type=jnp.float32)


def product_left(left, right):
    return lax.dot_general(
        left, right, (((0,), (0,)), ((), ())), preferred_element_type=jnp.float32
    )


def product_right(left, right):
    return lax.dot_general(
        left, right, (((1,), (1,)), ((), ())), preferred_element_type=jnp.float32
    )


def col_collect(value):
    return lax.all_gather(value, "col", axis=0, tiled=True)


def row_collect(value):
    return lax.all_gather(value, "row", axis=0, tiled=True)


def row_reduce(value):
    return lax.psum_scatter(value, "row", scatter_dimension=0, tiled=True)


def col_reduce(value):
    return lax.psum_scatter(value, "col", scatter_dimension=0, tiled=True)


def row_total(value):
    return lax.psum(value, "row")


def to_heads(value):
    return lax.all_to_all(value, "col", split_axis=0, concat_axis=1, tiled=True)


def to_rows(value):
    return lax.all_to_all(value, "col", split_axis=1, concat_axis=0, tiled=True)


def norm_forward(hidden, gain):
    total = row_total(jnp.sum(hidden * hidden, axis=1))
    scale = lax.rsqrt(total / D + EPS)
    return (scale, to_half(hidden * scale[:, None] * gain[None, :]))


def norm_backward(hidden, gain, scale, grad):
    inner = row_total(jnp.sum(grad * gain[None, :] * hidden, axis=1))
    back = (
        grad * gain[None, :] * scale[:, None]
        - hidden * (scale * scale * scale * inner / D)[:, None]
    )
    gain_grad = jnp.sum(grad * hidden * scale[:, None], axis=0)
    return (back, gain_grad)


def rotary(places):
    half = HD // 2
    freq = 10000.0 ** (-2.0 * jnp.arange(half, dtype=jnp.float32) / HD)
    angle = places[:, None] * freq[None, :]
    return (jnp.cos(angle), jnp.sin(angle))


def rotate(heads, cosine, sine):
    half = HD // 2
    first = heads[..., :half]
    second = heads[..., half:]
    cosine = cosine[:, None, :]
    sine = sine[:, None, :]
    return jnp.concatenate(
        [first * cosine - second * sine, second * cosine + first * sine], axis=-1
    )


def rotate_back(heads, cosine, sine):
    half = HD // 2
    first = heads[..., :half]
    second = heads[..., half:]
    cosine = cosine[:, None, :]
    sine = sine[:, None, :]
    return jnp.concatenate(
        [first * cosine + second * sine, second * cosine - first * sine], axis=-1
    )


def piece_ids(pieces, places):
    inside = (places[:, None] >= pieces[None, :]) & (places[:, None] < pieces[None, :] + PIECE)
    number = jnp.arange(1, PIECES + 1, dtype=jnp.int32)
    return jnp.sum(jnp.where(inside, number[None, :], 0), axis=1) - 1


def block_scores(queries, keys, places, ids, pieces, start):
    key_places = start + jnp.arange(keys.shape[0], dtype=jnp.int32)
    key_ids = piece_ids(pieces, key_places)
    raw = jnp.einsum("tkgd,skd->kgts", queries, keys, preferred_element_type=jnp.float32) * HD ** (
        -0.5
    )
    allowed = (key_places[None, :] <= places[:, None]) | (key_ids[None, :] == ids[:, None]) & (
        ids[:, None] >= 0
    )
    allowed = allowed[None, None]
    return (jnp.where(allowed, raw, MASKED), allowed)


def split_blocks(keyvals, width):
    count = keyvals.shape[0] // width
    blocks = keyvals.reshape(count, width, 2, KV_HEADS, HD)
    firsts = jnp.arange(count, dtype=jnp.int32) * width
    return (blocks, firsts)


def attend(queries, keyvals, places, ids, pieces, width):
    blocks, firsts = split_blocks(keyvals, width)
    shape = (KV_HEADS, queries.shape[2], queries.shape[0])

    def measure(carry, item):
        high, total = carry
        scores, allowed = block_scores(queries, item[0][:, 0], places, ids, pieces, item[1])
        new_high = jnp.maximum(high, jnp.max(scores, axis=-1))
        weights = jnp.where(allowed, jnp.exp(scores - new_high[..., None]), 0.0)
        return ((new_high, total * jnp.exp(high - new_high) + jnp.sum(weights, axis=-1)), None)

    start_state = (jnp.full(shape, MASKED, jnp.float32), jnp.zeros(shape, jnp.float32))
    (high, total), unused = lax.scan(measure, start_state, (blocks, firsts))
    logsum = high + jnp.log(total)

    def accumulate(acc, item):
        scores, allowed = block_scores(queries, item[0][:, 0], places, ids, pieces, item[1])
        probs = to_half(jnp.where(allowed, jnp.exp(scores - logsum[..., None]), 0.0))
        return (
            acc
            + jnp.einsum(
                "kgts,skd->tkgd", probs, item[0][:, 1], preferred_element_type=jnp.float32
            ),
            None,
        )

    output, unused = lax.scan(accumulate, jnp.zeros(queries.shape, jnp.float32), (blocks, firsts))
    return (output, logsum)


def attend_back(queries, keyvals, places, ids, pieces, width, logsum, grad_out, output):
    blocks, firsts = split_blocks(keyvals, width)
    delta = jnp.einsum("tkgd,tkgd->kgt", grad_out.astype(jnp.float32), output)
    factor = HD ** (-0.5)

    def sweep(acc, item):
        keys = item[0][:, 0]
        values = item[0][:, 1]
        scores, allowed = block_scores(queries, keys, places, ids, pieces, item[1])
        probs = jnp.where(allowed, jnp.exp(scores - logsum[..., None]), 0.0)
        grad_probs = jnp.einsum(
            "tkgd,skd->kgts", grad_out, values, preferred_element_type=jnp.float32
        )
        grad_scores = to_half(probs * (grad_probs - delta[..., None]))
        acc = (
            acc
            + jnp.einsum("kgts,skd->tkgd", grad_scores, keys, preferred_element_type=jnp.float32)
            * factor
        )
        grad_keys = (
            jnp.einsum("kgts,tkgd->skd", grad_scores, queries, preferred_element_type=jnp.float32)
            * factor
        )
        grad_values = jnp.einsum(
            "kgts,tkgd->skd", to_half(probs), grad_out, preferred_element_type=jnp.float32
        )
        joined = jnp.concatenate(
            [grad_keys.reshape(width, -1), grad_values.reshape(width, -1)], axis=1
        )
        return (acc, joined)

    grad_queries, grad_blocks = lax.scan(
        sweep, jnp.zeros(queries.shape, jnp.float32), (blocks, firsts)
    )
    return (grad_queries, grad_blocks.reshape(keyvals.shape[0], -1))


def adamw(weight, first, second, grad, rate, decay):
    first_new = BETA * first + (1.0 - BETA) * grad
    second_new = BETA * second + (1.0 - BETA) * grad * grad
    fix = 1.0 - BETA**STEP
    update = first_new / fix / (jnp.sqrt(second_new / fix) + TINY)
    weight_new = weight - rate * (update + decay * weight)
    return (first_new, second_new, weight_new)


def grid_plan(tokens, cotangent, starts, gains, w_query, w_keyval, w_output, w_gateup, w_down):
    columns = lax.axis_size("col")
    column = lax.axis_index("col")
    seq_len = TD * columns
    width = min(1024, seq_len)
    group = HEADS // KV_HEADS
    query_width = w_query.shape[1]
    key_width = w_keyval.shape[2]
    feed_width = w_gateup.shape[2]
    pieces = lax.dynamic_index_in_dim(starts, lax.axis_index("row"), 0, keepdims=False)
    hidden = tokens.astype(jnp.float32)
    inner_weights = to_half(jnp.concatenate([w_query, w_keyval[0], w_keyval[1]], axis=1))
    feed_weights = to_half(jnp.concatenate([w_gateup[0], w_gateup[1]], axis=1))
    out_weights = to_half(w_output)
    down_weights = to_half(w_down)
    scale_one, normed_one = norm_forward(hidden, gains[0])
    gathered_one = col_collect(normed_one)
    mixed = to_half(row_reduce(product(gathered_one, inner_weights)))
    spread = to_heads(mixed[:, None, :])
    query_raw = spread[:, :, :query_width].reshape(TD, HEADS, HD)
    key_raw = spread[:, :, query_width : query_width + key_width].reshape(TD, KV_HEADS, HD)
    value_heads = spread[:, :, query_width + key_width :].reshape(TD, KV_HEADS * HD)
    places = column * TD + jnp.arange(TD, dtype=jnp.int32)
    cosine, sine = rotary(places.astype(jnp.float32))
    queries = to_half(rotate(query_raw.astype(jnp.float32), cosine, sine)).reshape(
        TD, KV_HEADS, group, HD
    )
    keys = to_half(rotate(key_raw.astype(jnp.float32), cosine, sine))
    keyvals_local = jnp.concatenate([keys.reshape(TD, KV_HEADS * HD), value_heads], axis=1)
    keyvals = lax.all_gather(keyvals_local, "col", axis=0, tiled=True)
    ids = piece_ids(pieces, places)
    output, logsum = attend(queries, keyvals, places, ids, pieces, width)
    attended = to_half(output)
    attended_rows = to_rows(attended.reshape(TD, columns, query_width))[:, 0, :]
    gathered_att = row_collect(attended_rows)
    branch = col_reduce(product(gathered_att, out_weights))
    middle = hidden + branch
    scale_two, normed_two = norm_forward(middle, gains[1])
    gathered_two = col_collect(normed_two)
    feed = row_reduce(product(gathered_two, feed_weights))
    gate = feed[:, :feed_width]
    upward = feed[:, feed_width:]
    sigma = jax.nn.sigmoid(gate)
    swish = gate * sigma
    activated = to_half(swish * upward)
    gathered_act = row_collect(activated)
    result = middle + col_reduce(product(gathered_act, down_weights))
    block_out = to_half(result)
    both = lax.all_gather(jnp.stack([normed_one, normed_two]), "col", axis=1, tiled=True)
    back_one = both[0]
    back_two = both[1]
    grad_rows = col_collect(cotangent)
    grad_down = product_left(gathered_act, grad_rows)
    grad_act = row_reduce(product_right(grad_rows, down_weights))
    slope = sigma * (1.0 + gate * (1.0 - sigma))
    grad_feed = to_half(jnp.concatenate([grad_act * upward * slope, grad_act * swish], axis=1))
    gathered_feed = row_collect(grad_feed)
    grad_both = product_left(back_two, gathered_feed)
    grad_gateup = jnp.stack([grad_both[:, :feed_width], grad_both[:, feed_width:]])
    grad_normed_two = col_reduce(product_right(gathered_feed, feed_weights))
    norm_two_back, gain_two = norm_backward(middle, gains[1], scale_two, grad_normed_two)
    grad_middle = cotangent.astype(jnp.float32) + norm_two_back
    gathered_mid = col_collect(to_half(grad_middle))
    grad_output = product_left(gathered_att, gathered_mid)
    grad_att = to_half(row_reduce(product_right(gathered_mid, out_weights)))
    grad_heads = to_heads(grad_att[:, None, :]).reshape(TD, KV_HEADS, group, HD)
    keyvals_back = lax.all_gather(keyvals_local, "col", axis=0, tiled=True)
    grad_queries, grad_keyvals = attend_back(
        queries, keyvals_back, places, ids, pieces, width, logsum, grad_heads, output
    )
    local_keyvals = lax.psum_scatter(grad_keyvals, "col", scatter_dimension=0, tiled=True)
    kv_split = KV_HEADS * HD
    grad_query_raw = rotate_back(grad_queries.reshape(TD, HEADS, HD), cosine, sine)
    grad_key_raw = rotate_back(local_keyvals[:, :kv_split].reshape(TD, KV_HEADS, HD), cosine, sine)
    grad_value = local_keyvals[:, kv_split:]
    joined = jnp.concatenate(
        [
            to_half(grad_query_raw).reshape(TD, columns, query_width),
            to_half(grad_key_raw).reshape(TD, columns, key_width),
            to_half(grad_value).reshape(TD, columns, key_width),
        ],
        axis=2,
    )
    grad_mixed = to_rows(joined)[:, 0, :]
    gathered_mixed = row_collect(grad_mixed)
    grad_inner = product_left(back_one, gathered_mixed)
    grad_query = grad_inner[:, :query_width]
    grad_keyval = jnp.stack(
        [
            grad_inner[:, query_width : query_width + key_width],
            grad_inner[:, query_width + key_width :],
        ]
    )
    grad_normed_one = col_reduce(product_right(gathered_mixed, inner_weights))
    norm_one_back, gain_one = norm_backward(hidden, gains[0], scale_one, grad_normed_one)
    input_grad = to_half(grad_middle + norm_one_back)
    gain_grads = lax.psum(jnp.stack([gain_one, gain_two]), "col")
    return (
        block_out,
        input_grad,
        gain_grads,
        grad_query,
        grad_keyval,
        grad_output,
        grad_gateup,
        grad_down,
    )


def local_general(
    tokens,
    cotangent,
    starts,
    gains,
    gains_m,
    gains_v,
    w_query,
    w_query_m,
    w_query_v,
    w_keyval,
    w_keyval_m,
    w_keyval_v,
    w_output,
    w_output_m,
    w_output_v,
    w_gateup,
    w_gateup_m,
    w_gateup_v,
    w_down,
    w_down_m,
    w_down_v,
):
    results = grid_plan(
        tokens, cotangent, starts, gains, w_query, w_keyval, w_output, w_gateup, w_down
    )
    (
        block_out,
        input_grad,
        gain_grads,
        grad_query,
        grad_keyval,
        grad_output,
        grad_gateup,
        grad_down,
    ) = results
    rate_in = D ** (-0.5)
    rate_down = FF ** (-0.5)
    gain_m, gain_v, gain_w = adamw(gains, gains_m, gains_v, gain_grads, 0.25, 0.0)
    query_m, query_v, query_w = adamw(w_query, w_query_m, w_query_v, grad_query, rate_in, DECAY)
    keyval_m, keyval_v, keyval_w = adamw(
        w_keyval, w_keyval_m, w_keyval_v, grad_keyval, rate_in, DECAY
    )
    output_m, output_v, output_w = adamw(
        w_output, w_output_m, w_output_v, grad_output, rate_in, DECAY
    )
    gateup_m, gateup_v, gateup_w = adamw(
        w_gateup, w_gateup_m, w_gateup_v, grad_gateup, rate_in, DECAY
    )
    down_m, down_v, down_w = adamw(w_down, w_down_m, w_down_v, grad_down, rate_down, DECAY)
    return (
        block_out,
        input_grad,
        gain_m,
        gain_v,
        gain_w,
        query_m,
        query_v,
        query_w,
        to_half(query_w),
        keyval_m,
        keyval_v,
        keyval_w,
        to_half(keyval_w),
        output_m,
        output_v,
        output_w,
        to_half(output_w),
        gateup_m,
        gateup_v,
        gateup_w,
        to_half(gateup_w),
        down_m,
        down_v,
        down_w,
        to_half(down_w),
    )


TB = 128
LOG_BASE = 9.210340371976184
MESH = pl.DeviceIdType.MESH
half = jnp.bfloat16
full = jnp.float32
VM = pl.BlockSpec(memory_space=pltpu.VMEM)
SM = pl.BlockSpec(memory_space=pltpu.SMEM)


def mate(r, m):
    x = lax.rem(lax.rem(r, 2) + lax.rem(m, 2), 2)
    y = lax.rem(r // 2 + m // 2, 2)
    return 2 * y + x


def other_core(c):
    return c + 1 - 2 * lax.rem(c, 2)


def z_ahead(c, m):
    return lax.rem(c + 2 * m, 8)


def block_rows(b):
    return pl.ds(pl.multiple_of(b * TB, TB), TB)


def part_rows(b, h):
    if h is None:
        return block_rows(b)
    return pl.ds(pl.multiple_of(b * TB + 64 * h, 64), 64)


def slice_rows(b, h=None):
    if h is None:
        return pl.ds(pl.multiple_of(b * 288, 32), 288)
    return pl.ds(pl.multiple_of(b * 288 + 144 * h, 16), 144)


def greet(targets):
    barrier = pltpu.get_barrier_semaphore()
    for target in targets:
        pl.semaphore_signal(barrier, inc=1, device_id=target, device_id_type=MESH)
    return lambda: pl.semaphore_wait(barrier, len(targets))


def remote(src, dst, send, recv, target):
    return pltpu.make_async_remote_copy(
        src_ref=src, dst_ref=dst, send_sem=send, recv_sem=recv, device_id=target, device_id_type=MESH
    )


class Gather:
    def __init__(self, view, r, c, send, recv):
        x, y, far = mate(r, 1), mate(r, 2), mate(r, 3)
        self.first = [
            remote(view(r, 0), view(r, 0), send.at[0], recv.at[0], (x, c)),
            remote(view(r, 1), view(r, 1), send.at[1], recv.at[1], (y, c)),
            remote(view(r, 1), view(r, 1), send.at[4], recv.at[4], (x, c)),
            remote(view(r, 0), view(r, 0), send.at[5], recv.at[5], (y, c)),
        ]
        self.onward = [
            remote(view(x, 0), view(x, 0), send.at[2], recv.at[2], (y, c)),
            remote(view(y, 1), view(y, 1), send.at[3], recv.at[3], (x, c)),
        ]
        self.arrive = [
            remote(view(x, 0), view(x, 0), send.at[0], recv.at[0], (x, c)),
            remote(view(y, 1), view(y, 1), send.at[1], recv.at[1], (y, c)),
            remote(view(far, 0), view(far, 0), send.at[2], recv.at[2], (y, c)),
            remote(view(far, 1), view(far, 1), send.at[3], recv.at[3], (x, c)),
            remote(view(x, 1), view(x, 1), send.at[4], recv.at[4], (x, c)),
            remote(view(y, 0), view(y, 0), send.at[5], recv.at[5], (y, c)),
        ]

    def start(self):
        for copy in self.first:
            copy.start()

    def relay(self):
        for i in range(2):
            self.arrive[i].wait_recv()
            self.onward[i].start()
        for i in (4, 5):
            self.arrive[i].wait_recv()

    def finish(self):
        self.arrive[2].wait_recv()
        self.arrive[3].wait_recv()

    def sent(self):
        for copy in self.first + self.onward:
            copy.wait_send()


class Scatter:
    def __init__(self, out, near, mid, last, r, c, send, recv):
        x, y = (mate(r, 1), c), (mate(r, 2), c)
        up, low = pl.ds(0, 64), pl.ds(64, 64)
        self.out, self.near, self.mid, self.last = out, near, mid, last
        self.first = [
            remote(out.at[0, up], near.at[0, 0], send.at[0], recv.at[0], x),
            remote(out.at[1, low], near.at[1, 0], send.at[1], recv.at[1], y),
            remote(out.at[2, up], near.at[0, 1], send.at[2], recv.at[2], x),
            remote(out.at[2, low], near.at[1, 1], send.at[3], recv.at[3], y),
        ]
        self.second = [
            remote(mid.at[0], last.at[0], send.at[4], recv.at[4], y),
            remote(mid.at[1], last.at[1], send.at[5], recv.at[5], x),
        ]

    def start(self, which=(2, 3, 0, 1)):
        for i in which:
            self.first[i].start()

    def relay(self):
        self.first[2].wait_recv()
        self.mid[0] = (self.out[1, 0:64].astype(full) + self.near[0, 1].astype(full)).astype(half)
        self.second[0].start()
        self.first[3].wait_recv()
        self.mid[1] = (self.out[0, 64:128].astype(full) + self.near[1, 1].astype(full)).astype(half)
        self.second[1].start()

    def finish(self, own):
        for copy in self.first[:2] + self.second:
            copy.wait_recv()
        upper = own[0:64] + self.near[0, 0].astype(full) + self.last[0].astype(full)
        lower = own[64:128] + self.near[1, 0].astype(full) + self.last[1].astype(full)
        return jnp.concatenate([upper, lower], axis=0)

    def sent(self):
        for copy in self.first + self.second:
            copy.wait_send()


def scatter_buffers(width):
    v = pltpu.VMEM
    return [
        v((3, TB, width), half),
        v((2, 2, 64, width), half),
        v((2, 64, width), half),
        v((2, 64, width), half),
    ]


def idle_plane(r, k):
    x = lax.rem(r, 2)
    return 2 * (1 - lax.rem(x + k, 2)) + 1 - r // 2


def tile_place(r, k, z):
    return jnp.minimum(lax.rem(z - idle_plane(r, k) + 3, 4), 2)


def has_tile(b, z, k):
    return (b // 2 == lax.rem(z, 2)) | (lax.rem(b, 2) == lax.rem(k + z // 2, 2))


def tile_of(b, z):
    return jnp.where(b // 2 == lax.rem(z, 2), lax.rem(b, 2), 2)


def tile_cols(place):
    return pl.ds(pl.multiple_of(place * 128, 128), 128)


class TileGather:
    def __init__(self, mine, view, r, c, zs, zr, cs, cr):
        self.r, self.z, self.k = r, c // 2, lax.rem(c, 2)
        core = (r, other_core(c))
        z, k = self.z, self.k
        self.has = has_tile(r, z, k)
        here = view(3 * k + tile_place(r, k, z))
        self.out = [remote(mine, here, zs.at[m], zr.at[m], (r, z_ahead(c, m + 1))) for m in range(3)]
        self.out.append(remote(mine, here, cs.at[3], cr.at[3], core))
        self.relays = []
        for m in range(3):
            src = lax.rem(z + 3 - m, 4)
            slot = view(3 * k + tile_place(r, k, src))
            self.relays.append(
                (
                    has_tile(r, src, k),
                    remote(slot, slot, zs.at[m], zr.at[m], core),
                    remote(slot, slot, cs.at[m], cr.at[m], core),
                )
            )
        self.others = []
        for m in range(4):
            src = z if m == 3 else lax.rem(z + 3 - m, 4)
            slot = view(3 * (1 - k) + tile_place(r, 1 - k, src))
            self.others.append(
                (has_tile(r, src, 1 - k), remote(slot, slot, cs.at[m], cr.at[m], core))
            )

    def start(self):
        for copy in self.out:
            copy.start()

    def relay(self):
        for flag, come, go in self.relays:

            @pl.when(flag)
            def _():
                come.wait_recv()
                go.start()

    def finish(self):
        for flag, come in self.others:

            @pl.when(flag)
            def _():
                come.wait_recv()

    def sent(self):
        @pl.when(self.has)
        def _():
            for copy in self.out:
                copy.wait_send()

        for flag, come, go in self.relays:

            @pl.when(flag)
            def _():
                go.wait_send()


class PlaneSum:
    def __init__(self, part, over, joint, last, r, c, send, recv, has=None):
        z, k = c // 2, lax.rem(c, 2)
        side = z // 2
        beside = 2 * side + 1 - lax.rem(z, 2)
        self.far = (2 - side, 3 - 3 * side)
        self.part, self.over, self.joint, self.last = part, over, joint, last
        has = has or (lambda plane: plane >= 0)
        at_end = (z == 0) | (z == 3)
        self.owns = has(z)
        to = lambda plane: (r, 2 * plane + k)
        self.direct = (
            has(beside), remote(part(beside), last.at[0], send.at[0], recv.at[0], to(beside))
        )
        self.first = []
        self.second = []
        for i in range(2):
            plane = self.far[i]
            self.first.append(
                (
                    at_end & has(plane),
                    remote(part(plane), over.at[i], send.at[1 + i], recv.at[1 + i], to(beside)),
                )
            )
            self.second.append(
                (
                    (1 - at_end.astype(jnp.int32) > 0) & has(plane),
                    remote(joint.at[i], last.at[1], send.at[3 + i], recv.at[3], to(plane)),
                )
            )

    def start(self):
        for flag, copy in (self.first[1], self.first[0], self.direct):

            @pl.when(flag)
            def _():
                copy.start()

    def relay(self):
        for i in (1, 0):
            flag, copy = self.second[i]

            @pl.when(flag)
            def _():
                self.first[i][1].wait_recv()
                value = self.part(self.far[i])[...].astype(full) + self.over[i].astype(full)
                self.joint[i] = value.astype(half)
                copy.start()

    def arrive(self):
        self.direct[1].wait_recv()
        self.second[0][1].wait_recv()
        return self.last[0].astype(full) + self.last[1].astype(full)

    def sent(self):
        for flag, copy in [self.direct] + self.first + self.second:

            @pl.when(flag)
            def _():
                copy.wait_send()


def turn(value, cosine, sine):
    lane = lax.broadcasted_iota(jnp.int32, (value.shape[0], 128), 1)
    first = lax.rem(lane, 64) < 32
    parts = []
    for i in range(value.shape[1] // 128):
        part = value[:, 128 * i : 128 * i + 128]
        swapped = jnp.where(first, pltpu.roll(part, 96, 1), pltpu.roll(part, 32, 1))
        parts.append(part * cosine + swapped * sine)
    return jnp.concatenate(parts, axis=1)


def turn_tables(base):
    lane = lax.broadcasted_iota(jnp.int32, (TB, 128), 1)
    place = (lax.broadcasted_iota(jnp.int32, (TB, 128), 0) + base).astype(full)
    power = lax.rem(lane, 32).astype(full) * (-2.0 / HD)
    angle = place * jnp.exp(power * LOG_BASE)
    sine = jnp.sin(angle)
    return jnp.cos(angle), jnp.where(lax.rem(lane, 64) < 32, -sine, sine)


def mask_bias(starts_ref, seq, base):
    keys = lax.broadcasted_iota(jnp.int32, (1, 1024), 1)
    rows = lax.broadcasted_iota(jnp.int32, (TB, 1), 0) + base
    key_id = jnp.zeros((1, 1024), jnp.int32)
    row_id = jnp.zeros((TB, 1), jnp.int32)
    for j in range(PIECES):
        first = starts_ref[seq, j]
        key_id = key_id + jnp.where((keys >= first) & (keys < first + PIECE), j + 1, 0)
        row_id = row_id + jnp.where((rows >= first) & (rows < first + PIECE), j + 1, 0)
    row_id = jnp.where(row_id == 0, -1, row_id)
    allowed = (keys <= rows) | (key_id == row_id)
    return jnp.where(allowed, 0.0, MASKED)


def forward_kernel(
    tok_ref, cot_ref, wq_ref, wkv_ref, wo_ref, wgu_ref, wd_ref, gains_ref, starts_ref,
    mid_hbm, q_hbm, kv_hbm, lse_hbm, out_hbm, wof_hbm, wi_hbm, n1_hbm, srow_hbm, sown_hbm,
    down_hbm, gm_hbm, att_hbm, gain_hbm, dwz_hbm, dwd_hbm,
    mid_ref, q_ref, kv_ref, lse_ref, out_ref, wof_ref, wi_ref, n1_ref, srow_ref, sown_ref,
    down_ref, gm_ref, att_all, gain_out, dwz, dwd_ref,
    gain2_src, cotall_ref, w_ref, all_ref, d_ref, wd, act, slope, swish, px_out, px_in, dwzd, zin,
    tempd, own_grad, b0, b1, b2, b3,
    wsrc, osrc, w3, blk, tile, tok_own, sums, gain_parts, kv_own, q_own, wo_all,
    hid, kvb0, kvb1, kvb2, kvb3, qb0, qb1, qb2, qb3,
    zq_s, zq_r, cq_s, cq_r, a_s, a_r, zo_s, zo_r, po_s, po_r, co_s, co_r, t_s, t_r, c_s, c_r,
    g_s, g_r, kp_s, kp_r, qp_s, qp_r, kv_s, kv_r, ck_s, ck_r, zt_s, zt_r, ct_s, ct_r, ss_s, ss_r,
    n_s, n_r, s_s, s_r, zd_s, zd_r, cd_s, cd_r, px_s, px_r, z_s, z_r, at_s, at_r, out_s,
):
    r = lax.axis_index("row")
    c = lax.axis_index("col")
    z = c // 2
    k = lax.rem(c, 2)
    oc = other_core(c)
    mates = [(mate(r, m), c) for m in (1, 2, 3)]
    aheads = [(r, z_ahead(c, m)) for m in (1, 2, 3)]
    core = (r, oc)
    ready = greet(mates + [core] + aheads)
    mine = slice_rows(r)
    sent = []

    def send(src, dst, send_sem, recv_sem, target):
        copy = remote(src, dst, send_sem, recv_sem, target)
        copy.start()
        sent.append(copy)
        return copy

    stores = []

    def store(src, dst):
        copy = pltpu.make_async_copy(src, dst, out_s.at[len(stores)])
        copy.start()
        stores.append(copy)

    joined = jnp.concatenate([wq_ref[...], wkv_ref[0], wkv_ref[1]], axis=0)
    wsrc[...] = jnp.transpose(joined).astype(half)
    blk[c] = wsrc[...]
    tokens = tok_ref[...].astype(full)
    sums[r] = jnp.broadcast_to(jnp.sum(tokens * tokens, axis=0, keepdims=True), (8, 512))
    gain2_src[...] = jnp.broadcast_to(gains_ref[1:2, :], (8, 288))
    ready()
    qz = [send(wsrc, blk.at[c], zq_s.at[m], zq_r.at[m], aheads[m]) for m in range(3)]
    q_core = [send(wsrc, blk.at[c], cq_s.at[3], cq_r.at[3], core)]
    sum_copies = [
        send(sums.at[r], sums.at[r], ss_s.at[m], ss_r.at[m], mates[m]) for m in range(3)
    ]
    tok_copies = [
        send(tok_ref.at[:, block_rows(mates[m][0])], tok_own.at[mine], t_s.at[m], t_r.at[m], mates[m])
        for m in range(3)
    ]
    gain_copies = [
        send(gain2_src, gain_parts.at[r], g_s.at[m], g_r.at[m], mates[m]) for m in range(3)
    ]
    for i in range(3):
        for t in range(3):
            src = wd_ref[...] if t == 2 else wgu_ref[t]
            w3[i, t] = src[:, 128 * i : 128 * i + 128].astype(half)
    tile_sends = []
    for m in range(3):
        b = mates[m][0]
        copy = remote(
            w3.at[tile_of(b, z)], tile.at[:, mine, :], a_s.at[m], a_r.at[m], mates[m]
        )
        tile_sends.append((has_tile(b, z, k), copy))

        @pl.when(has_tile(b, z, k))
        def _():
            copy.start()

    cotall_ref[mine, :] = cot_ref[...]
    cot_gather = Gather(lambda b, h: cotall_ref.at[slice_rows(b, h)], r, c, c_s, c_r)
    cot_gather.start()
    for j in range(3):
        osrc[:, 288 * j : 288 * j + 288] = wo_ref[48 * j : 48 * j + 48, :].astype(half)
    wo_all[r, z, k] = osrc[...]
    tok_own[mine, :] = tok_ref[:, block_rows(r)]
    gain_parts[r] = gain2_src[...]

    @pl.when(has_tile(r, z, k))
    def _():
        tile[:, mine, :] = w3[tile_of(r, z)]

    for copy in sum_copies:
        copy.wait_recv()
    scale_row = lax.rsqrt((sums[0] + sums[1] + sums[2] + sums[3]) / D + EPS)
    srow_ref[...] = scale_row
    gain1 = jnp.transpose(jnp.broadcast_to(gains_ref[0:1, :], (128, 288)))[:, 0:1]
    n1_ref[...] = (tokens * scale_row[0:1, :] * gain1).astype(half)
    cosine, sine = turn_tables(512 * k + TB * r)
    bias = mask_bias(starts_ref, z, 512 * k + TB * r)
    for m in range(3):
        src = lax.rem(c + 6 - 2 * m, 8)
        remote(wsrc, blk.at[src], zq_s.at[m], zq_r.at[m], core).wait_recv()
        q_core.append(send(blk.at[src], blk.at[src], cq_s.at[m], cq_r.at[m], core))
    oz = [send(osrc, wo_all.at[r, z, k], zo_s.at[m], zo_r.at[m], aheads[m]) for m in range(3)]
    gate_up = TileGather(
        tile.at[0:2],
        lambda slot: w_ref.at[:, :, tile_cols(slot)],
        r, c, zt_s, zt_r, ct_s, ct_r,
    )

    downs = TileGather(
        tile.at[2], lambda slot: wd.at[:, tile_cols(slot)], r, c, zd_s, zd_r, cd_s, cd_r
    )

    @pl.when(gate_up.has)
    def _():
        for m in range(3):
            src = slice_rows(mates[m][0])
            remote(w3.at[0], tile.at[:, src, :], a_s.at[m], a_r.at[m], mates[m]).wait_recv()
        gate_up.start()

    for m in range(3):
        src = lax.rem(oc + 6 - 2 * m, 8)
        remote(blk.at[src], blk.at[src], cq_s.at[m], cq_r.at[m], core).wait_recv()
    remote(wsrc, blk.at[oc], cq_s.at[3], cq_r.at[3], core).wait_recv()
    for i in range(8):
        wi_ref[:, 144 * i : 144 * i + 144] = blk[i, :, 0:144]
        wi_ref[:, 1152 + 48 * i : 1200 + 48 * i] = blk[i, :, 144:192]
        wi_ref[:, 1536 + 48 * i : 1584 + 48 * i] = blk[i, :, 192:240]
    store(wi_ref, wi_hbm)
    store(n1_ref, n1_hbm)
    store(srow_ref, srow_hbm)
    kv_scatter = Scatter(kvb0, kvb1, kvb2, kvb3, r, c, kp_s, kp_r)
    q_scatter = Scatter(qb0, qb1, qb2, qb3, r, c, qp_s, qp_r)
    for m in (2, 0, 1):
        part = n1_ref[:, block_rows(mates[m][0])]
        kvb0[m] = product_left(part, wi_ref[:, 1152:]).astype(half)
        kv_scatter.start(((0,), (1,), (2, 3))[m])
    cot_gather.relay()
    for m in (2, 0, 1):
        part = n1_ref[:, block_rows(mates[m][0])]
        qb0[m] = product_left(part, wi_ref[:, :1152]).astype(half)
    kv_scatter.relay()
    q_scatter.start()
    part = n1_ref[:, block_rows(r)]
    kv_own[...] = product_left(part, wi_ref[:, 1152:])
    q_own[...] = product_left(part, wi_ref[:, :1152])
    for m in range(3):
        src = slice_rows(mates[m][0])
        remote(
            tok_ref.at[:, block_rows(0)], tok_own.at[src], t_s.at[m], t_r.at[m], mates[m]
        ).wait_recv()
    hidden = jnp.transpose(tok_own[...].astype(full))
    hid[...] = hidden
    scale = lax.rsqrt(jnp.sum(hidden * hidden, axis=1, keepdims=True) / D + EPS)
    sown_ref[...] = jnp.broadcast_to(scale, (TB, 128))
    raw = kv_scatter.finish(kv_own).astype(half)
    my_block = block_rows(4 * k + r)
    kv_ref[my_block, 0:384] = turn(raw[:, 0:384].astype(full), cosine, sine).astype(half)
    kv_ref[my_block, 384:768] = raw[:, 384:768]
    kv_gather = Gather(lambda b, h: kv_ref.at[part_rows(4 * k + b, h)], r, c, kv_s, kv_r)
    kv_gather.start()

    def kv_core(j, b):
        rows = block_rows(4 * k + b)
        return send(kv_ref.at[rows], kv_ref.at[rows], ck_s.at[j], ck_r.at[j], core)

    kv_core(3, r)
    q_scatter.relay()
    for copy in oz:
        copy.wait_recv()
    wo_gather = Gather(
        lambda b, h: wo_all.at[b, :, k] if h is None else wo_all.at[b, 2 * h : 2 * h + 2, k],
        r, c, po_s, po_r,
    )
    kv_gather.relay()
    wo_gather.start()
    raw = q_scatter.finish(q_own).astype(half)
    queries = turn(raw.astype(full), cosine, sine).astype(half)
    q_ref[...] = queries
    queries = queries * jnp.bfloat16(0.125)
    for m in range(2):
        kv_core(m, mates[m][0])
    kv_gather.finish()
    kv_core(2, mates[2][0])
    for j in range(4):
        b = r if j == 3 else mates[j][0]
        rows = block_rows(4 * (1 - k) + b)
        remote(kv_ref.at[rows], kv_ref.at[rows], ck_s.at[j], ck_r.at[j], core).wait_recv()
    cot_gather.finish()
    def wo_swap(j, b):
        return send(wo_all.at[b, :, k], wo_all.at[b, :, k], co_s.at[j], co_r.at[j], core)

    store(kv_ref, kv_hbm)
    store(q_ref, q_hbm)
    store(sown_ref, sown_hbm)
    for g in range(KV_HEADS):
        if g == 3:

            @pl.when(downs.has)
            def _():
                downs.start()

        if g == 4:
            wo_swap(3, r)
            wo_gather.relay()
            wo_swap(0, mates[0][0])
            wo_swap(1, mates[1][0])
        keys = kv_ref[:, 64 * g : 64 * g + 64]
        values = kv_ref[:, 384 + 64 * g : 448 + 64 * g]
        heads = jnp.concatenate(
            [queries[:, 64 * h : 64 * h + 64] for h in range(3 * g, 3 * g + 3)], axis=0
        )
        scores = product_right(heads, keys).reshape(3, TB, 1024) + bias[None]
        high = jnp.max(scores, axis=-1, keepdims=True)
        weights = jnp.exp(scores - high)
        total = jnp.sum(weights, axis=-1, keepdims=True)
        probs = (weights * (1.0 / total)).astype(half).reshape(3 * TB, 1024)
        lse_ref[:, g : g + 1] = (high + jnp.log(total)).reshape(3 * TB, 1)
        output = product(probs, values)
        for j in range(3):
            h = 3 * g + j
            out_ref[:, 64 * h : 64 * h + 64] = output[TB * j : TB * j + TB]
    attended = out_ref[...].astype(half)
    store(lse_ref, lse_hbm)
    store(out_ref, out_hbm)
    gate_up.relay()

    wo_gather.finish()
    wo_swap(2, mates[2][0])
    for j in range(4):
        b = r if j == 3 else mates[j][0]
        remote(
            wo_all.at[b, :, 1 - k], wo_all.at[b, :, 1 - k], co_s.at[j], co_r.at[j], core
        ).wait_recv()
    for b in range(4):
        for i in range(4):
            for kk in range(2):
                for j in range(3):
                    row = 144 * (2 * i + kk) + 48 * j
                    wof_ref[row : row + 48, 288 * b : 288 * b + 288] = wo_all[
                        b, i, kk, :, 288 * j : 288 * j + 288
                    ]
    middle = hid[...] + product(attended, wof_ref[...])
    mid_ref[...] = middle
    store(wof_ref, wof_hbm)
    store(mid_ref, mid_hbm)
    for copy in gain_copies:
        copy.wait_recv()
    gain = jnp.concatenate([gain_parts[i] for i in range(4)], axis=1)
    scale_two = lax.rsqrt(jnp.sum(middle * middle, axis=1, keepdims=True) / D + EPS)
    my_rows = block_rows(r)
    all_ref[my_rows, :] = (middle * scale_two * gain[0:1, :]).astype(half)
    gather = Gather(lambda b, h: all_ref.at[part_rows(b, h)], r, c, n_s, n_r)
    scatter = Scatter(b0, b1, b2, b3, r, c, s_s, s_r)
    gather.start()

    @pl.when(gate_up.has)
    def _():
        cols = tile_cols(3 * k + tile_place(r, k, z))
        w_ref[:, :, cols] = tile[0:2]
        wd[:, cols] = tile[2]

    att_all[my_rows, :] = attended
    gate_up.finish()

    def up_to(b):
        rows = block_rows(b)
        normed = all_ref[rows, :]
        for j in range(3):
            cs = slice(256 * j, 256 * j + 256)
            gate = product(normed, w_ref[0, :, cs])
            up = product(normed, w_ref[1, :, cs])
            sigma = 1.0 / (1.0 + jnp.exp(-gate))
            hidden = gate * sigma
            act[rows, cs] = (hidden * up).astype(half)
            swish[rows, cs] = hidden
            slope[rows, cs] = up * (sigma * (1.0 + gate * (1.0 - sigma)))

    up_to(r)
    gather.relay()
    up_to(mates[0][0])
    up_to(mates[1][0])
    downs.relay()
    gather.finish()
    att_gather = Gather(lambda b, h: att_all.at[part_rows(b, h)], r, c, at_s, at_r)
    att_gather.start()
    up_to(mates[2][0])

    def tile_grads(t, core_index):
        cols = pl.ds(pl.multiple_of(384 * core_index, 128), 384)
        if t == 2:
            return product(cotall_ref[...], act[:, cols])
        return product_left(all_ref[...], d_ref[t, :, cols])

    px_copies = {}

    def to_other_core(t):
        part = tile_grads(t, 1 - k)
        for j in range(3):
            px_out[t, j] = part[:, 128 * j : 128 * j + 128].astype(half)
        px_copies[t] = send(px_out.at[t], px_in.at[t], px_s.at[t], px_r.at[t], core)

    downs.finish()

    def back(b):
        rows = block_rows(b)
        cot = cotall_ref[:, rows]
        for j in range(3):
            cs = slice(256 * j, 256 * j + 256)
            grad = product_left(cot, wd[:, cs])
            d_ref[0, rows, cs] = (grad * slope[rows, cs]).astype(half)
            d_ref[1, rows, cs] = (grad * swish[rows, cs]).astype(half)
        return product_right(d_ref[0, rows, :], w_ref[0]) + product_right(
            d_ref[1, rows, :], w_ref[1]
        )

    to_other_core(2)
    b0[2] = back(mates[2][0]).astype(half)
    scatter.start((2, 3))
    b0[0] = back(mates[0][0]).astype(half)
    scatter.start((0,))
    part = tile_grads(2, k)
    px_copies[2].wait_recv()
    for j in range(3):
        value = part[:, 128 * j : 128 * j + 128] + px_in[2, j].astype(full)
        tempd[j] = value
        dwzd[j] = value.astype(half)
    z_sends = []
    for m in range(3):
        ahead = lax.rem(z + m + 1, 4)
        place = tile_place(r, k, ahead)
        copy = remote(dwzd.at[place], zin.at[m], z_s.at[m], z_r.at[m], aheads[m])
        flag = has_tile(r, ahead, k)
        z_sends.append((flag, copy))

        @pl.when(flag)
        def _():
            copy.start()

    b0[1] = back(mates[1][0]).astype(half)
    scatter.start((1,))
    own_grad[...] = back(r)
    scatter.relay()
    att_gather.relay()
    to_other_core(0)
    to_other_core(1)
    for i in range(2):
        rows = slice(256 * i, 256 * i + 256)
        down_ref[rows, :] = product_right(act[rows, :], wd[...]).astype(half)
    store(down_ref, down_hbm)
    scale = scale_two
    cot = jnp.transpose(cotall_ref[:, my_rows].astype(full))
    hidden = mid_ref[...]
    grad = scatter.finish(own_grad)
    inner = jnp.sum(grad * gain[0:1, :] * hidden, axis=1, keepdims=True)
    gm = cot + grad * gain[0:1, :] * scale - hidden * (scale * scale * scale * inner / D)
    gm_ref[...] = gm.astype(half)
    store(gm_ref, gm_hbm)
    gain_out[...] = jnp.broadcast_to(
        jnp.sum(grad * hidden * scale, axis=0, keepdims=True), gain_out.shape
    )
    for t in range(2):
        part = tile_grads(t, k)
        px_copies[t].wait_recv()
        for j in range(3):
            value = part[:, 128 * j : 128 * j + 128] + px_in[t, j].astype(full)
            dwz[t, j] = value.astype(half)
    store(gain_out, gain_hbm)
    store(dwz, dwz_hbm)
    att_gather.finish()
    store(att_all, att_hbm)

    dwd_ref[...] = jnp.zeros_like(dwd_ref)

    @pl.when(downs.has)
    def _():
        value = tempd[tile_place(r, k, z)]
        for m in range(3):
            remote(dwzd.at[0], zin.at[m], z_s.at[m], z_r.at[m], aheads[m]).wait_recv()
            value = value + zin[m].astype(full)
        dwd_ref[...] = value

    store(dwd_ref, dwd_hbm)
    for copy in sent:
        copy.wait_send()
    for part in (
        cot_gather, kv_gather, wo_gather, gate_up, kv_scatter, q_scatter, downs, gather, scatter,
        att_gather,
    ):
        part.sent()
    for copy in stores:
        copy.wait()
    for flag, copy in tile_sends + z_sends:

        @pl.when(flag)
        def _():
            copy.wait_send()


def forward(*args):
    shape = jax.ShapeDtypeStruct
    v = pltpu.VMEM
    sems = []
    counts = (3, 6, 3, 3, 6, 6, 3, 6, 3, 6, 6, 6, 6, 3, 6, 3, 6, 6, 3, 6, 3, 3, 6)
    for count in counts:
        sems += [pltpu.SemaphoreType.DMA((count,))] * 2
    return pl.pallas_call(
        forward_kernel,
        out_shape=(
            shape((TB, D), full),
            shape((TB, D), half),
            shape((1024, 768), half),
            shape((3 * TB, 128), full),
            shape((TB, D), full),
            shape((D, D), half),
            shape((288, 1920), half),
            shape((288, 512), half),
            shape((8, 512), full),
            shape((TB, 128), full),
            shape((512, D), half),
            shape((TB, D), half),
            shape((512, D), half),
            shape((8, D), full),
            shape((2, 3, D, 128), half),
            shape((D, 128), full),
        ),
        in_specs=[VM] * 8 + [SM],
        out_specs=(pl.BlockSpec(memory_space=pl.ANY),) * 16,
        scratch_shapes=[
            v((TB, D), full),
            v((TB, D), half),
            v((1024, 768), half),
            v((3 * TB, 128), full),
            v((TB, D), full),
            v((D, D), half),
            v((288, 1920), half),
            v((288, 512), half),
            v((8, 512), full),
            v((TB, 128), full),
            v((512, D), half),
            v((TB, D), half),
            v((512, D), half),
            v((8, D), full),
            v((2, 3, D, 128), half),
            v((D, 128), full),
            v((8, 288), full),
            v((D, 512), half),
            v((2, D, 768), half),
            v((512, D), half),
            v((2, 512, 768), half),
            v((D, 768), half),
            v((512, 768), half),
            v((512, 768), full),
            v((512, 768), full),
            v((3, 3, D, 128), half),
            v((3, 3, D, 128), half),
            v((3, D, 128), half),
            v((3, D, 128), half),
            v((3, D, 128), full),
            v((TB, D), full),
        ]
        + scatter_buffers(D)
        + [
            v((288, 240), half),
            v((48, 864), half),
            v((3, 3, 288, 128), half),
            v((8, 288, 240), half),
            v((3, D, 128), half),
            v((D, TB), half),
            v((4, 8, 512), full),
            v((4, 8, 288), full),
            v((TB, 768), full),
            v((TB, D), full),
            v((4, 4, 2, 48, 864), half),
            v((TB, D), full),
        ]
        + scatter_buffers(768)
        + scatter_buffers(D)
        + sems
        + [pltpu.SemaphoreType.DMA((16,))],
        compiler_params=pltpu.CompilerParams(
            collective_id=1, has_side_effects=True, vmem_limit_bytes=60 << 20
        ),
    )(*args)


def back_kernel(
    mid_in, q_in, kv_in, lse_in, out_in, wof_in, wi_in, n1_in, srow_in, sown_in, down_in, gm_in,
    att_in, gain2_in, dwz_in, dwd_in, tok_ref, gains_in, starts_ref,
    bo_ref, ig_ref, dw_ref, dq_ref, do_ref, gains_ref,
    mid_ref, q_ref, kv_ref, lse_ref, out_ref, wof_ref, wi_ref, n1_ref, srow_ref, sown_ref,
    down_ref, gm_ref, att_all, gain2_ref, dwz, dwd_ref,
    gm_out, gm_nat, bo_out, z_over, z_joint, z_last, tile_out, dkv, dkv_co, dkv_ci, sdq, sdk, dqs, dwq, dwq_co, dwq_ci, dwq_z,
    dwq_over, dwq_joint, dwq_in,
    dwk, dwk_co, dwk_ci, dwk_z, dwk_in,
    dwo, dwo_co, dwo_ci, dwo_z, dwo_over, dwo_joint, dwo_in, g2_out, g2_in, gl, gl_ci, gl_z, gl_in, coef_all, dn_own,
    n0, n1, n2, n3, e0, e1, e2, e3,
    dn_s, dn_r, bo_s, bo_r, z_s, z_r, t_s, t_r, kc_s, kc_r, kp_s, kp_r, sd_s, sd_r, sk_s, sk_r,
    qc_s, qc_r, qz_s, qz_r, kk_s, kk_r, kz_s, kz_r, oc_s, oc_r, oz_s, oz_r, g2_s, g2_r, gc_s, gc_r,
    gz_s, gz_r, cf_s, cf_r, gm_s, gm_r, in_s,
):
    r = lax.axis_index("row")
    c = lax.axis_index("col")
    z = c // 2
    k = lax.rem(c, 2)
    mates = [(mate(r, m), c) for m in (1, 2, 3)]
    aheads = [(r, z_ahead(c, m)) for m in (1, 2, 3)]
    ahead_z = [lax.rem(z + m, 4) for m in (1, 2, 3)]
    core = (r, other_core(c))
    ready = greet(mates + [core] + aheads)
    loads = {}
    order = (
        ("dwz", dwz_in, dwz), ("gm", gm_in, gm_ref), ("gain2", gain2_in, gain2_ref),
        ("dwd", dwd_in, dwd_ref), ("down", down_in, down_ref), ("wof", wof_in, wof_ref),
        ("q", q_in, q_ref), ("kv", kv_in, kv_ref), ("lse", lse_in, lse_ref),
        ("out", out_in, out_ref), ("att", att_in, att_all), ("n1", n1_in, n1_ref),
        ("wi", wi_in, wi_ref), ("sown", sown_in, sown_ref), ("srow", srow_in, srow_ref),
        ("mid", mid_in, mid_ref),
    )
    for i, (name, src, dst) in enumerate(order):
        loads[name] = pltpu.make_async_copy(src, dst, in_s.at[i])
        loads[name].start()
    mine = block_rows(r)
    sent = []

    def send(src, dst, send_sem, recv_sem, target):
        copy = remote(src, dst, send_sem, recv_sem, target)
        copy.start()
        sent.append(copy)
        return copy

    loads["gm"].wait()
    loads["gain2"].wait()
    for i in range(4):
        g2_out[i] = gain2_ref[:, 288 * i : 288 * i + 288]
    turned = jnp.transpose(gm_ref[...].astype(full)).astype(half)
    for i in range(4):
        gm_out[i] = turned[288 * i : 288 * i + 288]
    gm_nat[:, mine] = gm_out[r]
    loads["down"].wait()
    for m in range(3):
        n0[m] = down_ref[block_rows(mates[m][0]), :]
    mine_has = has_tile(r, z, k)
    my_place = tile_place(r, k, z)
    ready()
    loads["dwz"].wait()
    tile_sums = [
        PlaneSum(
            lambda plane, t=t: dwz.at[t, tile_place(r, k, plane)],
            z_over.at[t], z_joint.at[t], z_last.at[t], r, c, z_s.at[t], z_r.at[t],
            lambda plane: has_tile(r, plane, k),
        )
        for t in range(2)
    ]
    tile_sums[0].start()
    gm_copies = [
        send(gm_out.at[mates[m][0]], gm_nat.at[:, mine], gm_s.at[m], gm_r.at[m], mates[m])
        for m in range(3)
    ]

    def tile_copy(t, m):
        return remote(
            tile_out.at[mates[m][0], t],
            dw_ref.at[tile_of(r, z), t],
            t_s.at[3 * t + m],
            t_r.at[3 * t + m],
            mates[m],
        )

    def tile_back(t):
        @pl.when(mine_has)
        def _():
            value = dwd_ref[...] if t == 2 else dwz[t, my_place].astype(full)
            if t < 2:
                value = value + tile_sums[t].arrive()
            for b in range(4):
                tile_out[b, t] = value[288 * b : 288 * b + 288].astype(half)
            for m in range(3):
                tile_copy(t, m).start()
            dw_ref[tile_of(r, z), t] = tile_out[r, t]

    downs = Scatter(n0, n1, n2, n3, r, c, dn_s, dn_r)
    downs.start()
    g2_copies = [
        send(g2_out.at[mates[m][0]], g2_in.at[m], g2_s.at[m], g2_r.at[m], mates[m])
        for m in range(3)
    ]
    loads["wof"].wait()
    ga = product_right(gm_ref[...], wof_ref[...]).astype(half)
    gaf = ga.astype(full)
    loads["q"].wait()
    queries = q_ref[...] * jnp.bfloat16(0.125)
    cosine, sine = turn_tables(512 * k + TB * r)
    sine = -sine
    bias = mask_bias(starts_ref, z, 512 * k + TB * r)
    loads["kv"].wait()
    loads["lse"].wait()
    loads["out"].wait()
    for g in range(KV_HEADS):
        keys = kv_ref[:, 64 * g : 64 * g + 64]
        values = kv_ref[:, 384 + 64 * g : 448 + 64 * g]
        heads = range(3 * g, 3 * g + 3)
        qh = jnp.concatenate([queries[:, 64 * h : 64 * h + 64] for h in heads], axis=0)
        gh = jnp.concatenate([ga[:, 64 * h : 64 * h + 64] for h in heads], axis=0)
        delta = jnp.concatenate(
            [
                jnp.sum(
                    gaf[:, 64 * h : 64 * h + 64] * out_ref[:, 64 * h : 64 * h + 64],
                    axis=1,
                    keepdims=True,
                )
                for h in heads
            ],
            axis=0,
        )
        scores = product_right(qh, keys).reshape(3, TB, 1024) + bias[None]
        probs = jnp.exp(scores.reshape(3 * TB, 1024) - lse_ref[:, g : g + 1])
        grad_probs = product_right(gh, values)
        grad_scores = (probs * (grad_probs - delta)).astype(half)
        grad_q = product(grad_scores, keys) * 0.125
        for j in range(3):
            h = 3 * g + j
            dqs[:, 64 * h : 64 * h + 64] = grad_q[TB * j : TB * j + TB]
        dkv[:, 64 * g : 64 * g + 64] = product_left(grad_scores, qh)
        dkv[:, 384 + 64 * g : 448 + 64 * g] = product_left(probs.astype(half), gh)
    other_rows = pl.ds(pl.multiple_of(512 * (1 - k), 512), 512)
    dkv_co[...] = dkv[other_rows, :].astype(half)
    kc = send(dkv_co, dkv_ci, kc_s.at[0], kc_r.at[0], core)
    grad_q = dqs[...]
    inner = jnp.sum(grad_q * q_ref[...].astype(full), axis=1, keepdims=True)
    sdq[mine, :] = turn(grad_q, cosine, sine).astype(half)
    q_gather = Gather(lambda b, h: sdq.at[part_rows(b, h)], r, c, sd_s, sd_r)
    q_gather.start()
    tile_sums[0].relay()
    tile_sums[1].start()
    kc.wait_recv()
    pairs = Scatter(e0, e1, e2, e3, r, c, kp_s, kp_r)
    for m in (2, 0, 1):
        b = mates[m][0]
        e0[m] = (dkv[block_rows(4 * k + b), :] + dkv_ci[block_rows(b), :].astype(full)).astype(half)
        pairs.start(((0,), (1,), (2, 3))[m])
    my_block = block_rows(4 * k + r)
    dkv[my_block, :] = dkv[my_block, :] + dkv_ci[mine, :].astype(full)
    for m in range(3):
        cols = block_rows(mates[m][0])
        remote(gm_out.at[0], gm_nat.at[:, cols], gm_s.at[m], gm_r.at[m], mates[m]).wait_recv()
    loads["att"].wait()
    grad_wo = lax.dot_general(
        att_all[...], gm_nat[...], (((0,), (1,)), ((), ())), preferred_element_type=full
    )
    for i in range(8):
        dwo[i] = grad_wo[144 * i : 144 * i + 144]

    def wide(value):
        n = value.shape[0] // 3
        return jnp.concatenate([value[n * j : n * j + n] for j in range(3)], axis=1)

    def tall(value):
        n = value.shape[1] // 3
        return jnp.concatenate([value[:, n * j : n * j + n] for j in range(3)], axis=0)

    for i in range(4):
        dwo_co[i] = dwo[2 * i + 1 - k].astype(half)
    oc_copy = send(dwo_co, dwo_ci, oc_s.at[0], oc_r.at[0], core)
    pairs.relay()
    q_gather.relay()
    tile_sums[1].relay()
    downs.relay()
    oc_copy.wait_recv()
    for i in range(4):
        value = dwo[2 * i + k] + dwo_ci[i].astype(full)
        dwo_z[i] = wide(value).astype(half)
        dwo[2 * i + k] = value
    o_sum = PlaneSum(lambda plane: dwo_z.at[plane], dwo_over, dwo_joint, dwo_in, r, c, oz_s, oz_r)
    o_sum.start()
    grad_kv = pairs.finish(dkv[my_block, :])
    sdk[mine, 0:384] = turn(grad_kv[:, 0:384], cosine, sine).astype(half)
    sdk[mine, 384:768] = grad_kv[:, 384:768].astype(half)
    k_gather = Gather(lambda b, h: sdk.at[part_rows(b, h)], r, c, sk_s, sk_r)
    k_gather.start()
    inner = inner + jnp.sum(grad_kv * kv_ref[my_block, :].astype(full), axis=1, keepdims=True)
    loads["sown"].wait()
    scale = sown_ref[...]
    coef = jnp.transpose(inner * (scale * scale) / D)
    coef_all[r] = coef[0:8]
    coef_copies = [
        send(coef_all.at[r], coef_all.at[r], cf_s.at[m], cf_r.at[m], mates[m]) for m in range(3)
    ]
    o_sum.relay()
    loads["n1"].wait()
    q_gather.finish()
    grad_wi = product(n1_ref[...], sdq[...])
    for i in range(8):
        dwq[i] = grad_wi[:, 144 * i : 144 * i + 144]
    for i in range(4):
        dwq_co[i] = dwq[2 * i + 1 - k].astype(half)
    qc_copy = send(dwq_co, dwq_ci, qc_s.at[0], qc_r.at[0], core)
    k_gather.relay()
    loads["dwd"].wait()
    tile_back(2)
    tile_back(0)
    qc_copy.wait_recv()
    for i in range(4):
        value = dwq[2 * i + k] + dwq_ci[i].astype(full)
        dwq_z[i] = wide(value).astype(half)
        dwq[2 * i + k] = value
    q_sum = PlaneSum(lambda plane: dwq_z.at[plane], dwq_over, dwq_joint, dwq_in, r, c, qz_s, qz_r)
    q_sum.start()
    loads["wi"].wait()
    back = product_right(wi_ref[:, 0:1152], sdq[...])
    k_gather.finish()
    grad_wi = product(n1_ref[...], sdk[...])
    for i in range(8):
        dwk[i, :, 0:48] = grad_wi[:, 48 * i : 48 * i + 48]
        dwk[i, :, 48:96] = grad_wi[:, 384 + 48 * i : 432 + 48 * i]
    for i in range(4):
        dwk_co[i] = dwk[2 * i + 1 - k].astype(half)
    kk_copy = send(dwk_co, dwk_ci, kk_s.at[0], kk_r.at[0], core)
    loads["srow"].wait()
    back = (back + product_right(wi_ref[:, 1152:1920], sdk[...])) * srow_ref[0:1, :]
    kk_copy.wait_recv()
    for i in range(4):
        value = dwk[2 * i + k] + dwk_ci[i].astype(full)
        dwk_z[i] = value.astype(half)
        dwk[2 * i + k] = value
    kz_copies = [
        send(dwk_z.at[ahead_z[m]], dwk_in.at[m], kz_s.at[m], kz_r.at[m], aheads[m])
        for m in range(3)
    ]
    q_sum.relay()
    tile_back(1)
    loads["mid"].wait()
    dn_own[...] = mid_ref[...] + down_ref[mine, :].astype(full)
    result = downs.finish(dn_own)
    result = jnp.transpose(result).astype(half)
    for i in range(4):
        bo_out[i] = result[288 * i : 288 * i + 288]
    bo_ref[:, mine] = bo_out[r]
    bo_copies = [
        send(bo_out.at[mates[m][0]], bo_ref.at[:, mine], bo_s.at[m], bo_r.at[m], mates[m])
        for m in range(3)
    ]
    for m in range(3):
        b = mates[m][0]
        remote(coef_all.at[b], coef_all.at[b], cf_s.at[m], cf_r.at[m], mates[m]).wait_recv()
    coef = jnp.concatenate([coef_all[i] for i in range(4)], axis=1)[0:1, :]
    tokens = tok_ref[...].astype(full)
    gain1 = jnp.transpose(jnp.broadcast_to(gains_in[0:1, :], (128, 288)))[:, 0:1]
    ig_ref[...] = (gm_nat[...].astype(full) + back * gain1 - tokens * coef).astype(half)
    for copy in g2_copies:
        copy.wait_recv()
    column = jnp.sum(back * tokens, axis=1, keepdims=True)
    gl[0] = jnp.transpose(jnp.broadcast_to(column, (288, 128)))[0:8]
    gl[1] = g2_out[r] + g2_in[0] + g2_in[1] + g2_in[2]
    gc_copy = send(gl, gl_ci, gc_s.at[0], gc_r.at[0], core)
    gc_copy.wait_recv()
    gl_z[...] = gl[...] + gl_ci[...]
    gz_copies = [send(gl_z, gl_in.at[m], gz_s.at[m], gz_r.at[m], aheads[m]) for m in range(3)]
    total = dwo[2 * z + k] + tall(o_sum.arrive())
    do_ref[...] = total
    for m in range(3):
        cols = block_rows(mates[m][0])
        remote(bo_out.at[0], bo_ref.at[:, cols], bo_s.at[m], bo_r.at[m], mates[m]).wait_recv()
    for m in range(3):
        b = mates[m][0]

        @pl.when(has_tile(b, z, k))
        def _():
            for t in range(3):
                remote(
                    tile_out.at[0, t],
                    dw_ref.at[tile_of(b, z), t],
                    t_s.at[3 * t + m],
                    t_r.at[3 * t + m],
                    mates[m],
                ).wait_recv()

    total = dwq[2 * z + k] + tall(q_sum.arrive())
    dq_ref[:, 0:144] = total
    total = dwk[2 * z + k]
    for m in range(3):
        kz_copies[m].wait_recv()
        total = total + dwk_in[m].astype(full)
    dq_ref[:, 144:240] = total
    total = gl_z[...]
    for m in range(3):
        gz_copies[m].wait_recv()
        total = total + gl_in[m]
    gains_ref[...] = total
    for copy in sent:
        copy.wait_send()
    for part in (downs, pairs, q_gather, k_gather, o_sum, q_sum, *tile_sums):
        part.sent()
    @pl.when(mine_has)
    def _():
        for t in range(3):
            for m in range(3):
                tile_copy(t, m).wait_send()


def back(*args):
    shape = jax.ShapeDtypeStruct
    sems = []
    for count in (6, 3, (2, 5), 9, 1, 6, 6, 6, 1, 5, 1, 3, 1, 5, 3, 1, 3, 3, 3):
        count = count if isinstance(count, tuple) else (count,)
        sems += [pltpu.SemaphoreType.DMA(count)] * 2
    v = pltpu.VMEM
    return pl.pallas_call(
        back_kernel,
        out_shape=(
            shape((288, 512), half),
            shape((288, 512), half),
            shape((3, 3, 288, 128), half),
            shape((288, 240), full),
            shape((144, 288), full),
            shape((2, 8, 288), full),
        ),
        in_specs=[pl.BlockSpec(memory_space=pl.ANY)] * 16 + [VM] * 2 + [SM],
        out_specs=(VM,) * 6,
        scratch_shapes=[
            v((TB, D), full),
            v((TB, D), half),
            v((1024, 768), half),
            v((3 * TB, 128), full),
            v((TB, D), full),
            v((D, D), half),
            v((288, 1920), half),
            v((288, 512), half),
            v((8, 512), full),
            v((TB, 128), full),
            v((512, D), half),
            v((TB, D), half),
            v((512, D), half),
            v((8, D), full),
            v((2, 3, D, 128), half),
            v((D, 128), full),
            v((4, 288, TB), half),
            v((288, 512), half),
            v((4, 288, TB), half),
            v((2, 2, D, 128), half),
            v((2, 2, D, 128), half),
            v((2, 2, D, 128), half),
            v((4, 3, 288, 128), half),
            v((1024, 768), full),
            v((512, 768), half),
            v((512, 768), half),
            v((512, D), half),
            v((512, 768), half),
            v((TB, D), full),
            v((8, 288, 144), full),
            v((4, 288, 144), half),
            v((4, 288, 144), half),
            v((4, 96, 432), half),
            v((2, 96, 432), half),
            v((2, 96, 432), half),
            v((2, 96, 432), half),
            v((8, 288, 96), full),
            v((4, 288, 96), half),
            v((4, 288, 96), half),
            v((4, 288, 96), half),
            v((3, 288, 96), half),
            v((8, 144, 288), full),
            v((4, 144, 288), half),
            v((4, 144, 288), half),
            v((4, 48, 864), half),
            v((2, 48, 864), half),
            v((2, 48, 864), half),
            v((2, 48, 864), half),
            v((4, 8, 288), full),
            v((3, 8, 288), full),
            v((2, 8, 288), full),
            v((2, 8, 288), full),
            v((2, 8, 288), full),
            v((3, 2, 8, 288), full),
            v((4, 8, TB), full),
            v((TB, D), full),
        ]
        + scatter_buffers(D)
        + scatter_buffers(768)
        + sems
        + [pltpu.SemaphoreType.DMA((16,))],
        compiler_params=pltpu.CompilerParams(
            collective_id=3, has_side_effects=True, vmem_limit_bytes=60 << 20
        ),
    )(*args)


SETS = (("gu", (2, 288, 384)), ("d", (288, 384)), ("o", (144, 288)), ("q", (144, 288)),
        ("kv", (2, 48, 288)), ("g", (2, 288)))


def update_kernel(*refs):
    grads, refs = refs[:6], refs[6:]
    ins, refs = refs[:18], refs[18:]
    acts, refs = refs[:2], refs[2:]
    outs, refs = refs[:23], refs[23:]
    grad_v, refs = refs[:6], refs[6:]
    in_v, refs = refs[:18], refs[18:]
    out_v, refs = refs[:23], refs[23:]
    grad_s, in_s, out_s = refs
    loads = []
    for n in range(6):
        for i in range(3):
            j = 3 * n + i
            loads.append(pltpu.make_async_copy(ins[j], in_v[j], in_s.at[j]))
    grad_loads = [pltpu.make_async_copy(grads[i], grad_v[i], grad_s.at[i]) for i in range(6)]
    grad_loads[2].start()
    for copy in loads[:6]:
        copy.start()
    for i in (4, 3, 5, 0, 1):
        grad_loads[i].start()
    for copy in loads[6:]:
        copy.start()
    stores = []

    def store(src, dst):
        copy = pltpu.make_async_copy(src, dst, out_s.at[len(stores)])
        copy.start()
        stores.append(copy)

    fix = 1.0 - BETA**STEP

    def step(n, at, grad, rate, decay):
        weight = in_v[3 * n][at]
        first = BETA * in_v[3 * n + 1][at] + (1.0 - BETA) * grad
        second = BETA * in_v[3 * n + 2][at] + (1.0 - BETA) * grad * grad
        change = first / fix / (jnp.sqrt(second / fix) + TINY)
        weight = weight - rate * (change + decay * weight)
        out_v[4 * n][at] = first
        out_v[4 * n + 1][at] = second
        out_v[4 * n + 2][at] = weight
        if n < 5:
            out_v[4 * n + 3][at] = weight.astype(half)

    def ready(n):
        for copy in loads[3 * n : 3 * n + 3]:
            copy.wait()

    def done(n, at=None):
        for j in range(4 * n, min(4 * n + 4, 23)):
            if at is None:
                store(out_v[j], outs[j])
            else:
                store(out_v[j].at[at], outs[j].at[at])

    rate = D**-0.5
    every = (slice(None), slice(None))
    cols = [(slice(None), slice(128 * i, 128 * i + 128)) for i in range(3)]
    dw, dq, do, dg = grad_v[2:]
    grad_loads[2].wait()
    ready(0)
    for t in range(2):
        for i in range(3):
            step(0, (t,) + cols[i], dw[i, t].astype(full), rate, DECAY)
        done(0, t)
    ready(1)
    for i in range(3):
        step(1, cols[i], dw[i, 2].astype(full), FF**-0.5, DECAY)
    done(1)
    grad_loads[4].wait()
    ready(2)
    step(2, every, do[...], rate, DECAY)
    done(2)
    grad_loads[3].wait()
    ready(3)
    turned = jnp.transpose(dq[...])
    step(3, every, turned[0:144], rate, DECAY)
    done(3)
    ready(4)
    for t in range(2):
        step(4, (t, slice(None), slice(None)), turned[144 + 48 * t : 192 + 48 * t], rate, DECAY)
    done(4)
    grad_loads[5].wait()
    ready(5)
    step(5, every, jnp.concatenate([dg[0, 0:1], dg[1, 0:1]], axis=0), 0.25, 0.0)
    done(5)
    for i in range(2):
        grad_loads[i].wait()
        store(grad_v[i], acts[i])
    for copy in stores:
        copy.wait()


def update(grads, params):
    shape = jax.ShapeDtypeStruct
    v = pltpu.VMEM
    outs = []
    for name, dims in SETS:
        outs += [shape(dims, full)] * 3
        if name != "g":
            outs.append(shape(dims, half))
    acts = [shape((288, 512), half)] * 2
    hbm = pl.BlockSpec(memory_space=pl.ANY)
    result = pl.pallas_call(
        update_kernel,
        out_shape=tuple(acts + outs),
        in_specs=[hbm] * 24,
        out_specs=(hbm,) * 25,
        scratch_shapes=[v(g.shape, g.dtype) for g in grads]
        + [v(dims, full) for name, dims in SETS for i in range(3)]
        + [v(o.shape, o.dtype) for o in outs]
        + [
            pltpu.SemaphoreType.DMA((6,)),
            pltpu.SemaphoreType.DMA((18,)),
            pltpu.SemaphoreType.DMA((32,)),
        ],
        compiler_params=pltpu.CompilerParams(vmem_limit_bytes=60 << 20),
    )(*grads, *params)
    gu, d, o, q, kv, g = (result[2 + 4 * n : 6 + 4 * n] for n in range(6))
    return (*result[:2], *g, *q, *kv, *o, *gu, *d)


def swap(value):
    return jnp.swapaxes(value, -1, -2)


def local_fast(
    tokens,
    cotangent,
    starts,
    gains,
    gains_m,
    gains_v,
    w_query,
    w_query_m,
    w_query_v,
    w_keyval,
    w_keyval_m,
    w_keyval_v,
    w_output,
    w_output_m,
    w_output_v,
    w_gateup,
    w_gateup_m,
    w_gateup_v,
    w_down,
    w_down_m,
    w_down_v,
):
    tok = swap(tokens)
    kept = forward(
        tok, swap(cotangent), swap(w_query), swap(w_keyval), w_output, w_gateup, swap(w_down),
        gains, starts
    )
    grads = back(*kept, tok, gains, starts)
    params = []
    for group in (
        (w_gateup, w_gateup_m, w_gateup_v),
        (swap(w_down), swap(w_down_m), swap(w_down_v)),
        (w_output, w_output_m, w_output_v),
        (swap(w_query), swap(w_query_m), swap(w_query_v)),
        (swap(w_keyval), swap(w_keyval_m), swap(w_keyval_v)),
        (gains, gains_m, gains_v),
    ):
        params += group
    outs = update(grads, params)
    turned = (0, 1, 5, 6, 7, 8, 9, 10, 11, 12, 21, 22, 23, 24)
    return tuple(swap(value) if i in turned else value for i, value in enumerate(outs))


def local(tokens, *others):
    fits = lax.axis_size("row") == 4 and lax.axis_size("col") == 8 and tokens.shape == (512, 288)
    plan = local_fast if fits else local_general
    return plan(tokens, *others)


def solution(mesh):
    return jax.shard_map(
        local,
        mesh=mesh,
        in_specs=(
            P("col", "row"),
            P("col", "row"),
            P(),
            P(None, "row"),
            P(None, "row"),
            P(None, "row"),
            P("row", "col"),
            P("row", "col"),
            P("row", "col"),
            P(None, "row", "col"),
            P(None, "row", "col"),
            P(None, "row", "col"),
            P("col", "row"),
            P("col", "row"),
            P("col", "row"),
            P(None, "row", "col"),
            P(None, "row", "col"),
            P(None, "row", "col"),
            P("col", "row"),
            P("col", "row"),
            P("col", "row"),
        ),
        out_specs=(
            P("col", "row"),
            P("col", "row"),
            P(None, "row"),
            P(None, "row"),
            P(None, "row"),
            P("row", "col"),
            P("row", "col"),
            P("row", "col"),
            P("row", "col"),
            P(None, "row", "col"),
            P(None, "row", "col"),
            P(None, "row", "col"),
            P(None, "row", "col"),
            P("col", "row"),
            P("col", "row"),
            P("col", "row"),
            P("col", "row"),
            P(None, "row", "col"),
            P(None, "row", "col"),
            P(None, "row", "col"),
            P(None, "row", "col"),
            P("col", "row"),
            P("col", "row"),
            P("col", "row"),
            P("col", "row"),
        ),
        check_vma=False,
    )
```

```python
import jax
import jax.numpy as jnp
from jax import lax
from jax.experimental import pallas as pl
from jax.experimental.pallas import tpu as pltpu
from jax.sharding import PartitionSpec as P

D = 1152
HEADS = 18
KV_HEADS = 6
HD = 64
FF = 3072
TD = 128
PIECE = 256
PIECES = 4
STEP = 7


EPS = 1e-05
BETA = 0.5
TINY = 1e-08
DECAY = 0.1
MASKED = -1e30


def to_half(value):
    return value.astype(jnp.bfloat16)


def product(left, right):
    return jnp.dot(left, right, preferred_element_type=jnp.float32)


def product_left(left, right):
    return lax.dot_general(
        left, right, (((0,), (0,)), ((), ())), preferred_element_type=jnp.float32
    )


def product_right(left, right):
    return lax.dot_general(
        left, right, (((1,), (1,)), ((), ())), preferred_element_type=jnp.float32
    )


def col_collect(value):
    return lax.all_gather(value, "col", axis=0, tiled=True)


def row_collect(value):
    return lax.all_gather(value, "row", axis=0, tiled=True)


def row_reduce(value):
    return lax.psum_scatter(value, "row", scatter_dimension=0, tiled=True)


def col_reduce(value):
    return lax.psum_scatter(value, "col", scatter_dimension=0, tiled=True)


def row_total(value):
    return lax.psum(value, "row")


def to_heads(value):
    return lax.all_to_all(value, "col", split_axis=0, concat_axis=1, tiled=True)


def to_rows(value):
    return lax.all_to_all(value, "col", split_axis=1, concat_axis=0, tiled=True)


def norm_forward(hidden, gain):
    total = row_total(jnp.sum(hidden * hidden, axis=1))
    scale = lax.rsqrt(total / D + EPS)
    return (scale, to_half(hidden * scale[:, None] * gain[None, :]))


def norm_backward(hidden, gain, scale, grad):
    inner = row_total(jnp.sum(grad * gain[None, :] * hidden, axis=1))
    back = (
        grad * gain[None, :] * scale[:, None]
        - hidden * (scale * scale * scale * inner / D)[:, None]
    )
    gain_grad = jnp.sum(grad * hidden * scale[:, None], axis=0)
    return (back, gain_grad)


def rotary(places):
    half = HD // 2
    freq = 10000.0 ** (-2.0 * jnp.arange(half, dtype=jnp.float32) / HD)
    angle = places[:, None] * freq[None, :]
    return (jnp.cos(angle), jnp.sin(angle))


def rotate(heads, cosine, sine):
    half = HD // 2
    first = heads[..., :half]
    second = heads[..., half:]
    cosine = cosine[:, None, :]
    sine = sine[:, None, :]
    return jnp.concatenate(
        [first * cosine - second * sine, second * cosine + first * sine], axis=-1
    )


def rotate_back(heads, cosine, sine):
    half = HD // 2
    first = heads[..., :half]
    second = heads[..., half:]
    cosine = cosine[:, None, :]
    sine = sine[:, None, :]
    return jnp.concatenate(
        [first * cosine + second * sine, second * cosine - first * sine], axis=-1
    )


def piece_ids(pieces, places):
    inside = (places[:, None] >= pieces[None, :]) & (places[:, None] < pieces[None, :] + PIECE)
    number = jnp.arange(1, PIECES + 1, dtype=jnp.int32)
    return jnp.sum(jnp.where(inside, number[None, :], 0), axis=1) - 1


def block_scores(queries, keys, places, ids, pieces, start):
    key_places = start + jnp.arange(keys.shape[0], dtype=jnp.int32)
    key_ids = piece_ids(pieces, key_places)
    raw = jnp.einsum("tkgd,skd->kgts", queries, keys, preferred_element_type=jnp.float32) * HD ** (
        -0.5
    )
    allowed = (key_places[None, :] <= places[:, None]) | (key_ids[None, :] == ids[:, None]) & (
        ids[:, None] >= 0
    )
    allowed = allowed[None, None]
    return (jnp.where(allowed, raw, MASKED), allowed)


def split_blocks(keyvals, width):
    count = keyvals.shape[0] // width
    blocks = keyvals.reshape(count, width, 2, KV_HEADS, HD)
    firsts = jnp.arange(count, dtype=jnp.int32) * width
    return (blocks, firsts)


def attend(queries, keyvals, places, ids, pieces, width):
    blocks, firsts = split_blocks(keyvals, width)
    shape = (KV_HEADS, queries.shape[2], queries.shape[0])

    def measure(carry, item):
        high, total = carry
        scores, allowed = block_scores(queries, item[0][:, 0], places, ids, pieces, item[1])
        new_high = jnp.maximum(high, jnp.max(scores, axis=-1))
        weights = jnp.where(allowed, jnp.exp(scores - new_high[..., None]), 0.0)
        return ((new_high, total * jnp.exp(high - new_high) + jnp.sum(weights, axis=-1)), None)

    start_state = (jnp.full(shape, MASKED, jnp.float32), jnp.zeros(shape, jnp.float32))
    (high, total), unused = lax.scan(measure, start_state, (blocks, firsts))
    logsum = high + jnp.log(total)

    def accumulate(acc, item):
        scores, allowed = block_scores(queries, item[0][:, 0], places, ids, pieces, item[1])
        probs = to_half(jnp.where(allowed, jnp.exp(scores - logsum[..., None]), 0.0))
        return (
            acc
            + jnp.einsum(
                "kgts,skd->tkgd", probs, item[0][:, 1], preferred_element_type=jnp.float32
            ),
            None,
        )

    output, unused = lax.scan(accumulate, jnp.zeros(queries.shape, jnp.float32), (blocks, firsts))
    return (output, logsum)


def attend_back(queries, keyvals, places, ids, pieces, width, logsum, grad_out, output):
    blocks, firsts = split_blocks(keyvals, width)
    delta = jnp.einsum("tkgd,tkgd->kgt", grad_out.astype(jnp.float32), output)
    factor = HD ** (-0.5)

    def sweep(acc, item):
        keys = item[0][:, 0]
        values = item[0][:, 1]
        scores, allowed = block_scores(queries, keys, places, ids, pieces, item[1])
        probs = jnp.where(allowed, jnp.exp(scores - logsum[..., None]), 0.0)
        grad_probs = jnp.einsum(
            "tkgd,skd->kgts", grad_out, values, preferred_element_type=jnp.float32
        )
        grad_scores = to_half(probs * (grad_probs - delta[..., None]))
        acc = (
            acc
            + jnp.einsum("kgts,skd->tkgd", grad_scores, keys, preferred_element_type=jnp.float32)
            * factor
        )
        grad_keys = (
            jnp.einsum("kgts,tkgd->skd", grad_scores, queries, preferred_element_type=jnp.float32)
            * factor
        )
        grad_values = jnp.einsum(
            "kgts,tkgd->skd", to_half(probs), grad_out, preferred_element_type=jnp.float32
        )
        joined = jnp.concatenate(
            [grad_keys.reshape(width, -1), grad_values.reshape(width, -1)], axis=1
        )
        return (acc, joined)

    grad_queries, grad_blocks = lax.scan(
        sweep, jnp.zeros(queries.shape, jnp.float32), (blocks, firsts)
    )
    return (grad_queries, grad_blocks.reshape(keyvals.shape[0], -1))


def adamw(weight, first, second, grad, rate, decay):
    first_new = BETA * first + (1.0 - BETA) * grad
    second_new = BETA * second + (1.0 - BETA) * grad * grad
    fix = 1.0 - BETA**STEP
    update = first_new / fix / (jnp.sqrt(second_new / fix) + TINY)
    weight_new = weight - rate * (update + decay * weight)
    return (first_new, second_new, weight_new)


def grid_plan(tokens, cotangent, starts, gains, w_query, w_keyval, w_output, w_gateup, w_down):
    columns = lax.axis_size("col")
    column = lax.axis_index("col")
    seq_len = TD * columns
    width = min(1024, seq_len)
    group = HEADS // KV_HEADS
    query_width = w_query.shape[1]
    key_width = w_keyval.shape[2]
    feed_width = w_gateup.shape[2]
    pieces = lax.dynamic_index_in_dim(starts, lax.axis_index("row"), 0, keepdims=False)
    hidden = tokens.astype(jnp.float32)
    inner_weights = to_half(jnp.concatenate([w_query, w_keyval[0], w_keyval[1]], axis=1))
    feed_weights = to_half(jnp.concatenate([w_gateup[0], w_gateup[1]], axis=1))
    out_weights = to_half(w_output)
    down_weights = to_half(w_down)
    scale_one, normed_one = norm_forward(hidden, gains[0])
    gathered_one = col_collect(normed_one)
    mixed = to_half(row_reduce(product(gathered_one, inner_weights)))
    spread = to_heads(mixed[:, None, :])
    query_raw = spread[:, :, :query_width].reshape(TD, HEADS, HD)
    key_raw = spread[:, :, query_width : query_width + key_width].reshape(TD, KV_HEADS, HD)
    value_heads = spread[:, :, query_width + key_width :].reshape(TD, KV_HEADS * HD)
    places = column * TD + jnp.arange(TD, dtype=jnp.int32)
    cosine, sine = rotary(places.astype(jnp.float32))
    queries = to_half(rotate(query_raw.astype(jnp.float32), cosine, sine)).reshape(
        TD, KV_HEADS, group, HD
    )
    keys = to_half(rotate(key_raw.astype(jnp.float32), cosine, sine))
    keyvals_local = jnp.concatenate([keys.reshape(TD, KV_HEADS * HD), value_heads], axis=1)
    keyvals = lax.all_gather(keyvals_local, "col", axis=0, tiled=True)
    ids = piece_ids(pieces, places)
    output, logsum = attend(queries, keyvals, places, ids, pieces, width)
    attended = to_half(output)
    attended_rows = to_rows(attended.reshape(TD, columns, query_width))[:, 0, :]
    gathered_att = row_collect(attended_rows)
    branch = col_reduce(product(gathered_att, out_weights))
    middle = hidden + branch
    scale_two, normed_two = norm_forward(middle, gains[1])
    gathered_two = col_collect(normed_two)
    feed = row_reduce(product(gathered_two, feed_weights))
    gate = feed[:, :feed_width]
    upward = feed[:, feed_width:]
    sigma = jax.nn.sigmoid(gate)
    swish = gate * sigma
    activated = to_half(swish * upward)
    gathered_act = row_collect(activated)
    result = middle + col_reduce(product(gathered_act, down_weights))
    block_out = to_half(result)
    both = lax.all_gather(jnp.stack([normed_one, normed_two]), "col", axis=1, tiled=True)
    back_one = both[0]
    back_two = both[1]
    grad_rows = col_collect(cotangent)
    grad_down = product_left(gathered_act, grad_rows)
    grad_act = row_reduce(product_right(grad_rows, down_weights))
    slope = sigma * (1.0 + gate * (1.0 - sigma))
    grad_feed = to_half(jnp.concatenate([grad_act * upward * slope, grad_act * swish], axis=1))
    gathered_feed = row_collect(grad_feed)
    grad_both = product_left(back_two, gathered_feed)
    grad_gateup = jnp.stack([grad_both[:, :feed_width], grad_both[:, feed_width:]])
    grad_normed_two = col_reduce(product_right(gathered_feed, feed_weights))
    norm_two_back, gain_two = norm_backward(middle, gains[1], scale_two, grad_normed_two)
    grad_middle = cotangent.astype(jnp.float32) + norm_two_back
    gathered_mid = col_collect(to_half(grad_middle))
    grad_output = product_left(gathered_att, gathered_mid)
    grad_att = to_half(row_reduce(product_right(gathered_mid, out_weights)))
    grad_heads = to_heads(grad_att[:, None, :]).reshape(TD, KV_HEADS, group, HD)
    keyvals_back = lax.all_gather(keyvals_local, "col", axis=0, tiled=True)
    grad_queries, grad_keyvals = attend_back(
        queries, keyvals_back, places, ids, pieces, width, logsum, grad_heads, output
    )
    local_keyvals = lax.psum_scatter(grad_keyvals, "col", scatter_dimension=0, tiled=True)
    kv_split = KV_HEADS * HD
    grad_query_raw = rotate_back(grad_queries.reshape(TD, HEADS, HD), cosine, sine)
    grad_key_raw = rotate_back(local_keyvals[:, :kv_split].reshape(TD, KV_HEADS, HD), cosine, sine)
    grad_value = local_keyvals[:, kv_split:]
    joined = jnp.concatenate(
        [
            to_half(grad_query_raw).reshape(TD, columns, query_width),
            to_half(grad_key_raw).reshape(TD, columns, key_width),
            to_half(grad_value).reshape(TD, columns, key_width),
        ],
        axis=2,
    )
    grad_mixed = to_rows(joined)[:, 0, :]
    gathered_mixed = row_collect(grad_mixed)
    grad_inner = product_left(back_one, gathered_mixed)
    grad_query = grad_inner[:, :query_width]
    grad_keyval = jnp.stack(
        [
            grad_inner[:, query_width : query_width + key_width],
            grad_inner[:, query_width + key_width :],
        ]
    )
    grad_normed_one = col_reduce(product_right(gathered_mixed, inner_weights))
    norm_one_back, gain_one = norm_backward(hidden, gains[0], scale_one, grad_normed_one)
    input_grad = to_half(grad_middle + norm_one_back)
    gain_grads = lax.psum(jnp.stack([gain_one, gain_two]), "col")
    return (
        block_out,
        input_grad,
        gain_grads,
        grad_query,
        grad_keyval,
        grad_output,
        grad_gateup,
        grad_down,
    )


def local_general(
    tokens,
    cotangent,
    starts,
    gains,
    gains_m,
    gains_v,
    w_query,
    w_query_m,
    w_query_v,
    w_keyval,
    w_keyval_m,
    w_keyval_v,
    w_output,
    w_output_m,
    w_output_v,
    w_gateup,
    w_gateup_m,
    w_gateup_v,
    w_down,
    w_down_m,
    w_down_v,
):
    results = grid_plan(
        tokens, cotangent, starts, gains, w_query, w_keyval, w_output, w_gateup, w_down
    )
    (
        block_out,
        input_grad,
        gain_grads,
        grad_query,
        grad_keyval,
        grad_output,
        grad_gateup,
        grad_down,
    ) = results
    rate_in = D ** (-0.5)
    rate_down = FF ** (-0.5)
    gain_m, gain_v, gain_w = adamw(gains, gains_m, gains_v, gain_grads, 0.25, 0.0)
    query_m, query_v, query_w = adamw(w_query, w_query_m, w_query_v, grad_query, rate_in, DECAY)
    keyval_m, keyval_v, keyval_w = adamw(
        w_keyval, w_keyval_m, w_keyval_v, grad_keyval, rate_in, DECAY
    )
    output_m, output_v, output_w = adamw(
        w_output, w_output_m, w_output_v, grad_output, rate_in, DECAY
    )
    gateup_m, gateup_v, gateup_w = adamw(
        w_gateup, w_gateup_m, w_gateup_v, grad_gateup, rate_in, DECAY
    )
    down_m, down_v, down_w = adamw(w_down, w_down_m, w_down_v, grad_down, rate_down, DECAY)
    return (
        block_out,
        input_grad,
        gain_m,
        gain_v,
        gain_w,
        query_m,
        query_v,
        query_w,
        to_half(query_w),
        keyval_m,
        keyval_v,
        keyval_w,
        to_half(keyval_w),
        output_m,
        output_v,
        output_w,
        to_half(output_w),
        gateup_m,
        gateup_v,
        gateup_w,
        to_half(gateup_w),
        down_m,
        down_v,
        down_w,
        to_half(down_w),
    )


TB = 128
LOG_BASE = 9.210340371976184
MESH = pl.DeviceIdType.MESH
half = jnp.bfloat16
full = jnp.float32
VM = pl.BlockSpec(memory_space=pltpu.VMEM)
SM = pl.BlockSpec(memory_space=pltpu.SMEM)


def mate(r, m):
    x = lax.rem(lax.rem(r, 2) + lax.rem(m, 2), 2)
    y = lax.rem(r // 2 + m // 2, 2)
    return 2 * y + x


def other_core(c):
    return c + 1 - 2 * lax.rem(c, 2)


def z_ahead(c, m):
    return lax.rem(c + 2 * m, 8)


def block_rows(b):
    return pl.ds(pl.multiple_of(b * TB, TB), TB)


def part_rows(b, h):
    if h is None:
        return block_rows(b)
    return pl.ds(pl.multiple_of(b * TB + 64 * h, 64), 64)


def slice_rows(b, h=None):
    if h is None:
        return pl.ds(pl.multiple_of(b * 288, 32), 288)
    return pl.ds(pl.multiple_of(b * 288 + 144 * h, 16), 144)


def greet(targets):
    barrier = pltpu.get_barrier_semaphore()
    for target in targets:
        pl.semaphore_signal(barrier, inc=1, device_id=target, device_id_type=MESH)
    return lambda: pl.semaphore_wait(barrier, len(targets))


def remote(src, dst, send, recv, target):
    return pltpu.make_async_remote_copy(
        src_ref=src, dst_ref=dst, send_sem=send, recv_sem=recv, device_id=target, device_id_type=MESH
    )


class Gather:
    def __init__(self, view, r, c, send, recv):
        x, y, far = mate(r, 1), mate(r, 2), mate(r, 3)
        self.first = [
            remote(view(r, 0), view(r, 0), send.at[0], recv.at[0], (x, c)),
            remote(view(r, 1), view(r, 1), send.at[1], recv.at[1], (y, c)),
            remote(view(r, 1), view(r, 1), send.at[4], recv.at[4], (x, c)),
            remote(view(r, 0), view(r, 0), send.at[5], recv.at[5], (y, c)),
        ]
        self.onward = [
            remote(view(x, 0), view(x, 0), send.at[2], recv.at[2], (y, c)),
            remote(view(y, 1), view(y, 1), send.at[3], recv.at[3], (x, c)),
        ]
        self.arrive = [
            remote(view(x, 0), view(x, 0), send.at[0], recv.at[0], (x, c)),
            remote(view(y, 1), view(y, 1), send.at[1], recv.at[1], (y, c)),
            remote(view(far, 0), view(far, 0), send.at[2], recv.at[2], (y, c)),
            remote(view(far, 1), view(far, 1), send.at[3], recv.at[3], (x, c)),
            remote(view(x, 1), view(x, 1), send.at[4], recv.at[4], (x, c)),
            remote(view(y, 0), view(y, 0), send.at[5], recv.at[5], (y, c)),
        ]

    def start(self):
        for copy in self.first:
            copy.start()

    def relay(self):
        for i in range(2):
            self.arrive[i].wait_recv()
            self.onward[i].start()
        for i in (4, 5):
            self.arrive[i].wait_recv()

    def finish(self):
        self.arrive[2].wait_recv()
        self.arrive[3].wait_recv()

    def sent(self):
        for copy in self.first + self.onward:
            copy.wait_send()


class Scatter:
    def __init__(self, out, near, mid, last, r, c, send, recv):
        x, y = (mate(r, 1), c), (mate(r, 2), c)
        up, low = pl.ds(0, 64), pl.ds(64, 64)
        self.out, self.near, self.mid, self.last = out, near, mid, last
        self.first = [
            remote(out.at[0, up], near.at[0, 0], send.at[0], recv.at[0], x),
            remote(out.at[1, low], near.at[1, 0], send.at[1], recv.at[1], y),
            remote(out.at[2, up], near.at[0, 1], send.at[2], recv.at[2], x),
            remote(out.at[2, low], near.at[1, 1], send.at[3], recv.at[3], y),
        ]
        self.second = [
            remote(mid.at[0], last.at[0], send.at[4], recv.at[4], y),
            remote(mid.at[1], last.at[1], send.at[5], recv.at[5], x),
        ]

    def start(self, which=(2, 3, 0, 1)):
        for i in which:
            self.first[i].start()

    def relay(self):
        self.first[2].wait_recv()
        self.mid[0] = (self.out[1, 0:64].astype(full) + self.near[0, 1].astype(full)).astype(half)
        self.second[0].start()
        self.first[3].wait_recv()
        self.mid[1] = (self.out[0, 64:128].astype(full) + self.near[1, 1].astype(full)).astype(half)
        self.second[1].start()

    def finish(self, own):
        for copy in self.first[:2] + self.second:
            copy.wait_recv()
        upper = own[0:64] + self.near[0, 0].astype(full) + self.last[0].astype(full)
        lower = own[64:128] + self.near[1, 0].astype(full) + self.last[1].astype(full)
        return jnp.concatenate([upper, lower], axis=0)

    def sent(self):
        for copy in self.first + self.second:
            copy.wait_send()


def scatter_buffers(width):
    v = pltpu.VMEM
    return [
        v((3, TB, width), half),
        v((2, 2, 64, width), half),
        v((2, 64, width), half),
        v((2, 64, width), half),
    ]


def idle_plane(r, k):
    x = lax.rem(r, 2)
    return 2 * (1 - lax.rem(x + k, 2)) + 1 - r // 2


def tile_place(r, k, z):
    return jnp.minimum(lax.rem(z - idle_plane(r, k) + 3, 4), 2)


def has_tile(b, z, k):
    return (b // 2 == lax.rem(z, 2)) | (lax.rem(b, 2) == lax.rem(k + z // 2, 2))


def tile_of(b, z):
    return jnp.where(b // 2 == lax.rem(z, 2), lax.rem(b, 2), 2)


def tile_cols(place):
    return pl.ds(pl.multiple_of(place * 128, 128), 128)


class TileGather:
    def __init__(self, mine, view, r, c, zs, zr, cs, cr):
        self.r, self.z, self.k = r, c // 2, lax.rem(c, 2)
        core = (r, other_core(c))
        z, k = self.z, self.k
        self.has = has_tile(r, z, k)
        here = view(3 * k + tile_place(r, k, z))
        self.out = [remote(mine, here, zs.at[m], zr.at[m], (r, z_ahead(c, m + 1))) for m in range(3)]
        self.out.append(remote(mine, here, cs.at[3], cr.at[3], core))
        self.relays = []
        for m in range(3):
            src = lax.rem(z + 3 - m, 4)
            slot = view(3 * k + tile_place(r, k, src))
            self.relays.append(
                (
                    has_tile(r, src, k),
                    remote(slot, slot, zs.at[m], zr.at[m], core),
                    remote(slot, slot, cs.at[m], cr.at[m], core),
                )
            )
        self.others = []
        for m in range(4):
            src = z if m == 3 else lax.rem(z + 3 - m, 4)
            slot = view(3 * (1 - k) + tile_place(r, 1 - k, src))
            self.others.append(
                (has_tile(r, src, 1 - k), remote(slot, slot, cs.at[m], cr.at[m], core))
            )

    def start(self):
        for copy in self.out:
            copy.start()

    def relay(self):
        for flag, come, go in self.relays:

            @pl.when(flag)
            def _():
                come.wait_recv()
                go.start()

    def finish(self):
        for flag, come in self.others:

            @pl.when(flag)
            def _():
                come.wait_recv()

    def sent(self):
        @pl.when(self.has)
        def _():
            for copy in self.out:
                copy.wait_send()

        for flag, come, go in self.relays:

            @pl.when(flag)
            def _():
                go.wait_send()


class PlaneSum:
    def __init__(self, part, over, joint, last, r, c, send, recv, has=None):
        z, k = c // 2, lax.rem(c, 2)
        side = z // 2
        beside = 2 * side + 1 - lax.rem(z, 2)
        self.far = (2 - side, 3 - 3 * side)
        self.part, self.over, self.joint, self.last = part, over, joint, last
        has = has or (lambda plane: plane >= 0)
        at_end = (z == 0) | (z == 3)
        self.owns = has(z)
        to = lambda plane: (r, 2 * plane + k)
        self.direct = (
            has(beside), remote(part(beside), last.at[0], send.at[0], recv.at[0], to(beside))
        )
        self.first = []
        self.second = []
        for i in range(2):
            plane = self.far[i]
            self.first.append(
                (
                    at_end & has(plane),
                    remote(part(plane), over.at[i], send.at[1 + i], recv.at[1 + i], to(beside)),
                )
            )
            self.second.append(
                (
                    (1 - at_end.astype(jnp.int32) > 0) & has(plane),
                    remote(joint.at[i], last.at[1], send.at[3 + i], recv.at[3], to(plane)),
                )
            )

    def start(self):
        for flag, copy in (self.first[1], self.first[0], self.direct):

            @pl.when(flag)
            def _():
                copy.start()

    def relay(self):
        for i in (1, 0):
            flag, copy = self.second[i]

            @pl.when(flag)
            def _():
                self.first[i][1].wait_recv()
                value = self.part(self.far[i])[...].astype(full) + self.over[i].astype(full)
                self.joint[i] = value.astype(half)
                copy.start()

    def arrive(self):
        self.direct[1].wait_recv()
        self.second[0][1].wait_recv()
        return self.last[0].astype(full) + self.last[1].astype(full)

    def sent(self):
        for flag, copy in [self.direct] + self.first + self.second:

            @pl.when(flag)
            def _():
                copy.wait_send()


def turn(value, cosine, sine):
    lane = lax.broadcasted_iota(jnp.int32, (value.shape[0], 128), 1)
    first = lax.rem(lane, 64) < 32
    parts = []
    for i in range(value.shape[1] // 128):
        part = value[:, 128 * i : 128 * i + 128]
        swapped = jnp.where(first, pltpu.roll(part, 96, 1), pltpu.roll(part, 32, 1))
        parts.append(part * cosine + swapped * sine)
    return jnp.concatenate(parts, axis=1)


def turn_tables(base):
    lane = lax.broadcasted_iota(jnp.int32, (TB, 128), 1)
    place = (lax.broadcasted_iota(jnp.int32, (TB, 128), 0) + base).astype(full)
    power = lax.rem(lane, 32).astype(full) * (-2.0 / HD)
    angle = place * jnp.exp(power * LOG_BASE)
    sine = jnp.sin(angle)
    return jnp.cos(angle), jnp.where(lax.rem(lane, 64) < 32, -sine, sine)


def mask_bias(starts_ref, seq, base):
    keys = lax.broadcasted_iota(jnp.int32, (1, 1024), 1)
    rows = lax.broadcasted_iota(jnp.int32, (TB, 1), 0) + base
    key_id = jnp.zeros((1, 1024), jnp.int32)
    row_id = jnp.zeros((TB, 1), jnp.int32)
    for j in range(PIECES):
        first = starts_ref[seq, j]
        key_id = key_id + jnp.where((keys >= first) & (keys < first + PIECE), j + 1, 0)
        row_id = row_id + jnp.where((rows >= first) & (rows < first + PIECE), j + 1, 0)
    row_id = jnp.where(row_id == 0, -1, row_id)
    allowed = (keys <= rows) | (key_id == row_id)
    return jnp.where(allowed, 0.0, MASKED)


def forward_kernel(
    tok_ref, cot_ref, wq_ref, wkv_ref, wo_ref, wgu_ref, wd_ref, gains_ref, starts_ref,
    mid_hbm, q_hbm, kv_hbm, lse_hbm, out_hbm, wof_hbm, wi_hbm, n1_hbm, srow_hbm, sown_hbm,
    down_hbm, gm_hbm, att_hbm, gain_hbm, dwz_hbm, dwd_hbm,
    mid_ref, q_ref, kv_ref, lse_ref, out_ref, wof_ref, wi_ref, n1_ref, srow_ref, sown_ref,
    down_ref, gm_ref, att_all, gain_out, dwz, dwd_ref,
    gain2_src, cotall_ref, w_ref, all_ref, d_ref, wd, act, slope, swish, px_out, px_in, dwzd, zin,
    tempd, own_grad, b0, b1, b2, b3,
    wsrc, osrc, w3, blk, tile, tok_own, sums, gain_parts, kv_own, q_own, wo_all,
    hid, kvb0, kvb1, kvb2, kvb3, qb0, qb1, qb2, qb3,
    zq_s, zq_r, cq_s, cq_r, a_s, a_r, zo_s, zo_r, po_s, po_r, co_s, co_r, t_s, t_r, c_s, c_r,
    g_s, g_r, kp_s, kp_r, qp_s, qp_r, kv_s, kv_r, ck_s, ck_r, zt_s, zt_r, ct_s, ct_r, ss_s, ss_r,
    n_s, n_r, s_s, s_r, zd_s, zd_r, cd_s, cd_r, px_s, px_r, z_s, z_r, at_s, at_r, out_s,
):
    r = lax.axis_index("row")
    c = lax.axis_index("col")
    z = c // 2
    k = lax.rem(c, 2)
    oc = other_core(c)
    mates = [(mate(r, m), c) for m in (1, 2, 3)]
    aheads = [(r, z_ahead(c, m)) for m in (1, 2, 3)]
    core = (r, oc)
    ready = greet(mates + [core] + aheads)
    mine = slice_rows(r)
    sent = []

    def send(src, dst, send_sem, recv_sem, target):
        copy = remote(src, dst, send_sem, recv_sem, target)
        copy.start()
        sent.append(copy)
        return copy

    stores = []

    def store(src, dst):
        copy = pltpu.make_async_copy(src, dst, out_s.at[len(stores)])
        copy.start()
        stores.append(copy)

    joined = jnp.concatenate([wq_ref[...], wkv_ref[0], wkv_ref[1]], axis=0)
    wsrc[...] = jnp.transpose(joined).astype(half)
    blk[c] = wsrc[...]
    tokens = tok_ref[...].astype(full)
    sums[r] = jnp.broadcast_to(jnp.sum(tokens * tokens, axis=0, keepdims=True), (8, 512))
    gain2_src[...] = jnp.broadcast_to(gains_ref[1:2, :], (8, 288))
    ready()
    qz = [send(wsrc, blk.at[c], zq_s.at[m], zq_r.at[m], aheads[m]) for m in range(3)]
    q_core = [send(wsrc, blk.at[c], cq_s.at[3], cq_r.at[3], core)]
    sum_copies = [
        send(sums.at[r], sums.at[r], ss_s.at[m], ss_r.at[m], mates[m]) for m in range(3)
    ]
    tok_copies = [
        send(tok_ref.at[:, block_rows(mates[m][0])], tok_own.at[mine], t_s.at[m], t_r.at[m], mates[m])
        for m in range(3)
    ]
    gain_copies = [
        send(gain2_src, gain_parts.at[r], g_s.at[m], g_r.at[m], mates[m]) for m in range(3)
    ]
    for i in range(3):
        for t in range(3):
            src = wd_ref[...] if t == 2 else wgu_ref[t]
            w3[i, t] = src[:, 128 * i : 128 * i + 128].astype(half)
    tile_sends = []
    for m in range(3):
        b = mates[m][0]
        copy = remote(
            w3.at[tile_of(b, z)], tile.at[:, mine, :], a_s.at[m], a_r.at[m], mates[m]
        )
        tile_sends.append((has_tile(b, z, k), copy))

        @pl.when(has_tile(b, z, k))
        def _():
            copy.start()

    cotall_ref[mine, :] = cot_ref[...]
    cot_gather = Gather(lambda b, h: cotall_ref.at[slice_rows(b, h)], r, c, c_s, c_r)
    cot_gather.start()
    for j in range(3):
        osrc[:, 288 * j : 288 * j + 288] = wo_ref[48 * j : 48 * j + 48, :].astype(half)
    wo_all[r, z, k] = osrc[...]
    tok_own[mine, :] = tok_ref[:, block_rows(r)]
    gain_parts[r] = gain2_src[...]

    @pl.when(has_tile(r, z, k))
    def _():
        tile[:, mine, :] = w3[tile_of(r, z)]

    for copy in sum_copies:
        copy.wait_recv()
    scale_row = lax.rsqrt((sums[0] + sums[1] + sums[2] + sums[3]) / D + EPS)
    srow_ref[...] = scale_row
    gain1 = jnp.transpose(jnp.broadcast_to(gains_ref[0:1, :], (128, 288)))[:, 0:1]
    n1_ref[...] = (tokens * scale_row[0:1, :] * gain1).astype(half)
    cosine, sine = turn_tables(512 * k + TB * r)
    bias = mask_bias(starts_ref, z, 512 * k + TB * r)
    for m in range(3):
        src = lax.rem(c + 6 - 2 * m, 8)
        remote(wsrc, blk.at[src], zq_s.at[m], zq_r.at[m], core).wait_recv()
        q_core.append(send(blk.at[src], blk.at[src], cq_s.at[m], cq_r.at[m], core))
    oz = [send(osrc, wo_all.at[r, z, k], zo_s.at[m], zo_r.at[m], aheads[m]) for m in range(3)]
    gate_up = TileGather(
        tile.at[0:2],
        lambda slot: w_ref.at[:, :, tile_cols(slot)],
        r, c, zt_s, zt_r, ct_s, ct_r,
    )

    downs = TileGather(
        tile.at[2], lambda slot: wd.at[:, tile_cols(slot)], r, c, zd_s, zd_r, cd_s, cd_r
    )

    @pl.when(gate_up.has)
    def _():
        for m in range(3):
            src = slice_rows(mates[m][0])
            remote(w3.at[0], tile.at[:, src, :], a_s.at[m], a_r.at[m], mates[m]).wait_recv()
        gate_up.start()

    for m in range(3):
        src = lax.rem(oc + 6 - 2 * m, 8)
        remote(blk.at[src], blk.at[src], cq_s.at[m], cq_r.at[m], core).wait_recv()
    remote(wsrc, blk.at[oc], cq_s.at[3], cq_r.at[3], core).wait_recv()
    for i in range(8):
        wi_ref[:, 144 * i : 144 * i + 144] = blk[i, :, 0:144]
        wi_ref[:, 1152 + 48 * i : 1200 + 48 * i] = blk[i, :, 144:192]
        wi_ref[:, 1536 + 48 * i : 1584 + 48 * i] = blk[i, :, 192:240]
    store(wi_ref, wi_hbm)
    store(n1_ref, n1_hbm)
    store(srow_ref, srow_hbm)
    kv_scatter = Scatter(kvb0, kvb1, kvb2, kvb3, r, c, kp_s, kp_r)
    q_scatter = Scatter(qb0, qb1, qb2, qb3, r, c, qp_s, qp_r)
    for m in (2, 0, 1):
        part = n1_ref[:, block_rows(mates[m][0])]
        kvb0[m] = product_left(part, wi_ref[:, 1152:]).astype(half)
        kv_scatter.start(((0,), (1,), (2, 3))[m])
    cot_gather.relay()
    for m in (2, 0, 1):
        part = n1_ref[:, block_rows(mates[m][0])]
        qb0[m] = product_left(part, wi_ref[:, :1152]).astype(half)
    kv_scatter.relay()
    q_scatter.start()
    part = n1_ref[:, block_rows(r)]
    kv_own[...] = product_left(part, wi_ref[:, 1152:])
    q_own[...] = product_left(part, wi_ref[:, :1152])
    for m in range(3):
        src = slice_rows(mates[m][0])
        remote(
            tok_ref.at[:, block_rows(0)], tok_own.at[src], t_s.at[m], t_r.at[m], mates[m]
        ).wait_recv()
    hidden = jnp.transpose(tok_own[...].astype(full))
    hid[...] = hidden
    scale = lax.rsqrt(jnp.sum(hidden * hidden, axis=1, keepdims=True) / D + EPS)
    sown_ref[...] = jnp.broadcast_to(scale, (TB, 128))
    raw = kv_scatter.finish(kv_own).astype(half)
    my_block = block_rows(4 * k + r)
    kv_ref[my_block, 0:384] = turn(raw[:, 0:384].astype(full), cosine, sine).astype(half)
    kv_ref[my_block, 384:768] = raw[:, 384:768]
    kv_gather = Gather(lambda b, h: kv_ref.at[part_rows(4 * k + b, h)], r, c, kv_s, kv_r)
    kv_gather.start()

    def kv_core(j, b):
        rows = block_rows(4 * k + b)
        return send(kv_ref.at[rows], kv_ref.at[rows], ck_s.at[j], ck_r.at[j], core)

    kv_core(3, r)
    q_scatter.relay()
    for copy in oz:
        copy.wait_recv()
    wo_gather = Gather(
        lambda b, h: wo_all.at[b, :, k] if h is None else wo_all.at[b, 2 * h : 2 * h + 2, k],
        r, c, po_s, po_r,
    )
    kv_gather.relay()
    wo_gather.start()
    raw = q_scatter.finish(q_own).astype(half)
    queries = turn(raw.astype(full), cosine, sine).astype(half)
    q_ref[...] = queries
    queries = queries * jnp.bfloat16(0.125)
    for m in range(2):
        kv_core(m, mates[m][0])
    kv_gather.finish()
    kv_core(2, mates[2][0])
    for j in range(4):
        b = r if j == 3 else mates[j][0]
        rows = block_rows(4 * (1 - k) + b)
        remote(kv_ref.at[rows], kv_ref.at[rows], ck_s.at[j], ck_r.at[j], core).wait_recv()
    cot_gather.finish()
    def wo_swap(j, b):
        return send(wo_all.at[b, :, k], wo_all.at[b, :, k], co_s.at[j], co_r.at[j], core)

    store(kv_ref, kv_hbm)
    store(q_ref, q_hbm)
    store(sown_ref, sown_hbm)
    for g in range(KV_HEADS):
        if g == 3:

            @pl.when(downs.has)
            def _():
                downs.start()

        if g == 4:
            wo_swap(3, r)
            wo_gather.relay()
            wo_swap(0, mates[0][0])
            wo_swap(1, mates[1][0])
        keys = kv_ref[:, 64 * g : 64 * g + 64]
        values = kv_ref[:, 384 + 64 * g : 448 + 64 * g]
        heads = jnp.concatenate(
            [queries[:, 64 * h : 64 * h + 64] for h in range(3 * g, 3 * g + 3)], axis=0
        )
        scores = product_right(heads, keys).reshape(3, TB, 1024) + bias[None]
        high = jnp.max(scores, axis=-1, keepdims=True)
        weights = jnp.exp(scores - high)
        total = jnp.sum(weights, axis=-1, keepdims=True)
        probs = (weights * (1.0 / total)).astype(half).reshape(3 * TB, 1024)
        lse_ref[:, g : g + 1] = (high + jnp.log(total)).reshape(3 * TB, 1)
        output = product(probs, values)
        for j in range(3):
            h = 3 * g + j
            out_ref[:, 64 * h : 64 * h + 64] = output[TB * j : TB * j + TB]
    attended = out_ref[...].astype(half)
    store(lse_ref, lse_hbm)
    store(out_ref, out_hbm)
    gate_up.relay()

    wo_gather.finish()
    wo_swap(2, mates[2][0])
    for j in range(4):
        b = r if j == 3 else mates[j][0]
        remote(
            wo_all.at[b, :, 1 - k], wo_all.at[b, :, 1 - k], co_s.at[j], co_r.at[j], core
        ).wait_recv()
    for b in range(4):
        for i in range(4):
            for kk in range(2):
                for j in range(3):
                    row = 144 * (2 * i + kk) + 48 * j
                    wof_ref[row : row + 48, 288 * b : 288 * b + 288] = wo_all[
                        b, i, kk, :, 288 * j : 288 * j + 288
                    ]
    middle = hid[...] + product(attended, wof_ref[...])
    mid_ref[...] = middle
    store(wof_ref, wof_hbm)
    store(mid_ref, mid_hbm)
    for copy in gain_copies:
        copy.wait_recv()
    gain = jnp.concatenate([gain_parts[i] for i in range(4)], axis=1)
    scale_two = lax.rsqrt(jnp.sum(middle * middle, axis=1, keepdims=True) / D + EPS)
    my_rows = block_rows(r)
    all_ref[my_rows, :] = (middle * scale_two * gain[0:1, :]).astype(half)
    gather = Gather(lambda b, h: all_ref.at[part_rows(b, h)], r, c, n_s, n_r)
    scatter = Scatter(b0, b1, b2, b3, r, c, s_s, s_r)
    gather.start()

    @pl.when(gate_up.has)
    def _():
        cols = tile_cols(3 * k + tile_place(r, k, z))
        w_ref[:, :, cols] = tile[0:2]
        wd[:, cols] = tile[2]

    att_all[my_rows, :] = attended
    gate_up.finish()

    def up_to(b):
        rows = block_rows(b)
        normed = all_ref[rows, :]
        for j in range(3):
            cs = slice(256 * j, 256 * j + 256)
            gate = product(normed, w_ref[0, :, cs])
            up = product(normed, w_ref[1, :, cs])
            sigma = 1.0 / (1.0 + jnp.exp(-gate))
            hidden = gate * sigma
            act[rows, cs] = (hidden * up).astype(half)
            swish[rows, cs] = hidden
            slope[rows, cs] = up * (sigma * (1.0 + gate * (1.0 - sigma)))

    up_to(r)
    gather.relay()
    up_to(mates[0][0])
    up_to(mates[1][0])
    downs.relay()
    gather.finish()
    att_gather = Gather(lambda b, h: att_all.at[part_rows(b, h)], r, c, at_s, at_r)
    att_gather.start()
    up_to(mates[2][0])

    def tile_grads(t, core_index):
        cols = pl.ds(pl.multiple_of(384 * core_index, 128), 384)
        if t == 2:
            return product(cotall_ref[...], act[:, cols])
        return product_left(all_ref[...], d_ref[t, :, cols])

    px_copies = {}

    def to_other_core(t):
        part = tile_grads(t, 1 - k)
        for j in range(3):
            px_out[t, j] = part[:, 128 * j : 128 * j + 128].astype(half)
        px_copies[t] = send(px_out.at[t], px_in.at[t], px_s.at[t], px_r.at[t], core)

    downs.finish()

    def back(b):
        rows = block_rows(b)
        cot = cotall_ref[:, rows]
        for j in range(3):
            cs = slice(256 * j, 256 * j + 256)
            grad = product_left(cot, wd[:, cs])
            d_ref[0, rows, cs] = (grad * slope[rows, cs]).astype(half)
            d_ref[1, rows, cs] = (grad * swish[rows, cs]).astype(half)
        return product_right(d_ref[0, rows, :], w_ref[0]) + product_right(
            d_ref[1, rows, :], w_ref[1]
        )

    to_other_core(2)
    b0[2] = back(mates[2][0]).astype(half)
    scatter.start((2, 3))
    b0[0] = back(mates[0][0]).astype(half)
    scatter.start((0,))
    part = tile_grads(2, k)
    px_copies[2].wait_recv()
    for j in range(3):
        value = part[:, 128 * j : 128 * j + 128] + px_in[2, j].astype(full)
        tempd[j] = value
        dwzd[j] = value.astype(half)
    z_sends = []
    for m in range(3):
        ahead = lax.rem(z + m + 1, 4)
        place = tile_place(r, k, ahead)
        copy = remote(dwzd.at[place], zin.at[m], z_s.at[m], z_r.at[m], aheads[m])
        flag = has_tile(r, ahead, k)
        z_sends.append((flag, copy))

        @pl.when(flag)
        def _():
            copy.start()

    b0[1] = back(mates[1][0]).astype(half)
    scatter.start((1,))
    own_grad[...] = back(r)
    scatter.relay()
    att_gather.relay()
    to_other_core(0)
    to_other_core(1)
    for i in range(2):
        rows = slice(256 * i, 256 * i + 256)
        down_ref[rows, :] = product_right(act[rows, :], wd[...]).astype(half)
    store(down_ref, down_hbm)
    scale = scale_two
    cot = jnp.transpose(cotall_ref[:, my_rows].astype(full))
    hidden = mid_ref[...]
    grad = scatter.finish(own_grad)
    inner = jnp.sum(grad * gain[0:1, :] * hidden, axis=1, keepdims=True)
    gm = cot + grad * gain[0:1, :] * scale - hidden * (scale * scale * scale * inner / D)
    gm_ref[...] = gm.astype(half)
    store(gm_ref, gm_hbm)
    gain_out[...] = jnp.broadcast_to(
        jnp.sum(grad * hidden * scale, axis=0, keepdims=True), gain_out.shape
    )
    for t in range(2):
        part = tile_grads(t, k)
        px_copies[t].wait_recv()
        for j in range(3):
            value = part[:, 128 * j : 128 * j + 128] + px_in[t, j].astype(full)
            dwz[t, j] = value.astype(half)
    store(gain_out, gain_hbm)
    store(dwz, dwz_hbm)
    att_gather.finish()
    store(att_all, att_hbm)

    dwd_ref[...] = jnp.zeros_like(dwd_ref)

    @pl.when(downs.has)
    def _():
        value = tempd[tile_place(r, k, z)]
        for m in range(3):
            remote(dwzd.at[0], zin.at[m], z_s.at[m], z_r.at[m], aheads[m]).wait_recv()
            value = value + zin[m].astype(full)
        dwd_ref[...] = value

    store(dwd_ref, dwd_hbm)
    for copy in sent:
        copy.wait_send()
    for part in (
        cot_gather, kv_gather, wo_gather, gate_up, kv_scatter, q_scatter, downs, gather, scatter,
        att_gather,
    ):
        part.sent()
    for copy in stores:
        copy.wait()
    for flag, copy in tile_sends + z_sends:

        @pl.when(flag)
        def _():
            copy.wait_send()


def forward(*args):
    shape = jax.ShapeDtypeStruct
    v = pltpu.VMEM
    sems = []
    counts = (3, 6, 3, 3, 6, 6, 3, 6, 3, 6, 6, 6, 6, 3, 6, 3, 6, 6, 3, 6, 3, 3, 6)
    for count in counts:
        sems += [pltpu.SemaphoreType.DMA((count,))] * 2
    return pl.pallas_call(
        forward_kernel,
        out_shape=(
            shape((TB, D), full),
            shape((TB, D), half),
            shape((1024, 768), half),
            shape((3 * TB, 128), full),
            shape((TB, D), full),
            shape((D, D), half),
            shape((288, 1920), half),
            shape((288, 512), half),
            shape((8, 512), full),
            shape((TB, 128), full),
            shape((512, D), half),
            shape((TB, D), half),
            shape((512, D), half),
            shape((8, D), full),
            shape((2, 3, D, 128), half),
            shape((D, 128), full),
        ),
        in_specs=[VM] * 8 + [SM],
        out_specs=(pl.BlockSpec(memory_space=pl.ANY),) * 16,
        scratch_shapes=[
            v((TB, D), full),
            v((TB, D), half),
            v((1024, 768), half),
            v((3 * TB, 128), full),
            v((TB, D), full),
            v((D, D), half),
            v((288, 1920), half),
            v((288, 512), half),
            v((8, 512), full),
            v((TB, 128), full),
            v((512, D), half),
            v((TB, D), half),
            v((512, D), half),
            v((8, D), full),
            v((2, 3, D, 128), half),
            v((D, 128), full),
            v((8, 288), full),
            v((D, 512), half),
            v((2, D, 768), half),
            v((512, D), half),
            v((2, 512, 768), half),
            v((D, 768), half),
            v((512, 768), half),
            v((512, 768), full),
            v((512, 768), full),
            v((3, 3, D, 128), half),
            v((3, 3, D, 128), half),
            v((3, D, 128), half),
            v((3, D, 128), half),
            v((3, D, 128), full),
            v((TB, D), full),
        ]
        + scatter_buffers(D)
        + [
            v((288, 240), half),
            v((48, 864), half),
            v((3, 3, 288, 128), half),
            v((8, 288, 240), half),
            v((3, D, 128), half),
            v((D, TB), half),
            v((4, 8, 512), full),
            v((4, 8, 288), full),
            v((TB, 768), full),
            v((TB, D), full),
            v((4, 4, 2, 48, 864), half),
            v((TB, D), full),
        ]
        + scatter_buffers(768)
        + scatter_buffers(D)
        + sems
        + [pltpu.SemaphoreType.DMA((16,))],
        compiler_params=pltpu.CompilerParams(
            collective_id=1, has_side_effects=True, vmem_limit_bytes=60 << 20
        ),
    )(*args)


def back_kernel(
    mid_in, q_in, kv_in, lse_in, out_in, wof_in, wi_in, n1_in, srow_in, sown_in, down_in, gm_in,
    att_in, gain2_in, dwz_in, dwd_in, tok_ref, gains_in, starts_ref,
    bo_ref, ig_ref, dw_ref, dq_ref, do_ref, gains_ref,
    mid_ref, q_ref, kv_ref, lse_ref, out_ref, wof_ref, wi_ref, n1_ref, srow_ref, sown_ref,
    down_ref, gm_ref, att_all, gain2_ref, dwz, dwd_ref,
    gm_out, gm_nat, bo_out, z_over, z_joint, z_last, tile_out, dkv, dkv_co, dkv_ci, sdq, sdk, dqs, dwq, dwq_co, dwq_ci, dwq_z,
    dwq_over, dwq_joint, dwq_in,
    dwk, dwk_co, dwk_ci, dwk_z, dwk_in,
    dwo, dwo_co, dwo_ci, dwo_z, dwo_over, dwo_joint, dwo_in, g2_out, g2_in, gl, gl_ci, gl_z, gl_in, coef_all, dn_own,
    n0, n1, n2, n3, e0, e1, e2, e3,
    dn_s, dn_r, bo_s, bo_r, z_s, z_r, t_s, t_r, kc_s, kc_r, kp_s, kp_r, sd_s, sd_r, sk_s, sk_r,
    qc_s, qc_r, qz_s, qz_r, kk_s, kk_r, kz_s, kz_r, oc_s, oc_r, oz_s, oz_r, g2_s, g2_r, gc_s, gc_r,
    gz_s, gz_r, cf_s, cf_r, gm_s, gm_r, in_s,
):
    r = lax.axis_index("row")
    c = lax.axis_index("col")
    z = c // 2
    k = lax.rem(c, 2)
    mates = [(mate(r, m), c) for m in (1, 2, 3)]
    aheads = [(r, z_ahead(c, m)) for m in (1, 2, 3)]
    ahead_z = [lax.rem(z + m, 4) for m in (1, 2, 3)]
    core = (r, other_core(c))
    ready = greet(mates + [core] + aheads)
    loads = {}
    order = (
        ("dwz", dwz_in, dwz), ("gm", gm_in, gm_ref), ("gain2", gain2_in, gain2_ref),
        ("dwd", dwd_in, dwd_ref), ("down", down_in, down_ref), ("wof", wof_in, wof_ref),
        ("q", q_in, q_ref), ("kv", kv_in, kv_ref), ("lse", lse_in, lse_ref),
        ("out", out_in, out_ref), ("att", att_in, att_all), ("n1", n1_in, n1_ref),
        ("wi", wi_in, wi_ref), ("sown", sown_in, sown_ref), ("srow", srow_in, srow_ref),
        ("mid", mid_in, mid_ref),
    )
    for i, (name, src, dst) in enumerate(order):
        loads[name] = pltpu.make_async_copy(src, dst, in_s.at[i])
        loads[name].start()
    mine = block_rows(r)
    sent = []

    def send(src, dst, send_sem, recv_sem, target):
        copy = remote(src, dst, send_sem, recv_sem, target)
        copy.start()
        sent.append(copy)
        return copy

    loads["gm"].wait()
    loads["gain2"].wait()
    for i in range(4):
        g2_out[i] = gain2_ref[:, 288 * i : 288 * i + 288]
    turned = jnp.transpose(gm_ref[...].astype(full)).astype(half)
    for i in range(4):
        gm_out[i] = turned[288 * i : 288 * i + 288]
    gm_nat[:, mine] = gm_out[r]
    loads["down"].wait()
    for m in range(3):
        n0[m] = down_ref[block_rows(mates[m][0]), :]
    mine_has = has_tile(r, z, k)
    my_place = tile_place(r, k, z)
    ready()
    loads["dwz"].wait()
    tile_sums = [
        PlaneSum(
            lambda plane, t=t: dwz.at[t, tile_place(r, k, plane)],
            z_over.at[t], z_joint.at[t], z_last.at[t], r, c, z_s.at[t], z_r.at[t],
            lambda plane: has_tile(r, plane, k),
        )
        for t in range(2)
    ]
    tile_sums[0].start()
    gm_copies = [
        send(gm_out.at[mates[m][0]], gm_nat.at[:, mine], gm_s.at[m], gm_r.at[m], mates[m])
        for m in range(3)
    ]

    def tile_copy(t, m):
        return remote(
            tile_out.at[mates[m][0], t],
            dw_ref.at[tile_of(r, z), t],
            t_s.at[3 * t + m],
            t_r.at[3 * t + m],
            mates[m],
        )

    def tile_back(t):
        @pl.when(mine_has)
        def _():
            value = dwd_ref[...] if t == 2 else dwz[t, my_place].astype(full)
            if t < 2:
                value = value + tile_sums[t].arrive()
            for b in range(4):
                tile_out[b, t] = value[288 * b : 288 * b + 288].astype(half)
            for m in range(3):
                tile_copy(t, m).start()
            dw_ref[tile_of(r, z), t] = tile_out[r, t]

    downs = Scatter(n0, n1, n2, n3, r, c, dn_s, dn_r)
    downs.start()
    g2_copies = [
        send(g2_out.at[mates[m][0]], g2_in.at[m], g2_s.at[m], g2_r.at[m], mates[m])
        for m in range(3)
    ]
    loads["wof"].wait()
    ga = product_right(gm_ref[...], wof_ref[...]).astype(half)
    gaf = ga.astype(full)
    loads["q"].wait()
    queries = q_ref[...] * jnp.bfloat16(0.125)
    cosine, sine = turn_tables(512 * k + TB * r)
    sine = -sine
    bias = mask_bias(starts_ref, z, 512 * k + TB * r)
    loads["kv"].wait()
    loads["lse"].wait()
    loads["out"].wait()
    for g in range(KV_HEADS):
        keys = kv_ref[:, 64 * g : 64 * g + 64]
        values = kv_ref[:, 384 + 64 * g : 448 + 64 * g]
        heads = range(3 * g, 3 * g + 3)
        qh = jnp.concatenate([queries[:, 64 * h : 64 * h + 64] for h in heads], axis=0)
        gh = jnp.concatenate([ga[:, 64 * h : 64 * h + 64] for h in heads], axis=0)
        delta = jnp.concatenate(
            [
                jnp.sum(
                    gaf[:, 64 * h : 64 * h + 64] * out_ref[:, 64 * h : 64 * h + 64],
                    axis=1,
                    keepdims=True,
                )
                for h in heads
            ],
            axis=0,
        )
        scores = product_right(qh, keys).reshape(3, TB, 1024) + bias[None]
        probs = jnp.exp(scores.reshape(3 * TB, 1024) - lse_ref[:, g : g + 1])
        grad_probs = product_right(gh, values)
        grad_scores = (probs * (grad_probs - delta)).astype(half)
        grad_q = product(grad_scores, keys) * 0.125
        for j in range(3):
            h = 3 * g + j
            dqs[:, 64 * h : 64 * h + 64] = grad_q[TB * j : TB * j + TB]
        dkv[:, 64 * g : 64 * g + 64] = product_left(grad_scores, qh)
        dkv[:, 384 + 64 * g : 448 + 64 * g] = product_left(probs.astype(half), gh)
    other_rows = pl.ds(pl.multiple_of(512 * (1 - k), 512), 512)
    dkv_co[...] = dkv[other_rows, :].astype(half)
    kc = send(dkv_co, dkv_ci, kc_s.at[0], kc_r.at[0], core)
    grad_q = dqs[...]
    inner = jnp.sum(grad_q * q_ref[...].astype(full), axis=1, keepdims=True)
    sdq[mine, :] = turn(grad_q, cosine, sine).astype(half)
    q_gather = Gather(lambda b, h: sdq.at[part_rows(b, h)], r, c, sd_s, sd_r)
    q_gather.start()
    tile_sums[0].relay()
    tile_sums[1].start()
    kc.wait_recv()
    pairs = Scatter(e0, e1, e2, e3, r, c, kp_s, kp_r)
    for m in (2, 0, 1):
        b = mates[m][0]
        e0[m] = (dkv[block_rows(4 * k + b), :] + dkv_ci[block_rows(b), :].astype(full)).astype(half)
        pairs.start(((0,), (1,), (2, 3))[m])
    my_block = block_rows(4 * k + r)
    dkv[my_block, :] = dkv[my_block, :] + dkv_ci[mine, :].astype(full)
    for m in range(3):
        cols = block_rows(mates[m][0])
        remote(gm_out.at[0], gm_nat.at[:, cols], gm_s.at[m], gm_r.at[m], mates[m]).wait_recv()
    loads["att"].wait()
    grad_wo = lax.dot_general(
        att_all[...], gm_nat[...], (((0,), (1,)), ((), ())), preferred_element_type=full
    )
    for i in range(8):
        dwo[i] = grad_wo[144 * i : 144 * i + 144]

    def wide(value):
        n = value.shape[0] // 3
        return jnp.concatenate([value[n * j : n * j + n] for j in range(3)], axis=1)

    def tall(value):
        n = value.shape[1] // 3
        return jnp.concatenate([value[:, n * j : n * j + n] for j in range(3)], axis=0)

    for i in range(4):
        dwo_co[i] = dwo[2 * i + 1 - k].astype(half)
    oc_copy = send(dwo_co, dwo_ci, oc_s.at[0], oc_r.at[0], core)
    pairs.relay()
    q_gather.relay()
    tile_sums[1].relay()
    downs.relay()
    oc_copy.wait_recv()
    for i in range(4):
        value = dwo[2 * i + k] + dwo_ci[i].astype(full)
        dwo_z[i] = wide(value).astype(half)
        dwo[2 * i + k] = value
    o_sum = PlaneSum(lambda plane: dwo_z.at[plane], dwo_over, dwo_joint, dwo_in, r, c, oz_s, oz_r)
    o_sum.start()
    grad_kv = pairs.finish(dkv[my_block, :])
    sdk[mine, 0:384] = turn(grad_kv[:, 0:384], cosine, sine).astype(half)
    sdk[mine, 384:768] = grad_kv[:, 384:768].astype(half)
    k_gather = Gather(lambda b, h: sdk.at[part_rows(b, h)], r, c, sk_s, sk_r)
    k_gather.start()
    inner = inner + jnp.sum(grad_kv * kv_ref[my_block, :].astype(full), axis=1, keepdims=True)
    loads["sown"].wait()
    scale = sown_ref[...]
    coef = jnp.transpose(inner * (scale * scale) / D)
    coef_all[r] = coef[0:8]
    coef_copies = [
        send(coef_all.at[r], coef_all.at[r], cf_s.at[m], cf_r.at[m], mates[m]) for m in range(3)
    ]
    o_sum.relay()
    loads["n1"].wait()
    q_gather.finish()
    grad_wi = product(n1_ref[...], sdq[...])
    for i in range(8):
        dwq[i] = grad_wi[:, 144 * i : 144 * i + 144]
    for i in range(4):
        dwq_co[i] = dwq[2 * i + 1 - k].astype(half)
    qc_copy = send(dwq_co, dwq_ci, qc_s.at[0], qc_r.at[0], core)
    k_gather.relay()
    loads["dwd"].wait()
    tile_back(2)
    tile_back(0)
    qc_copy.wait_recv()
    for i in range(4):
        value = dwq[2 * i + k] + dwq_ci[i].astype(full)
        dwq_z[i] = wide(value).astype(half)
        dwq[2 * i + k] = value
    q_sum = PlaneSum(lambda plane: dwq_z.at[plane], dwq_over, dwq_joint, dwq_in, r, c, qz_s, qz_r)
    q_sum.start()
    loads["wi"].wait()
    back = product_right(wi_ref[:, 0:1152], sdq[...])
    k_gather.finish()
    grad_wi = product(n1_ref[...], sdk[...])
    for i in range(8):
        dwk[i, :, 0:48] = grad_wi[:, 48 * i : 48 * i + 48]
        dwk[i, :, 48:96] = grad_wi[:, 384 + 48 * i : 432 + 48 * i]
    for i in range(4):
        dwk_co[i] = dwk[2 * i + 1 - k].astype(half)
    kk_copy = send(dwk_co, dwk_ci, kk_s.at[0], kk_r.at[0], core)
    loads["srow"].wait()
    back = (back + product_right(wi_ref[:, 1152:1920], sdk[...])) * srow_ref[0:1, :]
    kk_copy.wait_recv()
    for i in range(4):
        value = dwk[2 * i + k] + dwk_ci[i].astype(full)
        dwk_z[i] = value.astype(half)
        dwk[2 * i + k] = value
    kz_copies = [
        send(dwk_z.at[ahead_z[m]], dwk_in.at[m], kz_s.at[m], kz_r.at[m], aheads[m])
        for m in range(3)
    ]
    loads["mid"].wait()
    dn_own[...] = mid_ref[...] + down_ref[mine, :].astype(full)
    result = downs.finish(dn_own)
    result = jnp.transpose(result).astype(half)
    for i in range(4):
        bo_out[i] = result[288 * i : 288 * i + 288]
    bo_ref[:, mine] = bo_out[r]
    bo_copies = [
        send(bo_out.at[mates[m][0]], bo_ref.at[:, mine], bo_s.at[m], bo_r.at[m], mates[m])
        for m in range(3)
    ]
    q_sum.relay()
    tile_back(1)
    for m in range(3):
        b = mates[m][0]
        remote(coef_all.at[b], coef_all.at[b], cf_s.at[m], cf_r.at[m], mates[m]).wait_recv()
    coef = jnp.concatenate([coef_all[i] for i in range(4)], axis=1)[0:1, :]
    tokens = tok_ref[...].astype(full)
    gain1 = jnp.transpose(jnp.broadcast_to(gains_in[0:1, :], (128, 288)))[:, 0:1]
    ig_ref[...] = (gm_nat[...].astype(full) + back * gain1 - tokens * coef).astype(half)
    for copy in g2_copies:
        copy.wait_recv()
    column = jnp.sum(back * tokens, axis=1, keepdims=True)
    gl[0] = jnp.transpose(jnp.broadcast_to(column, (288, 128)))[0:8]
    gl[1] = g2_out[r] + g2_in[0] + g2_in[1] + g2_in[2]
    gc_copy = send(gl, gl_ci, gc_s.at[0], gc_r.at[0], core)
    gc_copy.wait_recv()
    gl_z[...] = gl[...] + gl_ci[...]
    gz_copies = [send(gl_z, gl_in.at[m], gz_s.at[m], gz_r.at[m], aheads[m]) for m in range(3)]
    total = dwo[2 * z + k] + tall(o_sum.arrive())
    do_ref[...] = total
    for m in range(3):
        cols = block_rows(mates[m][0])
        remote(bo_out.at[0], bo_ref.at[:, cols], bo_s.at[m], bo_r.at[m], mates[m]).wait_recv()
    for m in range(3):
        b = mates[m][0]

        @pl.when(has_tile(b, z, k))
        def _():
            for t in range(3):
                remote(
                    tile_out.at[0, t],
                    dw_ref.at[tile_of(b, z), t],
                    t_s.at[3 * t + m],
                    t_r.at[3 * t + m],
                    mates[m],
                ).wait_recv()

    total = dwq[2 * z + k] + tall(q_sum.arrive())
    dq_ref[:, 0:144] = total
    total = dwk[2 * z + k]
    for m in range(3):
        kz_copies[m].wait_recv()
        total = total + dwk_in[m].astype(full)
    dq_ref[:, 144:240] = total
    total = gl_z[...]
    for m in range(3):
        gz_copies[m].wait_recv()
        total = total + gl_in[m]
    gains_ref[...] = total
    for copy in sent:
        copy.wait_send()
    for part in (downs, pairs, q_gather, k_gather, o_sum, q_sum, *tile_sums):
        part.sent()
    @pl.when(mine_has)
    def _():
        for t in range(3):
            for m in range(3):
                tile_copy(t, m).wait_send()


def back(*args):
    shape = jax.ShapeDtypeStruct
    sems = []
    for count in (6, 3, (2, 5), 9, 1, 6, 6, 6, 1, 5, 1, 3, 1, 5, 3, 1, 3, 3, 3):
        count = count if isinstance(count, tuple) else (count,)
        sems += [pltpu.SemaphoreType.DMA(count)] * 2
    v = pltpu.VMEM
    return pl.pallas_call(
        back_kernel,
        out_shape=(
            shape((288, 512), half),
            shape((288, 512), half),
            shape((3, 3, 288, 128), half),
            shape((288, 240), full),
            shape((144, 288), full),
            shape((2, 8, 288), full),
        ),
        in_specs=[pl.BlockSpec(memory_space=pl.ANY)] * 16 + [VM] * 2 + [SM],
        out_specs=(VM,) * 6,
        scratch_shapes=[
            v((TB, D), full),
            v((TB, D), half),
            v((1024, 768), half),
            v((3 * TB, 128), full),
            v((TB, D), full),
            v((D, D), half),
            v((288, 1920), half),
            v((288, 512), half),
            v((8, 512), full),
            v((TB, 128), full),
            v((512, D), half),
            v((TB, D), half),
            v((512, D), half),
            v((8, D), full),
            v((2, 3, D, 128), half),
            v((D, 128), full),
            v((4, 288, TB), half),
            v((288, 512), half),
            v((4, 288, TB), half),
            v((2, 2, D, 128), half),
            v((2, 2, D, 128), half),
            v((2, 2, D, 128), half),
            v((4, 3, 288, 128), half),
            v((1024, 768), full),
            v((512, 768), half),
            v((512, 768), half),
            v((512, D), half),
            v((512, 768), half),
            v((TB, D), full),
            v((8, 288, 144), full),
            v((4, 288, 144), half),
            v((4, 288, 144), half),
            v((4, 96, 432), half),
            v((2, 96, 432), half),
            v((2, 96, 432), half),
            v((2, 96, 432), half),
            v((8, 288, 96), full),
            v((4, 288, 96), half),
            v((4, 288, 96), half),
            v((4, 288, 96), half),
            v((3, 288, 96), half),
            v((8, 144, 288), full),
            v((4, 144, 288), half),
            v((4, 144, 288), half),
            v((4, 48, 864), half),
            v((2, 48, 864), half),
            v((2, 48, 864), half),
            v((2, 48, 864), half),
            v((4, 8, 288), full),
            v((3, 8, 288), full),
            v((2, 8, 288), full),
            v((2, 8, 288), full),
            v((2, 8, 288), full),
            v((3, 2, 8, 288), full),
            v((4, 8, TB), full),
            v((TB, D), full),
        ]
        + scatter_buffers(D)
        + scatter_buffers(768)
        + sems
        + [pltpu.SemaphoreType.DMA((16,))],
        compiler_params=pltpu.CompilerParams(
            collective_id=3, has_side_effects=True, vmem_limit_bytes=60 << 20
        ),
    )(*args)


SETS = (("gu", (2, 288, 384)), ("d", (288, 384)), ("o", (144, 288)), ("q", (144, 288)),
        ("kv", (2, 48, 288)), ("g", (2, 288)))


def update_kernel(*refs):
    grads, refs = refs[:6], refs[6:]
    ins, refs = refs[:18], refs[18:]
    acts, refs = refs[:2], refs[2:]
    outs, refs = refs[:23], refs[23:]
    grad_v, refs = refs[:6], refs[6:]
    in_v, refs = refs[:18], refs[18:]
    out_v, refs = refs[:23], refs[23:]
    grad_s, in_s, out_s = refs
    loads = []
    for n in range(6):
        for i in range(3):
            j = 3 * n + i
            loads.append(pltpu.make_async_copy(ins[j], in_v[j], in_s.at[j]))
    grad_loads = [pltpu.make_async_copy(grads[i], grad_v[i], grad_s.at[i]) for i in range(6)]
    grad_loads[2].start()
    for copy in loads[:6]:
        copy.start()
    for i in (4, 3, 5, 0, 1):
        grad_loads[i].start()
    for copy in loads[6:]:
        copy.start()
    stores = []

    def store(src, dst):
        copy = pltpu.make_async_copy(src, dst, out_s.at[len(stores)])
        copy.start()
        stores.append(copy)

    fix = 1.0 - BETA**STEP

    def step(n, at, grad, rate, decay):
        weight = in_v[3 * n][at]
        first = BETA * in_v[3 * n + 1][at] + (1.0 - BETA) * grad
        second = BETA * in_v[3 * n + 2][at] + (1.0 - BETA) * grad * grad
        change = first / fix / (jnp.sqrt(second / fix) + TINY)
        weight = weight - rate * (change + decay * weight)
        out_v[4 * n][at] = first
        out_v[4 * n + 1][at] = second
        out_v[4 * n + 2][at] = weight
        if n < 5:
            out_v[4 * n + 3][at] = weight.astype(half)

    def ready(n):
        for copy in loads[3 * n : 3 * n + 3]:
            copy.wait()

    def done(n, at=None):
        for j in range(4 * n, min(4 * n + 4, 23)):
            if at is None:
                store(out_v[j], outs[j])
            else:
                store(out_v[j].at[at], outs[j].at[at])

    rate = D**-0.5
    every = (slice(None), slice(None))
    cols = [(slice(None), slice(128 * i, 128 * i + 128)) for i in range(3)]
    dw, dq, do, dg = grad_v[2:]
    grad_loads[2].wait()
    ready(0)
    for t in range(2):
        for i in range(3):
            step(0, (t,) + cols[i], dw[i, t].astype(full), rate, DECAY)
        done(0, t)
    ready(1)
    for i in range(3):
        step(1, cols[i], dw[i, 2].astype(full), FF**-0.5, DECAY)
    done(1)
    grad_loads[4].wait()
    ready(2)
    step(2, every, do[...], rate, DECAY)
    done(2)
    grad_loads[3].wait()
    ready(3)
    turned = jnp.transpose(dq[...])
    step(3, every, turned[0:144], rate, DECAY)
    done(3)
    ready(4)
    for t in range(2):
        step(4, (t, slice(None), slice(None)), turned[144 + 48 * t : 192 + 48 * t], rate, DECAY)
    done(4)
    grad_loads[5].wait()
    ready(5)
    step(5, every, jnp.concatenate([dg[0, 0:1], dg[1, 0:1]], axis=0), 0.25, 0.0)
    done(5)
    for i in range(2):
        grad_loads[i].wait()
        store(grad_v[i], acts[i])
    for copy in stores:
        copy.wait()


def update(grads, params):
    shape = jax.ShapeDtypeStruct
    v = pltpu.VMEM
    outs = []
    for name, dims in SETS:
        outs += [shape(dims, full)] * 3
        if name != "g":
            outs.append(shape(dims, half))
    acts = [shape((288, 512), half)] * 2
    hbm = pl.BlockSpec(memory_space=pl.ANY)
    result = pl.pallas_call(
        update_kernel,
        out_shape=tuple(acts + outs),
        in_specs=[hbm] * 24,
        out_specs=(hbm,) * 25,
        scratch_shapes=[v(g.shape, g.dtype) for g in grads]
        + [v(dims, full) for name, dims in SETS for i in range(3)]
        + [v(o.shape, o.dtype) for o in outs]
        + [
            pltpu.SemaphoreType.DMA((6,)),
            pltpu.SemaphoreType.DMA((18,)),
            pltpu.SemaphoreType.DMA((32,)),
        ],
        compiler_params=pltpu.CompilerParams(vmem_limit_bytes=60 << 20),
    )(*grads, *params)
    gu, d, o, q, kv, g = (result[2 + 4 * n : 6 + 4 * n] for n in range(6))
    return (*result[:2], *g, *q, *kv, *o, *gu, *d)


def swap(value):
    return jnp.swapaxes(value, -1, -2)


def local_fast(
    tokens,
    cotangent,
    starts,
    gains,
    gains_m,
    gains_v,
    w_query,
    w_query_m,
    w_query_v,
    w_keyval,
    w_keyval_m,
    w_keyval_v,
    w_output,
    w_output_m,
    w_output_v,
    w_gateup,
    w_gateup_m,
    w_gateup_v,
    w_down,
    w_down_m,
    w_down_v,
):
    tok = swap(tokens)
    kept = forward(
        tok, swap(cotangent), swap(w_query), swap(w_keyval), w_output, w_gateup, swap(w_down),
        gains, starts
    )
    grads = back(*kept, tok, gains, starts)
    params = []
    for group in (
        (w_gateup, w_gateup_m, w_gateup_v),
        (swap(w_down), swap(w_down_m), swap(w_down_v)),
        (w_output, w_output_m, w_output_v),
        (swap(w_query), swap(w_query_m), swap(w_query_v)),
        (swap(w_keyval), swap(w_keyval_m), swap(w_keyval_v)),
        (gains, gains_m, gains_v),
    ):
        params += group
    outs = update(grads, params)
    turned = (0, 1, 5, 6, 7, 8, 9, 10, 11, 12, 21, 22, 23, 24)
    return tuple(swap(value) if i in turned else value for i, value in enumerate(outs))


def local(tokens, *others):
    fits = lax.axis_size("row") == 4 and lax.axis_size("col") == 8 and tokens.shape == (512, 288)
    plan = local_fast if fits else local_general
    return plan(tokens, *others)


def solution(mesh):
    return jax.shard_map(
        local,
        mesh=mesh,
        in_specs=(
            P("col", "row"),
            P("col", "row"),
            P(),
            P(None, "row"),
            P(None, "row"),
            P(None, "row"),
            P("row", "col"),
            P("row", "col"),
            P("row", "col"),
            P(None, "row", "col"),
            P(None, "row", "col"),
            P(None, "row", "col"),
            P("col", "row"),
            P("col", "row"),
            P("col", "row"),
            P(None, "row", "col"),
            P(None, "row", "col"),
            P(None, "row", "col"),
            P("col", "row"),
            P("col", "row"),
            P("col", "row"),
        ),
        out_specs=(
            P("col", "row"),
            P("col", "row"),
            P(None, "row"),
            P(None, "row"),
            P(None, "row"),
            P("row", "col"),
            P("row", "col"),
            P("row", "col"),
            P("row", "col"),
            P(None, "row", "col"),
            P(None, "row", "col"),
            P(None, "row", "col"),
            P(None, "row", "col"),
            P("col", "row"),
            P("col", "row"),
            P("col", "row"),
            P("col", "row"),
            P(None, "row", "col"),
            P(None, "row", "col"),
            P(None, "row", "col"),
            P(None, "row", "col"),
            P("col", "row"),
            P("col", "row"),
            P("col", "row"),
            P("col", "row"),
        ),
        check_vma=False,
    )
```
